128 devices in a mesh: dp: 32 (over x_hi, y, z), feat: 4 (over x_lo, core).
Axes of the slice: x: 4 (x_hi: 2, x_lo: 2; x = x_hi * 2 + x_lo), y: 4, z: 4, core: 2. Of those that a mesh axis runs over, the one named last changes fastest.
Arguments:
- view_a: bfloat16 [24576, 4096], P('dp', 'feat'), may hold values from -4000 to 4000, as said below
- view_b: bfloat16 [24576, 4096], P('dp', 'feat'), may hold values from -4000 to 4000, as said below
Outputs:
- loss: float32 [], replicated
- grad_a: bfloat16 [24576, 4096], P('dp', 'feat')
- grad_b: bfloat16 [24576, 4096], P('dp', 'feat')
The draws below stay inside these ranges and needn't reach their ends.
Inputs may be any that keep to these rules, and one draw needn't show every extreme that they name: `view_a`: for every feature, the magnitude of its mean over all 24576 samples is at most 20 times its standard deviation over them, and that standard deviation is 0.5 or more. `view_b`: for every feature, the magnitude of its mean over all 24576 samples is at most 20 times its standard deviation over them, and that standard deviation is 0.5 or more.
All inputs are finite; a program needn't handle non-finite values.
Results may differ from the reference program's by a relative error of at most 0.0039.
Values may be sent and summed in bfloat16 or wider, within the bound.
No kernel may reach another device: no remote copies, remote signals or barrier semaphores. Data moves between devices by JAX's collectives and lax.ppermute only.
A program may use at most 128 MiB of HBM per device.

```python
import math
import jax
import jax.numpy as jnp
from jax import lax

WIN = 4096
PAIRS = 24576


def shared_parts(key, spread, offset_scale):
    keys = jax.random.split(key, 7)
    normal_part = jax.random.truncated_normal(keys[0], -4.0, 4.0, (PAIRS, WIN), jnp.float32)
    signal = normal_part
    factors = jax.random.truncated_normal(keys[2], -3.0, 3.0, (PAIRS, 4), jnp.float32)
    loadings = 0.3 * jax.random.truncated_normal(keys[3], -3.0, 3.0, (4, WIN), jnp.float32)
    for factor in range(4):
        signal = signal + factors[:, factor:factor + 1] * loadings[factor:factor + 1, :]
    col_offset = offset_scale * jax.random.truncated_normal(keys[4], -2.0, 2.0, (1, WIN), jnp.float32)
    col_scale = jnp.exp(jax.random.uniform(keys[5], (1, WIN), jnp.float32, 0.0, math.log(10.0)))
    position = jnp.arange(PAIRS, dtype=jnp.float32)[:, None] / PAIRS
    jitter = jax.random.uniform(keys[6], (PAIRS, 1), jnp.float32, 0.0, spread - math.log(3.0))
    row_scale = jnp.exp(math.log(3.0) * position + jitter)
    return (signal, col_offset, col_scale, row_scale)


def make_view(parts, key):
    signal, col_offset, col_scale, row_scale = parts
    keys = jax.random.split(key, 2)
    noise = jax.random.truncated_normal(keys[0], -4.0, 4.0, (PAIRS, WIN), jnp.float32)
    gains = jax.random.uniform(keys[1], (1, WIN), jnp.float32, 0.7, 1.4)
    values = col_offset + col_scale * gains * row_scale * (signal + 0.6 * noise)
    return values.astype(jnp.bfloat16)


def draw_view_a(key, part):
    parts = shared_parts(key, math.log(10.0), 2.0)
    key = jax.random.fold_in(key, 11)
    return make_view(parts, key)


def draw_view_b(key, part):
    parts = shared_parts(key, math.log(10.0), 2.0)
    key = jax.random.fold_in(key, 23)
    return make_view(parts, key)


def setup_inputs(seed: int = 0) -> dict:
    arg_keys = jax.random.split(jax.random.key(seed), 3)
    view_a = draw_view_a(jax.random.fold_in(arg_keys[2], 71), 0)
    view_b = draw_view_b(jax.random.fold_in(arg_keys[2], 71), 0)
    return {"view_a": view_a, "view_b": view_b}


epsilon = 1e-05
off_weight = 0.0051

def normalize(view):
    values = view.astype(jnp.float32)
    mean_value = lax.optimization_barrier(jnp.mean(values, axis=0))
    centred = values - mean_value
    inverse = lax.rsqrt(lax.optimization_barrier(jnp.mean(centred * centred, axis=0)) + epsilon)
    return (centred * inverse, inverse)

def backward(upstream, normed, inverse):
    mean_up = lax.optimization_barrier(jnp.mean(upstream, axis=0))
    mean_cross = lax.optimization_barrier(jnp.mean(upstream * normed, axis=0))
    return (inverse * (upstream - mean_up - normed * mean_cross)).astype(jnp.bfloat16)

def reference(view_a, view_b):
    norm_a, inv_a = normalize(view_a)
    norm_b, inv_b = normalize(view_b)
    low_a = norm_a.astype(jnp.bfloat16)
    low_b = norm_b.astype(jnp.bfloat16)
    corr = lax.dot_general(low_a, low_b, (((0,), (0,)), ((), ())), preferred_element_type=jnp.float32) / PAIRS
    indices = jnp.arange(WIN, dtype=jnp.int32)
    on_diagonal = indices[:, None] == indices[None, :]
    loss = jnp.sum(jnp.where(on_diagonal, (1.0 - corr) * (1.0 - corr), off_weight * corr * corr))
    slope = jnp.where(on_diagonal, -2.0 * (1.0 - corr), 2.0 * off_weight * corr).astype(jnp.bfloat16)
    up_a = lax.dot_general(low_b, slope, (((1,), (1,)), ((), ())), preferred_element_type=jnp.float32)
    up_b = jnp.dot(low_a, slope, preferred_element_type=jnp.float32)
    return (loss, backward(up_a, norm_a, inv_a), backward(up_b, norm_b, inv_b))
```

```python
import jax
import jax.numpy as jnp
from jax import lax
from jax.sharding import PartitionSpec as P

epsilon = 1e-05
off_weight = 0.0051


def exchange(pieces):
    return lax.all_to_all(pieces, "dp", 0, 0, tiled=True)


def share(values):
    count = lax.axis_size("dp")
    return exchange(jnp.broadcast_to(values[None], (count,) + values.shape))


def local_moments(values):
    mean = jnp.mean(values, axis=0)
    centred = values - mean
    return mean, jnp.sum(centred * centred, axis=0)


def combine(means, squares, pairs):
    count = means.shape[0]
    mean = jnp.mean(means, axis=0)
    shift = means - mean
    var = (jnp.sum(squares, axis=0) + (pairs // count) * jnp.sum(shift * shift, axis=0)) / pairs
    return mean, lax.rsqrt(var + epsilon)


def backward(upstream, normed, inverse, sum_up, sum_cross, pairs):
    return (inverse * (upstream - sum_up / pairs - normed * (sum_cross / pairs))).astype(
        jnp.bfloat16
    )


def on_device(view_a, view_b):
    dp_count = lax.axis_size("dp")
    feat_count = lax.axis_size("feat")
    rows, width = view_a.shape
    pairs = rows * dp_count
    full_width = width * feat_count
    first = view_a.astype(jnp.float32)
    second = view_b.astype(jnp.float32)
    moments = jnp.stack(local_moments(first) + local_moments(second))
    shared = share(moments.reshape(-1, 128)).reshape(dp_count, 4, width)
    mean_a, inv_a = combine(shared[:, 0], shared[:, 1], pairs)
    mean_b, inv_b = combine(shared[:, 2], shared[:, 3], pairs)
    norm_a = (first - mean_a) * inv_a
    norm_b = (second - mean_b) * inv_b
    low_a = norm_a.astype(jnp.bfloat16)
    low_b = norm_b.astype(jnp.bfloat16)
    second_full = lax.all_gather(low_b, "feat", axis=1, tiled=True)
    dp_index = lax.axis_index("dp")
    feat_index = lax.axis_index("feat")
    keep = width // dp_count
    row_ids = feat_index * width + dp_index * keep + jnp.arange(keep, dtype=jnp.int32)
    col_ids = jnp.arange(full_width, dtype=jnp.int32)
    diagonal = jnp.sum(low_a.astype(jnp.float32) * low_b.astype(jnp.float32), axis=0)
    diagonal = jnp.sum(share(diagonal.reshape(-1, 128)), axis=0).reshape(dp_count, keep)
    diagonal = lax.dynamic_index_in_dim(diagonal, dp_index, 0, keepdims=False)
    part = lax.dot_general(
        low_a, second_full, (((0,), (0,)), ((), ())), preferred_element_type=jnp.float32
    ).astype(jnp.bfloat16)
    tiles = exchange(part.reshape(dp_count, keep, full_width))
    tile = jnp.sum(tiles.astype(jnp.float32), axis=0)
    on_diagonal = row_ids[:, None] == col_ids[None, :]
    corr_tile = jnp.where(on_diagonal, diagonal[:, None], tile) / pairs
    partial_value = jnp.sum(
        jnp.where(
            on_diagonal, (1.0 - corr_tile) * (1.0 - corr_tile), off_weight * corr_tile * corr_tile
        )
    )
    slope = jnp.where(on_diagonal, -2.0 * (1.0 - corr_tile), 2.0 * off_weight * corr_tile).astype(
        jnp.bfloat16
    )
    gathered = share(slope).reshape(width, full_width)
    part_b = jnp.dot(low_a, gathered, preferred_element_type=jnp.float32)
    up_b = lax.psum_scatter(
        part_b.astype(jnp.bfloat16), "feat", scatter_dimension=1, tiled=True
    ).astype(jnp.float32)
    up_a = lax.dot_general(
        second_full, gathered, (((1,), (1,)), ((), ())), preferred_element_type=jnp.float32
    )
    sums = jnp.stack(
        (
            jnp.sum(up_a, axis=0),
            jnp.sum(up_a * norm_a, axis=0),
            jnp.sum(up_b, axis=0),
            jnp.sum(up_b * norm_b, axis=0),
            jnp.full((width,), partial_value),
        )
    )
    sums = jnp.sum(share(sums.reshape(-1, 128)), axis=0).reshape(5, width)
    loss = jnp.sum(lax.all_gather(sums[4, :128], "feat")[:, 0])
    grad_a = backward(up_a, norm_a, inv_a, sums[0], sums[1], pairs)
    grad_b = backward(up_b, norm_b, inv_b, sums[2], sums[3], pairs)
    return (loss, grad_a, grad_b)


def solution(mesh):
    in_specs = (P("dp", "feat"), P("dp", "feat"))
    out_specs = (P(), P("dp", "feat"), P("dp", "feat"))
    return jax.shard_map(
        on_device, mesh=mesh, in_specs=in_specs, out_specs=out_specs, check_vma=False
    )
```

```python
import jax
import jax.numpy as jnp
from jax import lax
from jax.sharding import PartitionSpec as P

epsilon = 1e-05
off_weight = 0.0051
low = jnp.bfloat16
full = jnp.float32


def at_z(step):
    return lambda d: d // 4 * 4 + (d + step) % 4


def at_y(step):
    return lambda d: d // 16 * 16 + (d // 4 + step) % 4 * 4 + d % 4


def move(values, place, axis="dp"):
    count = lax.axis_size(axis)
    return lax.ppermute(values, axis, [(d, place(d)) for d in range(count)])


def across_core(values):
    return move(values, lambda f: f ^ 1, "feat")


def across_chip(values):
    return move(values, lambda f: f ^ 2, "feat")


def across_half(values):
    return move(values, lambda d: d ^ 16)


def share(values):
    count = lax.axis_size("dp")
    pieces = jnp.broadcast_to(values[None], (count,) + values.shape)
    return lax.all_to_all(pieces, "dp", 0, 0, tiled=True)


def local_moments(values):
    mean = jnp.mean(values, axis=0)
    centred = values - mean
    return mean, jnp.sum(centred * centred, axis=0)


def combine(means, squares, pairs):
    count = means.shape[0]
    mean = jnp.mean(means, axis=0)
    shift = means - mean
    var = (jnp.sum(squares, axis=0) + (pairs // count) * jnp.sum(shift * shift, axis=0)) / pairs
    return mean, lax.rsqrt(var + epsilon)


def ring_reduce(chunk, place):
    far = chunk(2)
    half = far.shape[0] // 2
    from_below = move(far[:half], place(1))
    from_above = move(far[half:], place(3))
    above, below = chunk(1), chunk(3)
    above = jnp.concatenate(
        ((above[:half].astype(full) + from_below.astype(full)).astype(low), above[half:])
    )
    below = jnp.concatenate(
        (below[:half], (below[half:].astype(full) + from_above.astype(full)).astype(low))
    )
    above = move(above, place(1))
    below = move(below, place(3))
    return chunk(0).astype(full) + above.astype(full) + below.astype(full)


def ring_gather(block, place, position):
    rows = block.shape[0]
    half = rows // 2
    below = move(block, place(1))
    above = move(block, place(3))
    far = jnp.concatenate((move(below[:half], place(1)), move(above[half:], place(3))))
    gathered = jnp.zeros((4 * rows,) + block.shape[1:], block.dtype)
    for step, part in ((0, block), (3, below), (1, above), (2, far)):
        start = (position + step) % 4 * rows
        gathered = lax.dynamic_update_slice_in_dim(gathered, part, start, 0)
    return gathered


def pick(stack, index, axis):
    return lax.dynamic_index_in_dim(stack, index, axis, keepdims=False)


def finish_reduce(sums, place, position, half_index):
    blocks = sums.reshape(2, 4, 64, sums.shape[-1])
    sent = blocks.astype(low)
    total = pick(blocks, position, 1)
    for step in (1, 2, 3):
        total = total + move(pick(sent, (position + step) % 4, 1), place(step)).astype(full)
    halves = total.reshape(2, 2, 32, sums.shape[-1])
    other = across_half(pick(halves, 1 - half_index, 1).astype(low))
    return pick(halves, half_index, 1) + other.astype(full)


def start_gather(tiles, place, position, half_index):
    other = across_half(tiles)
    pair = jnp.where(
        half_index == 0,
        jnp.concatenate((tiles, other), axis=1),
        jnp.concatenate((other, tiles), axis=1),
    )
    gathered = jnp.zeros((2, 4) + pair.shape[1:], pair.dtype)
    gathered = lax.dynamic_update_index_in_dim(gathered, pair, position, 1)
    for step in (1, 2, 3):
        part = move(pair, place(step))
        gathered = lax.dynamic_update_index_in_dim(gathered, part, (position - step) % 4, 1)
    return gathered.reshape(2, 256, pair.shape[-1])


def on_device(view_a, view_b):
    dp_count = lax.axis_size("dp")
    rows, width = view_a.shape
    pairs = rows * dp_count
    dp_index = lax.axis_index("dp")
    xi, yi, zi = dp_index // 16, dp_index // 4 % 4, dp_index % 4
    view_c = across_chip(view_b)
    first = view_a.astype(full)
    second = view_b.astype(full)
    moments = jnp.stack(local_moments(first) + local_moments(second))
    shared = share(moments.reshape(-1, 128)).reshape(dp_count, 4, width)
    mean_a, inv_a = combine(shared[:, 0], shared[:, 1], pairs)
    mean_b, inv_b = combine(shared[:, 2], shared[:, 3], pairs)
    stats_c = across_chip(jnp.stack((mean_b, inv_b)))
    norm_a = (first - mean_a) * inv_a
    norm_b = (second - mean_b) * inv_b
    low_a = norm_a.astype(low)
    lows = [norm_b.astype(low)]
    lows.append(across_core(lows[0]))
    lows.append(((view_c.astype(full) - stats_c[0]) * stats_c[1]).astype(low))
    lows.append(across_core(lows[2]))

    def chunk_of(block, position):
        def chunk(step):
            start = (position + step) % 4 * 256
            columns = lax.dynamic_slice_in_dim(low_a, start, 256, 1)
            return lax.dot_general(
                columns, lows[block], (((0,), (0,)), ((), ())), preferred_element_type=full
            ).astype(low)

        return chunk

    sums = [
        ring_reduce(chunk_of(block, position), place)
        for block, position, place in ((0, zi, at_z), (1, yi, at_y), (2, zi, at_z), (3, yi, at_y))
    ]
    ends = jnp.stack(
        (
            jnp.sum(low_a.astype(full) * lows[0].astype(full), axis=0),
            jnp.sum(low_a.astype(full), axis=0),
            jnp.sum(lows[0].astype(full), axis=0),
            jnp.zeros((width,), full),
        )
    )
    ends = jnp.sum(share(ends.reshape(-1, 128)), axis=0).reshape(4, width) / pairs
    diagonal, low_mean_a = ends[0], ends[1]
    low_means = [ends[2]]
    low_means.append(across_core(low_means[0]))
    low_means.append(across_chip(low_means[0]))
    low_means.append(across_core(low_means[2]))

    even = finish_reduce(jnp.stack((sums[0], sums[2])), at_y, yi, xi) / pairs
    odd = finish_reduce(jnp.stack((sums[1], sums[3])), at_z, zi, xi) / pairs
    own = zi * 256 + yi * 64 + xi * 32
    diagonal_rows = lax.dynamic_slice_in_dim(diagonal, own, 32, 0)
    shape = even.shape
    on_diagonal = (
        lax.broadcasted_iota(jnp.int32, shape, 2)
        == own + lax.broadcasted_iota(jnp.int32, shape, 1)
    ) & (lax.broadcasted_iota(jnp.int32, shape, 0) == 0)
    even = jnp.where(on_diagonal, diagonal_rows[None, :, None], even)
    slope_even = jnp.where(on_diagonal, -2.0 * (1.0 - even), 2.0 * off_weight * even).astype(low)
    slope_odd = (2.0 * off_weight * odd).astype(low)
    part_loss = jnp.sum(
        jnp.where(on_diagonal, (1.0 - even) * (1.0 - even), off_weight * even * even)
    ) + jnp.sum(off_weight * odd * odd)

    def row_terms(slope, corr, means):
        slope = slope.astype(full)
        cross = jnp.sum(slope * corr, axis=(0, 2))
        mean = jnp.sum(slope * jnp.stack(means)[:, None, :], axis=(0, 2))
        return jnp.concatenate((cross, mean))

    terms = jnp.concatenate(
        (
            row_terms(slope_even, even, low_means[0::2]),
            row_terms(slope_odd, odd, low_means[1::2]),
            jnp.full((896,), part_loss),
        )
    )
    terms = share(terms.reshape(8, 128))
    even_terms = terms[:, 0, :64].reshape(2, 4, 4, 2, 32).transpose(3, 2, 1, 0, 4)
    odd_terms = terms[:, 0, 64:].reshape(2, 4, 4, 2, 32).transpose(3, 1, 2, 0, 4)
    cross_a, mean_up_a = (even_terms.reshape(2, width) + odd_terms.reshape(2, width))
    part_loss = jnp.sum(terms[:, 1, 0])

    block_even = start_gather(slope_even, at_y, yi, xi)
    block_odd = start_gather(slope_odd, at_z, zi, xi)
    slopes = [None] * 4
    slopes[2] = ring_gather(block_even[1], at_z, zi)
    slopes[3] = ring_gather(block_odd[1], at_y, yi)
    slopes[0] = ring_gather(block_even[0], at_z, zi)
    slopes[1] = ring_gather(block_odd[0], at_y, yi)

    def times(block):
        return jnp.dot(low_a, slopes[block], preferred_element_type=full)

    own_diagonal = lax.broadcasted_iota(jnp.int32, (width, width), 0) == lax.broadcasted_iota(
        jnp.int32, (width, width), 1
    )

    def column_terms(block):
        slope = slopes[block].astype(full)
        squares = slope * slope
        if block == 0:
            squares = jnp.where(own_diagonal, 0.0, squares)
        cross = jnp.sum(squares, axis=0) / (2.0 * off_weight)
        if block == 0:
            cross = cross + (-2.0 * (1.0 - diagonal)).astype(low).astype(full) * diagonal
        mean = jnp.sum(slope * low_mean_a[:, None], axis=0)
        return jnp.stack((cross, mean))

    columns = [column_terms(block) for block in range(4)]
    far = times(2) + across_core(times(3).astype(low)).astype(full)
    far = across_chip(far.astype(low))
    up_b = times(0) + across_core(times(1).astype(low)).astype(full) + far.astype(full)
    small = across_core(
        jnp.concatenate((columns[1], columns[3], jnp.full((2, width), part_loss)))
    )
    part_loss = part_loss + small[4, 0]
    near = columns[0] + small[0:2]
    distant = across_chip(
        jnp.concatenate((columns[2] + small[2:4], jnp.full((2, width), part_loss)))
    )
    loss = part_loss + distant[2, 0]
    cross_b, mean_up_b = near + distant[0:2]
    up_a = sum(
        lax.dot_general(
            lows[block], slopes[block], (((1,), (1,)), ((), ())), preferred_element_type=full
        )
        for block in (2, 3, 0, 1)
    )
    grad_a = (inv_a * (up_a - mean_up_a - norm_a * cross_a)).astype(low)
    grad_b = (inv_b * (up_b - mean_up_b - norm_b * cross_b)).astype(low)
    return (loss, grad_a, grad_b)


def solution(mesh):
    in_specs = (P("dp", "feat"), P("dp", "feat"))
    out_specs = (P(), P("dp", "feat"), P("dp", "feat"))
    return jax.shard_map(
        on_device, mesh=mesh, in_specs=in_specs, out_specs=out_specs, check_vma=False
    )
```

```python
import jax
import jax.numpy as jnp
from jax import lax
from jax.sharding import PartitionSpec as P

epsilon = 1e-05
off_weight = 0.0051
low = jnp.bfloat16
full = jnp.float32


def at_z(step):
    return "dp", lambda d: d // 4 * 4 + (d + step) % 4


def at_y(step):
    return "dp", lambda d: d // 16 * 16 + (d // 4 + step) % 4 * 4 + d % 4


def flip(bits):
    return "dp", lambda d: d ^ bits


core = ("feat", lambda f: f ^ 1)
chip = ("feat", lambda f: f ^ 2)


def stage(sends, after=()):
    held = lax.optimization_barrier(tuple(values for values, _ in sends) + tuple(after))
    received = []
    for values, (_, (axis, place)) in zip(held, sends):
        count = lax.axis_size(axis)
        received.append(lax.ppermute(values, axis, [(d, place(d)) for d in range(count)]))
    return received


def share(values):
    count = lax.axis_size("dp")
    pieces = jnp.broadcast_to(values[None], (count,) + values.shape)
    return lax.all_to_all(pieces, "dp", 0, 0, tiled=True)


def local_moments(values):
    mean = jnp.mean(values, axis=0)
    centred = values - mean
    return mean, jnp.sum(centred * centred, axis=0)


def combine(means, squares, pairs):
    count = means.shape[0]
    mean = jnp.mean(means, axis=0)
    shift = means - mean
    var = (jnp.sum(squares, axis=0) + (pairs // count) * jnp.sum(shift * shift, axis=0)) / pairs
    return mean, lax.rsqrt(var + epsilon)


def add(one, other):
    return one.astype(full) + other.astype(full)


def ring_far(far, place):
    half = far.shape[0] // 2
    return [(far[:half], place(1)), (far[half:], place(3))]


def ring_near(above, below, from_below, from_above, place):
    half = from_below.shape[0]
    above = jnp.concatenate((add(above[:half], from_below).astype(low), above[half:]))
    below = jnp.concatenate((below[:half], add(below[half:], from_above).astype(low)))
    return [(above, place(1)), (below, place(3))]


def pick(stack, index, axis):
    return lax.dynamic_index_in_dim(stack, index, axis, keepdims=False)


def spread(block, place):
    return [(block, place(1)), (block, place(3))]


def forward(from_below, from_above, place):
    half = from_below.shape[0] // 2
    return [(from_below[:half], place(1)), (from_above[half:], place(3))]


def assemble(block, from_below, from_above, far_top, far_bottom, position):
    rows = block.shape[0]
    gathered = jnp.zeros((4 * rows,) + block.shape[1:], block.dtype)
    for step, part in ((0, block), (3, from_below), (1, from_above)):
        start = ((position + step) & 3) * rows
        gathered = lax.dynamic_update_slice_in_dim(gathered, part, start, 0)
    start = ((position + 2) & 3) * rows
    gathered = lax.dynamic_update_slice_in_dim(gathered, far_top, start, 0)
    return lax.dynamic_update_slice_in_dim(gathered, far_bottom, start + rows // 2, 0)


def on_device(view_a, view_b):
    dp_count = lax.axis_size("dp")
    rows, width = view_a.shape
    pairs = rows * dp_count
    dp_index = lax.axis_index("dp")
    xi, yi, zi = dp_index >> 4, (dp_index >> 2) & 3, dp_index & 3
    view_c = stage([(view_b, chip)])[0]
    first = view_a.astype(full)
    second = view_b.astype(full)
    moments = jnp.stack(local_moments(first) + local_moments(second))
    shared = share(moments.reshape(-1, 128)).reshape(dp_count, 4, width)
    mean_a, inv_a = combine(shared[:, 0], shared[:, 1], pairs)
    mean_b, inv_b = combine(shared[:, 2], shared[:, 3], pairs)
    norm_a = (first - mean_a) * inv_a
    norm_b = (second - mean_b) * inv_b
    low_a = norm_a.astype(low)
    low_b = norm_b.astype(low)
    stats_c, low_d = stage([(jnp.stack((mean_b, inv_b)), chip), (low_b, core)])
    low_c = ((view_c.astype(full) - stats_c[0]) * stats_c[1]).astype(low)
    lows = [low_b, low_d, low_c, stage([(low_c, core)])[0]]

    def chunk(block, position, step):
        start = ((position + step) & 3) * 256
        columns = lax.dynamic_slice_in_dim(low_a, start, 256, 1)
        return lax.dot_general(
            columns, lows[block], (((0,), (0,)), ((), ())), preferred_element_type=full
        ).astype(low)

    ends = jnp.concatenate(
        (
            jnp.sum(low_a.astype(full) * low_b.astype(full), axis=0),
            jnp.sum(low_a.astype(full), axis=0),
            jnp.sum(low_b.astype(full), axis=0),
        )
    ).reshape(-1, 128)

    sums = [None] * 4
    before = []
    for even, odd, bits in ((0, 1, (1, 2)), (2, 3, (4, 8))):
        sends = ring_far(chunk(even, zi, 2), at_z) + ring_far(chunk(odd, yi, 2), at_y)
        got = stage(sends + [(ends, flip(bits[0]))], before)
        ends = ends + got[4]
        before = got[:4]
        sends = ring_near(
            chunk(even, zi, 1), chunk(even, zi, 3), got[0], got[1], at_z
        ) + ring_near(chunk(odd, yi, 1), chunk(odd, yi, 3), got[2], got[3], at_y)
        got = stage(sends + [(ends, flip(bits[1]))])
        ends = ends + got[4]
        sums[even] = add(chunk(even, zi, 0), got[0]) + got[1].astype(full)
        sums[odd] = add(chunk(odd, yi, 0), got[2]) + got[3].astype(full)

    blocks = [
        jnp.stack((sums[0], sums[2])).reshape(2, 4, 64, width),
        jnp.stack((sums[1], sums[3])).reshape(2, 4, 64, width),
    ]
    ways = ((at_y, yi), (at_z, zi))
    sends = [
        (pick(part.astype(low), (position + step) & 3, 1), place(step))
        for part, (place, position) in zip(blocks, ways)
        for step in (1, 2, 3)
    ]
    got = stage(sends + [(ends, flip(16))])
    ends = (ends + got[6]) / pairs
    diagonal, low_mean_a, low_mean_b = ends.reshape(3, width)
    halves = []
    for index, (part, (_, position)) in enumerate(zip(blocks, ways)):
        total = pick(part, position, 1)
        for other in got[3 * index : 3 * index + 3]:
            total = total + other.astype(full)
        halves.append(total.reshape(2, 2, 32, width))
    got = stage(
        [(pick(half, 1 - xi, 1).astype(low), flip(16)) for half in halves] + [(low_mean_b, chip)]
    )
    low_mean_c = got[2]
    even, odd = (
        (pick(half, xi, 1) + other.astype(full)) / pairs for half, other in zip(halves, got)
    )

    own = zi * 256 + yi * 64 + xi * 32
    diagonal_rows = lax.dynamic_slice_in_dim(diagonal, own, 32, 0)
    shape = even.shape
    on_diagonal = (
        lax.broadcasted_iota(jnp.int32, shape, 2)
        == own + lax.broadcasted_iota(jnp.int32, shape, 1)
    ) & (lax.broadcasted_iota(jnp.int32, shape, 0) == 0)
    even = jnp.where(on_diagonal, diagonal_rows[None, :, None], even)
    slopes_even = jnp.where(on_diagonal, -2.0 * (1.0 - even), 2.0 * off_weight * even).astype(low)
    slopes_odd = (2.0 * off_weight * odd).astype(low)
    loss = jnp.sum(
        jnp.where(on_diagonal, (1.0 - even) * (1.0 - even), off_weight * even * even)
    ) + jnp.sum(off_weight * odd * odd)
    loss = jnp.full((8, 128), loss)

    tiles = [slopes_even, slopes_odd]
    got = stage(
        [(tile, flip(16)) for tile in tiles]
        + [(loss, flip(16)), (jnp.stack((low_mean_b, low_mean_c)), core)]
    )
    loss = loss + got[2]
    low_means = [low_mean_b, got[3][0], low_mean_c, got[3][1]]
    both = [
        jnp.where(
            xi == 0,
            jnp.concatenate((tile, other), axis=1),
            jnp.concatenate((other, tile), axis=1),
        )
        for tile, other in zip(tiles, got)
    ]
    got = stage(
        [(pair, place(step)) for pair, (place, _) in zip(both, ways) for step in (1, 2, 3)]
        + [(loss, flip(4))]
    )
    loss = loss + got[6]
    blocks = []
    for index, (pair, (_, position)) in enumerate(zip(both, ways)):
        gathered = jnp.zeros((2, 4) + pair.shape[1:], low)
        gathered = lax.dynamic_update_index_in_dim(gathered, pair, position, 1)
        for step in (1, 2, 3):
            part = got[3 * index + step - 1]
            gathered = lax.dynamic_update_index_in_dim(gathered, part, (position - step) & 3, 1)
        blocks.append(gathered.reshape(2, 256, width))

    def times(block):
        return jnp.dot(low_a, slopes[block], preferred_element_type=full)

    slopes = [None] * 4
    before = []
    for even, odd, bits in ((2, 3, (8, 1)), (0, 1, (2, None))):
        tile_even, tile_odd = blocks[0][even // 2], blocks[1][even // 2]
        sends = spread(tile_even, at_z) + spread(tile_odd, at_y) + [(loss, flip(bits[0]))]
        got = stage(sends, before)
        loss = loss + got[4]
        sends = forward(got[0], got[1], at_z) + forward(got[2], got[3], at_y)
        if even:
            sends.append((loss, flip(bits[1])))
        else:
            sends.append((across.astype(low), chip))
        far = stage(sends)
        slopes[even] = assemble(tile_even, got[0], got[1], far[0], far[1], zi)
        slopes[odd] = assemble(tile_odd, got[2], got[3], far[2], far[3], yi)
        before = far[:4]
        if even:
            loss = loss + far[4]
            across = times(2) + stage([(times(3).astype(low), core)])[0].astype(full)
        else:
            across = far[4]

    own_diagonal = lax.broadcasted_iota(jnp.int32, (width, width), 0) == lax.broadcasted_iota(
        jnp.int32, (width, width), 1
    )
    diagonal_term = (-2.0 * (1.0 - diagonal)).astype(low).astype(full) * diagonal
    columns = []
    row_cross = diagonal_term
    row_mean = jnp.zeros((width,), full)
    for block in (2, 3, 0, 1):
        slope = slopes[block].astype(full)
        squares = slope * slope / (2.0 * off_weight)
        if block == 0:
            squares = jnp.where(own_diagonal, 0.0, squares)
        cross = jnp.sum(squares, axis=0)
        if block == 0:
            cross = cross + diagonal_term
        columns.append(jnp.stack((cross, jnp.sum(slope * low_mean_a[:, None], axis=0))))
        row_cross = row_cross + jnp.sum(squares, axis=1)
        row_mean = row_mean + jnp.sum(slope * low_means[block], axis=1)
    near, small = stage(
        [
            (times(1).astype(low), core),
            (jnp.concatenate((columns[1], columns[3], jnp.full((2, width), loss[0, 0]))), core),
        ]
    )
    distant = stage(
        [
            (
                jnp.concatenate(
                    (columns[0] + small[0:2], jnp.full((2, width), loss[0, 0]) + small[4:6])
                ),
                chip,
            )
        ]
    )[0]
    loss = loss[0, 0] + small[4, 0] + distant[2, 0]
    cross_b, mean_up_b = columns[2] + small[2:4] + distant[0:2]
    up_b = times(0) + near.astype(full) + across.astype(full)
    up_a = sum(
        lax.dot_general(
            lows[block], slopes[block], (((1,), (1,)), ((), ())), preferred_element_type=full
        )
        for block in (2, 3, 0, 1)
    )
    grad_a = (inv_a * (up_a - row_mean - norm_a * row_cross)).astype(low)
    grad_b = (inv_b * (up_b - mean_up_b - norm_b * cross_b)).astype(low)
    return (loss, grad_a, grad_b)


def solution(mesh):
    in_specs = (P("dp", "feat"), P("dp", "feat"))
    out_specs = (P(), P("dp", "feat"), P("dp", "feat"))
    return jax.shard_map(
        on_device, mesh=mesh, in_specs=in_specs, out_specs=out_specs, check_vma=False
    )
```

```python
import jax
import jax.numpy as jnp
from jax import lax
from jax.sharding import PartitionSpec as P

epsilon = 1e-05
off_weight = 0.0051
low = jnp.bfloat16
full = jnp.float32


def at_z(step):
    return "dp", lambda d: d // 4 * 4 + (d + step) % 4


def at_y(step):
    return "dp", lambda d: d // 16 * 16 + (d // 4 + step) % 4 * 4 + d % 4


def flip(bits):
    return "dp", lambda d: d ^ bits


core = ("feat", lambda f: f ^ 1)
chip = ("feat", lambda f: f ^ 2)


def stage(sends, after=()):
    held = lax.optimization_barrier(tuple(values for values, _ in sends) + tuple(after))
    received = []
    for values, (_, (axis, place)) in zip(held, sends):
        count = lax.axis_size(axis)
        received.append(lax.ppermute(values, axis, [(d, place(d)) for d in range(count)]))
    return received


def share(values):
    count = lax.axis_size("dp")
    pieces = jnp.broadcast_to(values[None], (count,) + values.shape)
    return lax.all_to_all(pieces, "dp", 0, 0, tiled=True)


def combine(means, squares, pairs):
    count = means.shape[0]
    mean = jnp.mean(means, axis=0)
    shift = means - mean
    shifts = jnp.stack((shift[:, 0] ** 2, shift[:, 1] ** 2, shift[:, 0] * shift[:, 1]), axis=1)
    products = jnp.sum(squares + (pairs // count) * shifts, axis=0) / pairs
    inverse = lax.rsqrt(products[:2] + epsilon)
    return mean, inverse, products[2] * inverse[0] * inverse[1]


def add(one, other):
    return one.astype(full) + other.astype(full)


def pick(stack, index, axis):
    return lax.dynamic_index_in_dim(stack, index, axis, keepdims=False)


def put(stack, part, start):
    return lax.dynamic_update_slice_in_dim(stack, part, start, 0)


def three_parts(value):
    first = lax.reduce_precision(value, 8, 7)
    second = lax.reduce_precision(value - first, 8, 7)
    return first, second, value - first - second


def around(block, place):
    return [(block, place(step)) for step in (2, 1, 3)]


def assemble(block, others, position):
    rows = block.shape[0]
    gathered = jnp.zeros((4 * rows,) + block.shape[1:], block.dtype)
    for step, part in zip((0, 2, 1, 3), [block] + others):
        gathered = put(gathered, part, ((position - step) & 3) * rows)
    return gathered


def on_device(view_a, view_b):
    dp_count = lax.axis_size("dp")
    rows, width = view_a.shape
    pairs = rows * dp_count
    dp_index = lax.axis_index("dp")
    xi, yi, zi = dp_index >> 4, (dp_index >> 2) & 3, dp_index & 3
    view_c = stage([(view_b, chip)])[0]
    first = view_a.astype(full)
    second = view_b.astype(full)
    means = jnp.stack((jnp.mean(first, axis=0), jnp.mean(second, axis=0)))
    rest_a, rest_b = first - means[0], second - means[1]
    products = jnp.stack(
        (
            jnp.sum(rest_a * rest_a, axis=0),
            jnp.sum(rest_b * rest_b, axis=0),
            jnp.sum(rest_a * rest_b, axis=0),
        )
    )
    shared = share(jnp.concatenate((means, products)).reshape(-1, 128))
    shared = shared.reshape(dp_count, 5, width)
    mean, inverse, diagonal = combine(shared[:, :2], shared[:, 2:], pairs)
    inv_a, inv_b = inverse
    stats_c = stage([(jnp.stack((mean[1], inv_b)), chip)])[0]
    norm_a = (first - mean[0]) * inv_a
    norm_b = (second - mean[1]) * inv_b
    low_a = norm_a.astype(low)
    norm_c = (view_c.astype(full) - stats_c[0]) * stats_c[1]

    low_even = jnp.concatenate((norm_b.astype(low), norm_c.astype(low)), axis=1)
    low_odd = stage([(low_even, core)])[0]
    lows = [low_even[:, :width], low_odd[:, :width], low_even[:, width:], low_odd[:, width:]]
    ways = ((low_even, at_z, zi), (low_odd, at_y, yi))

    def product(right, start, size):
        columns = lax.dynamic_slice_in_dim(low_a, start, size, 1)
        return lax.dot_general(
            columns, right, (((0,), (0,)), ((), ())), preferred_element_type=full
        )

    sends = []
    for right, place, position in ways:
        start = ((position + 2) & 3) * 256
        sends.append((product(right, start, 128).astype(low), place(1)))
        sends.append((product(right, start + 128, 128).astype(low), place(3)))
    got = stage(sends)
    sends = []
    for index, (right, place, position) in enumerate(ways):
        above = product(right, ((position + 1) & 3) * 256, 256).astype(low)
        below = product(right, ((position + 3) & 3) * 256, 256).astype(low)
        above = put(above, add(above[:128], got[2 * index]).astype(low), 0)
        below = put(below, add(below[128:], got[2 * index + 1]).astype(low), 128)
        sends.extend(((above, place(1)), (below, place(3))))
    local = jnp.concatenate(
        (
            jnp.sum(low_a.astype(full), axis=0),
            jnp.sum(low_even.astype(full), axis=0),
            jnp.sum(low_odd.astype(full), axis=0),
        )
    )
    local, got = lax.optimization_barrier((local, got))
    low_means = jnp.sum(share(local.reshape(-1, 128)), axis=0).reshape(5, width) / pairs
    got = stage(sends)
    sums = [
        product(right, position * 256, 256) + add(got[2 * index], got[2 * index + 1])
        for index, (right, _, position) in enumerate(ways)
    ]

    others = ((at_y, yi), (at_z, zi))
    blocks = [part.reshape(4, 64, 2 * width) for part in sums]
    sends = [
        (pick(part, (position + step) & 3, 0).astype(low), place(step))
        for step in (2, 1, 3)
        for part, (place, position) in zip(blocks, others)
    ]
    low_means, blocks = lax.optimization_barrier((low_means, blocks))
    got = stage(sends)
    halves = jnp.stack(
        [
            sum((other.astype(full) for other in got[index::2]), pick(part, position, 0))
            for index, (part, (_, position)) in enumerate(zip(blocks, others))
        ]
    ).reshape(2, 2, 32, 2 * width)
    got = stage([(pick(halves, 1 - xi, 1).astype(low), flip(16))])[0]
    corr = (pick(halves, xi, 1) + got.astype(full)) / pairs

    own = zi * 256 + yi * 64 + xi * 32
    diagonal_rows = lax.dynamic_slice_in_dim(diagonal, own, 32, 0)
    shape = corr.shape
    on_diagonal = (
        lax.broadcasted_iota(jnp.int32, shape, 2)
        == own + lax.broadcasted_iota(jnp.int32, shape, 1)
    ) & (lax.broadcasted_iota(jnp.int32, shape, 0) == 0)
    loss = jnp.sum(jnp.where(on_diagonal, 0.0, off_weight * corr * corr)) + jnp.sum(
        (1.0 - diagonal_rows) * (1.0 - diagonal_rows)
    )
    row = lax.broadcasted_iota(jnp.int32, (32, 1), 0)
    slots = jnp.zeros((32, 1), full)
    for index, part in enumerate(three_parts(loss)):
        slots = jnp.where(row == index, part, slots)
    tiles = jnp.where(on_diagonal, slots, 2.0 * off_weight * corr).astype(low)

    got = stage([(tiles, flip(16))])[0]
    both = jnp.where(
        xi == 0,
        jnp.concatenate((tiles, got), axis=1),
        jnp.concatenate((got, tiles), axis=1),
    )
    got = stage(
        [(both[index], place(step)) for step in (2, 1, 3) for index, (place, _) in enumerate(others)]
    )
    blocks = [
        assemble(both[index], got[index::2], position) for index, (_, position) in enumerate(others)
    ]

    def times(block):
        return jnp.dot(low_a, slopes[block], preferred_element_type=full)

    slopes = [None] * 4
    near_even, near_odd = blocks[0][:, width:], blocks[1][:, width:]
    got = stage(around(near_even, at_z) + around(near_odd, at_y))
    slopes[2] = assemble(near_even, got[:3], zi)
    slopes[3] = assemble(near_odd, got[3:], yi)
    across = times(2) + stage([(times(3).astype(low), core)])[0].astype(full)
    near_even, near_odd = blocks[0][:, :width], blocks[1][:, :width]
    got = stage([(across.astype(low), chip)] + around(near_even, at_z) + around(near_odd, at_y))
    across = got[0]
    slopes[0] = assemble(near_even, got[1:4], zi)
    slopes[1] = assemble(near_odd, got[4:], yi)

    own_diagonal = lax.broadcasted_iota(jnp.int32, (width, width), 0) == lax.broadcasted_iota(
        jnp.int32, (width, width), 1
    )
    slots = jnp.sum(jnp.where(own_diagonal, slopes[0], 0).astype(full), axis=0)
    loss = jnp.sum(slots.reshape(32, 32)[:, :3])
    diagonal_slope = (-2.0 * (1.0 - diagonal)).astype(low)
    slopes[0] = jnp.where(own_diagonal, diagonal_slope, slopes[0])
    diagonal_term = diagonal_slope.astype(full) * diagonal
    columns = []
    row_cross = diagonal_term
    row_mean = jnp.zeros((width,), full)
    for block, mean_row in ((2, 2), (3, 4), (0, 1), (1, 3)):
        slope = slopes[block].astype(full)
        squares = slope * slope / (2.0 * off_weight)
        if block == 0:
            squares = jnp.where(own_diagonal, 0.0, squares)
        cross = jnp.sum(squares, axis=0)
        if block == 0:
            cross = cross + diagonal_term
        columns.append(jnp.stack((cross, jnp.sum(slope * low_means[0][:, None], axis=0))))
        row_cross = row_cross + jnp.sum(squares, axis=1)
        row_mean = row_mean + jnp.sum(slope * low_means[mean_row], axis=1)
    near, small = stage(
        [
            (times(1).astype(low), core),
            (jnp.concatenate((columns[1], columns[3], jnp.full((2, width), loss))), core),
        ]
    )
    distant = stage(
        [(jnp.concatenate((columns[0] + small[0:2], jnp.full((2, width), loss) + small[4:6])), chip)]
    )[0]
    loss = loss + small[4, 0] + distant[2, 0]
    cross_b, mean_up_b = columns[2] + small[2:4] + distant[0:2]
    up_b = times(0) + near.astype(full) + across.astype(full)
    up_a = sum(
        lax.dot_general(
            lows[block], slopes[block], (((1,), (1,)), ((), ())), preferred_element_type=full
        )
        for block in (2, 3, 0, 1)
    )
    grad_a = (inv_a * (up_a - row_mean - norm_a * row_cross)).astype(low)
    grad_b = (inv_b * (up_b - mean_up_b - norm_b * cross_b)).astype(low)
    return (loss, grad_a, grad_b)


def solution(mesh):
    in_specs = (P("dp", "feat"), P("dp", "feat"))
    out_specs = (P(), P("dp", "feat"), P("dp", "feat"))
    return jax.shard_map(
        on_device, mesh=mesh, in_specs=in_specs, out_specs=out_specs, check_vma=False
    )
```

```python
import jax
import jax.numpy as jnp
from jax import lax
from jax.sharding import PartitionSpec as P

epsilon = 1e-05
off_weight = 0.0051
low = jnp.bfloat16
full = jnp.float32


def at_z(step):
    return "dp", lambda d: d // 4 * 4 + (d + step) % 4


def at_y(step):
    return "dp", lambda d: d // 16 * 16 + (d // 4 + step) % 4 * 4 + d % 4


def flip(bits):
    return "dp", lambda d: d ^ bits


core = ("feat", lambda f: f ^ 1)
chip = ("feat", lambda f: f ^ 2)


def stage(sends, after=()):
    held = lax.optimization_barrier(tuple(values for values, _ in sends) + tuple(after))
    received = []
    for values, (_, (axis, place)) in zip(held, sends):
        count = lax.axis_size(axis)
        received.append(lax.ppermute(values, axis, [(d, place(d)) for d in range(count)]))
    return received


def together(sends):
    return list(lax.optimization_barrier(tuple(stage(sends))))


def share(values):
    count = lax.axis_size("dp")
    pieces = jnp.broadcast_to(values[None], (count,) + values.shape)
    return lax.all_to_all(pieces, "dp", 0, 0, tiled=True)


def combine(means, squares, pairs):
    count = means.shape[0]
    mean = jnp.mean(means, axis=0)
    shift = means - mean
    shifts = jnp.stack((shift[:, 0] ** 2, shift[:, 1] ** 2, shift[:, 0] * shift[:, 1]), axis=1)
    products = jnp.sum(squares + (pairs // count) * shifts, axis=0) / pairs
    inverse = lax.rsqrt(products[:2] + epsilon)
    return mean, inverse, products[2] * inverse[0] * inverse[1]


def add(one, other):
    return one.astype(full) + other.astype(full)


def pick(stack, index, axis):
    return lax.dynamic_index_in_dim(stack, index, axis, keepdims=False)


def put(stack, part, start):
    return lax.dynamic_update_slice_in_dim(stack, part, start, 0)


def three_parts(value):
    first = lax.reduce_precision(value, 8, 7)
    second = lax.reduce_precision(value - first, 8, 7)
    return first, second, value - first - second


def around(block, place):
    return [(block, place(step)) for step in (2, 1, 3)]


def assemble(block, others, position):
    rows = block.shape[0]
    gathered = jnp.zeros((4 * rows,) + block.shape[1:], block.dtype)
    for step, part in zip((0, 2, 1, 3), [block] + others):
        gathered = put(gathered, part, ((position - step) & 3) * rows)
    return gathered


def on_device(view_a, view_b):
    dp_count = lax.axis_size("dp")
    rows, width = view_a.shape
    pairs = rows * dp_count
    dp_index = lax.axis_index("dp")
    xi, yi, zi = dp_index >> 4, (dp_index >> 2) & 3, dp_index & 3
    view_c = stage([(view_b, chip)])[0]
    first = view_a.astype(full)
    second = view_b.astype(full)
    means = jnp.stack((jnp.mean(first, axis=0), jnp.mean(second, axis=0)))
    rest_a, rest_b = first - means[0], second - means[1]
    products = jnp.stack(
        (
            jnp.sum(rest_a * rest_a, axis=0),
            jnp.sum(rest_b * rest_b, axis=0),
            jnp.sum(rest_a * rest_b, axis=0),
        )
    )
    shared = share(jnp.concatenate((means, products)).reshape(-1, 128))
    shared, view_c = lax.optimization_barrier((shared, view_c))
    shared = shared.reshape(dp_count, 5, width)
    mean, inverse, diagonal = combine(shared[:, :2], shared[:, 2:], pairs)
    inv_a, inv_b = inverse
    stats_c = stage([(jnp.stack((mean[1], inv_b)), chip)])[0]
    norm_a = (first - mean[0]) * inv_a
    norm_b = (second - mean[1]) * inv_b
    low_a = norm_a.astype(low)
    norm_c = (view_c.astype(full) - stats_c[0]) * stats_c[1]

    low_even = jnp.concatenate((norm_b.astype(low), norm_c.astype(low)), axis=1)
    low_odd = stage([(low_even, core)])[0]
    lows = [low_even[:, :width], low_odd[:, :width], low_even[:, width:], low_odd[:, width:]]
    ways = ((low_even, at_z, zi), (low_odd, at_y, yi))

    def product(right, start, size):
        columns = lax.dynamic_slice_in_dim(low_a, start, size, 1)
        return lax.dot_general(
            columns, right, (((0,), (0,)), ((), ())), preferred_element_type=full
        )

    local = jnp.concatenate(
        (
            jnp.sum(low_a.astype(full), axis=0),
            jnp.sum(low_even.astype(full), axis=0),
            jnp.sum(low_odd.astype(full), axis=0),
        )
    )
    sends = [
        (product(right, ((position + step) & 3) * 256, 256).astype(low), place(step))
        for right, place, position in ways
        for step in (2, 1, 3)
    ]
    got = [stage([send])[0] for send in sends]
    low_means = jnp.sum(share(local.reshape(-1, 128)), axis=0).reshape(5, width) / pairs
    got = lax.optimization_barrier(tuple(got))
    sums = [
        sum(
            (other.astype(full) for other in got[3 * index : 3 * index + 3]),
            product(right, position * 256, 256),
        )
        for index, (right, _, position) in enumerate(ways)
    ]

    others = ((at_y, yi), (at_z, zi))
    blocks = [part.reshape(4, 64, 2 * width) for part in sums]
    sends = [
        (pick(part, (position + step) & 3, 0).astype(low), place(step))
        for step in (2, 1, 3)
        for part, (place, position) in zip(blocks, others)
    ]
    low_means, blocks = lax.optimization_barrier((low_means, blocks))
    got = stage(sends)
    halves = jnp.stack(
        [
            sum((other.astype(full) for other in got[index::2]), pick(part, position, 0))
            for index, (part, (_, position)) in enumerate(zip(blocks, others))
        ]
    ).reshape(2, 2, 32, 2 * width)
    got = stage([(pick(halves, 1 - xi, 1).astype(low), flip(16))])[0]
    corr = (pick(halves, xi, 1) + got.astype(full)) / pairs

    own = zi * 256 + yi * 64 + xi * 32
    diagonal_rows = lax.dynamic_slice_in_dim(diagonal, own, 32, 0)
    shape = corr.shape
    on_diagonal = (
        lax.broadcasted_iota(jnp.int32, shape, 2)
        == own + lax.broadcasted_iota(jnp.int32, shape, 1)
    ) & (lax.broadcasted_iota(jnp.int32, shape, 0) == 0)
    loss = jnp.sum(jnp.where(on_diagonal, 0.0, off_weight * corr * corr), axis=(0, 1))
    loss = jnp.sum(loss.reshape(1, -1), axis=1, keepdims=True) + jnp.sum(
        ((1.0 - diagonal_rows) * (1.0 - diagonal_rows)).reshape(1, -1), axis=1, keepdims=True
    )
    row = lax.broadcasted_iota(jnp.int32, (32, 1), 0)
    slots = jnp.zeros((32, 1), full)
    for index, part in enumerate(three_parts(loss)):
        slots = jnp.where(row == index, part, slots)
    tiles = jnp.where(on_diagonal, slots, 2.0 * off_weight * corr).astype(low)

    got = stage([(tiles, flip(16))])[0]
    both = jnp.where(
        xi == 0,
        jnp.concatenate((tiles, got), axis=1),
        jnp.concatenate((got, tiles), axis=1),
    )
    got = stage(
        [(both[index], place(step)) for step in (2, 1, 3) for index, (place, _) in enumerate(others)]
    )
    blocks = [
        assemble(both[index], got[index::2], position) for index, (_, position) in enumerate(others)
    ]

    def times(block):
        return jnp.dot(low_a, slopes[block], preferred_element_type=full)

    slopes = [None] * 4
    near_even, near_odd = blocks[0][:, width:], blocks[1][:, width:]
    got = together(around(near_even, at_z) + around(near_odd, at_y))
    slopes[2] = assemble(near_even, got[:3], zi)
    slopes[3] = assemble(near_odd, got[3:], yi)
    across = times(2) + stage([(times(3).astype(low), core)])[0].astype(full)
    near_even, near_odd = blocks[0][:, :width], blocks[1][:, :width]
    across, near_even, near_odd = lax.optimization_barrier((across.astype(low), near_even, near_odd))
    across = stage([(across, chip)])[0]
    got = together(
        [(near_even, at_z(1)), (near_even, at_z(3)), (near_odd, at_y(1)), (near_odd, at_y(3))]
    )
    far = together(
        [
            (got[0][:128], at_z(1)),
            (got[1][128:], at_z(3)),
            (got[2][:128], at_y(1)),
            (got[3][128:], at_y(3)),
        ]
    )
    for block, near, index, position in ((0, near_even, 0, zi), (1, near_odd, 2, yi)):
        gathered = assemble(near, [far[index], got[index], got[index + 1]], position)
        start = ((position + 2) & 3) * 256 + 128
        slopes[block] = put(gathered, far[index + 1], start)

    own_diagonal = lax.broadcasted_iota(jnp.int32, (width, width), 0) == lax.broadcasted_iota(
        jnp.int32, (width, width), 1
    )
    slots = jnp.sum(jnp.where(own_diagonal, slopes[0], 0).astype(full), axis=0)
    loss = jnp.sum(slots.reshape(32, 32)[:, :3])
    diagonal_slope = (-2.0 * (1.0 - diagonal)).astype(low)
    slopes[0] = jnp.where(own_diagonal, diagonal_slope, slopes[0])
    diagonal_term = diagonal_slope.astype(full) * diagonal
    columns = []
    row_cross = diagonal_term
    row_mean = jnp.zeros((width,), full)
    for block, mean_row in ((2, 2), (3, 4), (0, 1), (1, 3)):
        slope = slopes[block].astype(full)
        squares = slope * slope / (2.0 * off_weight)
        if block == 0:
            squares = jnp.where(own_diagonal, 0.0, squares)
        cross = jnp.sum(squares, axis=0)
        if block == 0:
            cross = cross + diagonal_term
        columns.append(jnp.stack((cross, jnp.sum(slope * low_means[0][:, None], axis=0))))
        row_cross = row_cross + jnp.sum(squares, axis=1)
        row_mean = row_mean + jnp.sum(slope * low_means[mean_row], axis=1)
    across, near = lax.optimization_barrier((across, times(1).astype(low)))
    near, small = stage(
        [
            (near, core),
            (jnp.concatenate((columns[1], columns[3], jnp.full((2, width), loss))), core),
        ]
    )
    distant = stage(
        [(jnp.concatenate((columns[0] + small[0:2], jnp.full((2, width), loss) + small[4:6])), chip)]
    )[0]
    loss = loss + small[4, 0] + distant[2, 0]
    cross_b, mean_up_b = columns[2] + small[2:4] + distant[0:2]
    up_b = times(0) + near.astype(full) + across.astype(full)
    up_a = sum(
        lax.dot_general(
            lows[block], slopes[block], (((1,), (1,)), ((), ())), preferred_element_type=full
        )
        for block in (2, 3, 0, 1)
    )
    grad_a = (inv_a * (up_a - row_mean - norm_a * row_cross)).astype(low)
    grad_b = (inv_b * (up_b - mean_up_b - norm_b * cross_b)).astype(low)
    return (loss, grad_a, grad_b)


def solution(mesh):
    in_specs = (P("dp", "feat"), P("dp", "feat"))
    out_specs = (P(), P("dp", "feat"), P("dp", "feat"))
    return jax.shard_map(
        on_device, mesh=mesh, in_specs=in_specs, out_specs=out_specs, check_vma=False
    )
```

```python
import jax
import jax.numpy as jnp
from jax import lax
from jax.experimental import pallas as pl
from jax.experimental.pallas import tpu as pltpu
from jax.sharding import PartitionSpec as P

epsilon = 1e-05
off_weight = 0.0051
low = jnp.bfloat16
full = jnp.float32


def at_z(step):
    return "dp", lambda d: d // 4 * 4 + (d + step) % 4


def at_y(step):
    return "dp", lambda d: d // 16 * 16 + (d // 4 + step) % 4 * 4 + d % 4


def flip(bits):
    return "dp", lambda d: d ^ bits


def across_both(member):
    return member ^ (16 * 4 + 2)


core = ("feat", lambda f: f ^ 1)
chip = ("feat", lambda f: f ^ 2)


def stage(sends, after=()):
    held = lax.optimization_barrier(tuple(values for values, _ in sends) + tuple(after))
    received = []
    for values, (_, (axis, place)) in zip(held, sends):
        count = 128 if isinstance(axis, tuple) else lax.axis_size(axis)
        received.append(lax.ppermute(values, axis, [(d, place(d)) for d in range(count)]))
    return received


def together(sends):
    return list(lax.optimization_barrier(tuple(stage(sends))))


def share(values, groups=None):
    count = len(groups[0]) if groups else lax.axis_size("dp")
    pieces = jnp.broadcast_to(values[None], (count,) + values.shape)
    return lax.all_to_all(pieces, "dp", 0, 0, tiled=True, axis_index_groups=groups)


def combine(means, products, rows):
    mean = jnp.mean(means, axis=0)
    shift = means - mean
    shifts = jnp.stack((shift[:, 0] ** 2, shift[:, 1] ** 2, shift[:, 0] * shift[:, 1]), axis=1)
    return mean, jnp.sum(products + rows * shifts, axis=0)


def normalise_kernel(view_b, view_c, stats, out):
    width = view_b.shape[1]
    for index, view in enumerate((view_b, view_c)):
        mean = stats[2 * index : 2 * index + 1, :]
        inverse = stats[2 * index + 1 : 2 * index + 2, :]
        values = (view[...].astype(full) - mean) * inverse
        out[:, index * width : (index + 1) * width] = values.astype(low)


def normalise(view_b, view_c, stats):
    rows, width = view_b.shape
    return pl.pallas_call(
        normalise_kernel,
        grid=(rows // 256,),
        in_specs=[
            pl.BlockSpec((256, width), lambda i: (i, 0)),
            pl.BlockSpec((256, width), lambda i: (i, 0)),
            pl.BlockSpec((8, width), lambda i: (0, 0)),
        ],
        out_specs=pl.BlockSpec((256, 2 * width), lambda i: (i, 0)),
        out_shape=jax.ShapeDtypeStruct((rows, 2 * width), low),
        compiler_params=pltpu.CompilerParams(vmem_limit_bytes=32 * 2**20),
    )(view_b, view_c, stats)


def add_kernel(*refs):
    for index in range(4):
        refs[8 + index][...] = (
            refs[index][...].astype(full) + refs[4 + index][...].astype(full)
        ).astype(low)


def add_halves(blocks, received):
    rows, columns = received[0].shape
    halves = [pl.BlockSpec((rows, 512), lambda i, h=h: (h, i)) for h in (0, 1, 0, 1)]
    return pl.pallas_call(
        add_kernel,
        grid=(columns // 512,),
        in_specs=halves + [pl.BlockSpec((rows, 512), lambda i: (0, i))] * 4,
        out_specs=halves,
        out_shape=[jax.ShapeDtypeStruct(block.shape, low) for block in blocks],
        input_output_aliases={index: index for index in range(4)},
        compiler_params=pltpu.CompilerParams(vmem_limit_bytes=32 * 2**20),
    )(*blocks, *received)


def assemble_kernel(position, *refs):
    step = pl.program_id(0)
    for index in range(4):

        @pl.when(step == index)
        def _():
            refs[4][...] = refs[index][...]


def add(one, other):
    return one.astype(full) + other.astype(full)


def pick(stack, index, axis):
    return lax.dynamic_index_in_dim(stack, index, axis, keepdims=False)


def put(stack, part, start):
    return lax.dynamic_update_slice_in_dim(stack, part, start, 0)


def three_parts(value):
    first = lax.reduce_precision(value, 8, 7)
    second = lax.reduce_precision(value - first, 8, 7)
    return first, second, value - first - second


def around(block, place):
    return [(block, place(step)) for step in (2, 1, 3)]


def assemble(block, others, position):
    rows, columns = block.shape
    return pl.pallas_call(
        assemble_kernel,
        grid_spec=pltpu.PrefetchScalarGridSpec(
            num_scalar_prefetch=1,
            grid=(4,),
            in_specs=[pl.BlockSpec((rows, columns), lambda k, p: (0, 0))] * 4,
            out_specs=pl.BlockSpec(
                (rows, columns),
                lambda k, p: ((p[0] - (k == 1) * 2 - (k == 2) * 1 - (k == 3) * 3) & 3, 0),
            ),
        ),
        out_shape=jax.ShapeDtypeStruct((4 * rows, columns), block.dtype),
        compiler_params=pltpu.CompilerParams(vmem_limit_bytes=32 * 2**20),
    )(position.astype(jnp.int32).reshape(1), block, *others)


def on_device(view_a, view_b):
    dp_count = lax.axis_size("dp")
    rows, width = view_a.shape
    pairs = rows * dp_count
    dp_index = lax.axis_index("dp")
    xi, yi, zi = dp_index >> 4, (dp_index >> 2) & 3, dp_index & 3
    view_c = stage([(view_b, chip)])[0]
    first = view_a.astype(full)
    second = view_b.astype(full)
    means = jnp.stack((jnp.mean(first, axis=0), jnp.mean(second, axis=0)))
    rest_a, rest_b = first - means[0], second - means[1]
    products = jnp.stack(
        (
            jnp.sum(rest_a * rest_a, axis=0),
            jnp.sum(rest_b * rest_b, axis=0),
            jnp.sum(rest_a * rest_b, axis=0),
        )
    )
    half_groups = [[16 * x + i for i in range(16)] for x in range(2)]
    shared = share(jnp.concatenate((means, products)).reshape(-1, 128), half_groups)
    shared = shared.reshape(16, 5, width)
    mean, products = combine(shared[:, :2], shared[:, 2:], rows)
    parts = jnp.concatenate((mean, products))
    part_b = jnp.stack((mean[1], products[1]))
    parts, part_b, view_c = lax.optimization_barrier((parts, part_b, view_c))
    other, part_c, part_d = stage(
        [(parts, flip(16)), (part_b, chip), (part_b, (("dp", "feat"), across_both))]
    )
    both = jnp.stack((parts, other))
    mean, products = combine(both[:, :2], both[:, 2:], pairs // 2)
    inverse = lax.rsqrt(products[:2] / pairs + epsilon)
    inv_a, inv_b = inverse
    diagonal = products[2] / pairs * inv_a * inv_b
    mean_c = 0.5 * (part_c[0] + part_d[0])
    products_c = part_c[1] + part_d[1] + (pairs // 4) * (part_c[0] - part_d[0]) ** 2
    inv_c = lax.rsqrt(products_c / pairs + epsilon)
    stats = jnp.concatenate(
        (jnp.stack((mean[1], inv_b, mean_c, inv_c)), jnp.zeros((4, width), full))
    )
    norm_a = (first - mean[0]) * inv_a
    norm_b = (second - mean[1]) * inv_b
    low_a = norm_a.astype(low)

    low_even = normalise(view_b, view_c, stats)
    low_odd = stage([(low_even, core)])[0]
    lows = [low_even[:, :width], low_odd[:, :width], low_even[:, width:], low_odd[:, width:]]
    ways = ((low_even, at_z, zi), (low_odd, at_y, yi))

    def product(right, start, size):
        columns = lax.dynamic_slice_in_dim(low_a, start, size, 1)
        return lax.dot_general(
            columns, right, (((0,), (0,)), ((), ())), preferred_element_type=full
        )

    sends = []
    for right, place, position in ways:
        start = ((position + 2) & 3) * 256
        sends.append((product(right, start, 128).astype(low), place(1)))
        sends.append((product(right, start + 128, 128).astype(low), place(3)))
    nears = [
        product(right, ((position + step) & 3) * 256, 256).astype(low)
        for right, _, position in ways
        for step in (1, 3)
    ]
    got = together(sends)
    nears = add_halves(nears, got)
    sends = [
        (near, place(step))
        for near, (place, step) in zip(nears, ((at_z, 1), (at_z, 3), (at_y, 1), (at_y, 3)))
    ]
    local = jnp.concatenate(
        (
            jnp.sum(low_a.astype(full), axis=0),
            jnp.sum(low_even.astype(full), axis=0),
            jnp.sum(low_odd.astype(full), axis=0),
        )
    )
    local = share(local.reshape(-1, 128))
    local, got = lax.optimization_barrier((local, tuple(stage(sends))))
    low_means = jnp.sum(local, axis=0).reshape(5, width) / pairs
    sums = [
        product(right, position * 256, 256) + add(got[2 * index], got[2 * index + 1])
        for index, (right, _, position) in enumerate(ways)
    ]

    others = ((at_y, yi), (at_z, zi))
    blocks = [part.reshape(4, 64, 2 * width) for part in sums]
    sends = [
        (pick(part, (position + step) & 3, 0).astype(low), place(step))
        for step in (2, 1, 3)
        for part, (place, position) in zip(blocks, others)
    ]
    got = together(sends)
    halves = jnp.stack(
        [
            sum((other.astype(full) for other in got[index::2]), pick(part, position, 0))
            for index, (part, (_, position)) in enumerate(zip(blocks, others))
        ]
    ).reshape(2, 2, 32, 2 * width)
    got = stage([(pick(halves, 1 - xi, 1).astype(low), flip(16))])[0]
    corr = (pick(halves, xi, 1) + got.astype(full)) / pairs

    own = zi * 256 + yi * 64 + xi * 32
    diagonal_rows = lax.dynamic_slice_in_dim(diagonal, own, 32, 0)
    shape = corr.shape
    on_diagonal = (
        lax.broadcasted_iota(jnp.int32, shape, 2)
        == own + lax.broadcasted_iota(jnp.int32, shape, 1)
    ) & (lax.broadcasted_iota(jnp.int32, shape, 0) == 0)
    loss = jnp.sum(jnp.where(on_diagonal, 0.0, off_weight * corr * corr), axis=(0, 1))
    loss = jnp.sum(loss.reshape(1, -1), axis=1, keepdims=True) + jnp.sum(
        ((1.0 - diagonal_rows) * (1.0 - diagonal_rows)).reshape(1, -1), axis=1, keepdims=True
    )
    row = lax.broadcasted_iota(jnp.int32, (32, 1), 0)
    slots = jnp.zeros((32, 1), full)
    for index, part in enumerate(three_parts(loss)):
        slots = jnp.where(row == index, part, slots)
    tiles = jnp.where(on_diagonal, slots, 2.0 * off_weight * corr).astype(low)

    got = stage([(tiles, flip(16))])[0]
    both = jnp.where(
        xi == 0,
        jnp.concatenate((tiles, got), axis=1),
        jnp.concatenate((got, tiles), axis=1),
    )
    got = together(
        [(both[index], place(step)) for step in (2, 1, 3) for index, (place, _) in enumerate(others)]
    )
    blocks = [
        assemble(both[index], got[index::2], position) for index, (_, position) in enumerate(others)
    ]

    def times(block):
        return jnp.dot(low_a, slopes[block], preferred_element_type=full)

    slopes = [None] * 4
    near_even, near_odd = blocks[0][:, width:], blocks[1][:, width:]
    got = together(around(near_even, at_z) + around(near_odd, at_y))
    slopes[2] = assemble(near_even, got[:3], zi)
    slopes[3] = assemble(near_odd, got[3:], yi)
    across = times(2) + stage([(times(3).astype(low), core)])[0].astype(full)
    near_even, near_odd = blocks[0][:, :width], blocks[1][:, :width]
    across, near_even, near_odd = lax.optimization_barrier((across.astype(low), near_even, near_odd))
    across = stage([(across, chip)])[0]
    got = together(around(near_even, at_z) + around(near_odd, at_y))
    slopes[0] = assemble(near_even, got[:3], zi)
    slopes[1] = assemble(near_odd, got[3:], yi)

    own_diagonal = lax.broadcasted_iota(jnp.int32, (width, width), 0) == lax.broadcasted_iota(
        jnp.int32, (width, width), 1
    )
    slots = jnp.sum(jnp.where(own_diagonal, slopes[0], 0).astype(full), axis=0)
    loss = jnp.sum(slots.reshape(32, 32)[:, :3])
    diagonal_slope = (-2.0 * (1.0 - diagonal)).astype(low)
    slopes[0] = jnp.where(own_diagonal, diagonal_slope, slopes[0])
    diagonal_term = diagonal_slope.astype(full) * diagonal
    columns = []
    row_cross = diagonal_term
    row_mean = jnp.zeros((width,), full)
    for block, mean_row in ((2, 2), (3, 4), (0, 1), (1, 3)):
        slope = slopes[block].astype(full)
        squares = slope * slope / (2.0 * off_weight)
        if block == 0:
            squares = jnp.where(own_diagonal, 0.0, squares)
        cross = jnp.sum(squares, axis=0)
        if block == 0:
            cross = cross + diagonal_term
        columns.append(jnp.stack((cross, jnp.sum(slope * low_means[0][:, None], axis=0))))
        row_cross = row_cross + jnp.sum(squares, axis=1)
        row_mean = row_mean + jnp.sum(slope * low_means[mean_row], axis=1)
    across, near = lax.optimization_barrier((across, times(1).astype(low)))
    near, small = stage(
        [
            (near, core),
            (jnp.concatenate((columns[1], columns[3], jnp.full((2, width), loss))), core),
        ]
    )
    distant = stage(
        [(jnp.concatenate((columns[0] + small[0:2], jnp.full((2, width), loss) + small[4:6])), chip)]
    )[0]
    loss = loss + small[4, 0] + distant[2, 0]
    cross_b, mean_up_b = columns[2] + small[2:4] + distant[0:2]
    up_b = times(0) + near.astype(full) + across.astype(full)
    up_a = sum(
        lax.dot_general(
            lows[block], slopes[block], (((1,), (1,)), ((), ())), preferred_element_type=full
        )
        for block in (2, 3, 0, 1)
    )
    grad_a = (inv_a * (up_a - row_mean - norm_a * row_cross)).astype(low)
    grad_b = (inv_b * (up_b - mean_up_b - norm_b * cross_b)).astype(low)
    return (loss, grad_a, grad_b)


def solution(mesh):
    in_specs = (P("dp", "feat"), P("dp", "feat"))
    out_specs = (P(), P("dp", "feat"), P("dp", "feat"))
    return jax.shard_map(
        on_device, mesh=mesh, in_specs=in_specs, out_specs=out_specs, check_vma=False
    )
```

```python
import functools

import jax
import jax.numpy as jnp
from jax import lax
from jax.experimental import pallas as pl
from jax.experimental.pallas import tpu as pltpu
from jax.sharding import PartitionSpec as P

epsilon = 1e-05
off_weight = 0.0051
low = jnp.bfloat16
full = jnp.float32


def at_z(step):
    return "dp", lambda d: d // 4 * 4 + (d + step) % 4


def at_y(step):
    return "dp", lambda d: d // 16 * 16 + (d // 4 + step) % 4 * 4 + d % 4


def flip(bits):
    return "dp", lambda d: d ^ bits


def across_both(member):
    return member ^ (16 * 4 + 2)


core = ("feat", lambda f: f ^ 1)
chip = ("feat", lambda f: f ^ 2)


def stage(sends, after=()):
    held = lax.optimization_barrier(tuple(values for values, _ in sends) + tuple(after))
    received = []
    for values, (_, (axis, place)) in zip(held, sends):
        count = 128 if isinstance(axis, tuple) else lax.axis_size(axis)
        received.append(lax.ppermute(values, axis, [(d, place(d)) for d in range(count)]))
    return received


def together(sends):
    return list(lax.optimization_barrier(tuple(stage(sends))))


def share(values, groups=None):
    count = len(groups[0]) if groups else lax.axis_size("dp")
    pieces = jnp.broadcast_to(values[None], (count,) + values.shape)
    return lax.all_to_all(pieces, "dp", 0, 0, tiled=True, axis_index_groups=groups)


def combine(means, products, rows):
    mean = jnp.mean(means, axis=0)
    shift = means - mean
    shifts = jnp.stack((shift[:, 0] ** 2, shift[:, 1] ** 2, shift[:, 0] * shift[:, 1]), axis=1)
    return mean, jnp.sum(products + rows * shifts, axis=0)


def normalise_kernel(view_b, view_c, stats, out):
    width = view_b.shape[1]
    for index, view in enumerate((view_b, view_c)):
        mean = stats[2 * index : 2 * index + 1, :]
        inverse = stats[2 * index + 1 : 2 * index + 2, :]
        values = (view[...].astype(full) - mean) * inverse
        out[:, index * width : (index + 1) * width] = values.astype(low)


def normalise(view_b, view_c, stats):
    rows, width = view_b.shape
    return pl.pallas_call(
        normalise_kernel,
        grid=(rows // 256,),
        in_specs=[
            pl.BlockSpec((256, width), lambda i: (i, 0)),
            pl.BlockSpec((256, width), lambda i: (i, 0)),
            pl.BlockSpec((8, width), lambda i: (0, 0)),
        ],
        out_specs=pl.BlockSpec((256, 2 * width), lambda i: (i, 0)),
        out_shape=jax.ShapeDtypeStruct((rows, 2 * width), low),
        compiler_params=pltpu.CompilerParams(vmem_limit_bytes=32 * 2**20),
    )(view_b, view_c, stats)


def add_kernel(*refs):
    for index in range(4):
        refs[8 + index][...] = (
            refs[index][...].astype(full) + refs[4 + index][...].astype(full)
        ).astype(low)


def add_halves(blocks, received):
    rows, columns = received[0].shape
    halves = [pl.BlockSpec((rows, 512), lambda i, h=h: (h, i)) for h in (0, 1, 0, 1)]
    return pl.pallas_call(
        add_kernel,
        grid=(columns // 512,),
        in_specs=halves + [pl.BlockSpec((rows, 512), lambda i: (0, i))] * 4,
        out_specs=halves,
        out_shape=[jax.ShapeDtypeStruct(block.shape, low) for block in blocks],
        input_output_aliases={index: index for index in range(4)},
        compiler_params=pltpu.CompilerParams(vmem_limit_bytes=32 * 2**20),
    )(*blocks, *received)


small_cost = pl.CostEstimate(flops=1, bytes_accessed=1, transcendentals=0)
params = pltpu.CompilerParams(vmem_limit_bytes=48 * 2**20)
over_columns = (((1,), (1,)), ((), ()))


def whole(*shape):
    return pl.BlockSpec(shape, lambda *_: (0,) * len(shape))


def slope_kernel(place, total, received, diagonal, out, *, pairs):
    corr = (total[:, 0] + received[...].astype(full)) / pairs
    shape = corr.shape
    own = place[0]
    row = lax.broadcasted_iota(jnp.int32, shape, 1)
    on_diagonal = (lax.broadcasted_iota(jnp.int32, shape, 2) == own + row) & (
        lax.broadcasted_iota(jnp.int32, shape, 0) == 0
    )
    lane = lax.broadcasted_iota(jnp.int32, diagonal.shape, 1)
    rest = 1.0 - diagonal[...]
    rest = jnp.where((lane >= own) & (lane < own + 32), rest * rest, 0.0)
    loss = jnp.sum(jnp.where(on_diagonal, 0.0, off_weight * corr * corr)) + jnp.sum(rest)
    loss = jnp.full((1, 1, 128), loss)
    high = loss.astype(low).astype(full)
    middle = (loss - high).astype(low).astype(full)
    slots = jnp.zeros(shape, full)
    for index, part in enumerate((high, middle, loss - high - middle)):
        slots = jnp.where(row == index, jnp.max(part), slots)
    out[...] = jnp.where(on_diagonal, slots, 2.0 * off_weight * corr).astype(low)


def slope_tiles(place, halves, received, diagonal, pairs):
    shape = received.shape
    block = (2, 1) + shape[1:]
    return pl.pallas_call(
        functools.partial(slope_kernel, pairs=pairs),
        grid_spec=pltpu.PrefetchScalarGridSpec(
            num_scalar_prefetch=1,
            grid=(1,),
            in_specs=[
                pl.BlockSpec(block, lambda i, p: (0, p[1], 0, 0)),
                whole(*shape),
                whole(1, diagonal.shape[1]),
            ],
            out_specs=whole(*shape),
        ),
        out_shape=jax.ShapeDtypeStruct(shape, low),
        compiler_params=params,
    )(place, halves, received, diagonal)


def product_kernel(left, right, out):
    out[...] = jnp.dot(left[...], right[...], preferred_element_type=full).astype(out.dtype)


def times(left, right, kind):
    rows, depth = left.shape
    columns = right.shape[1]
    return pl.pallas_call(
        product_kernel,
        grid=(rows // 256,),
        in_specs=[pl.BlockSpec((256, depth), lambda i: (i, 0)), whole(depth, columns)],
        out_specs=pl.BlockSpec((256, columns), lambda i: (i, 0)),
        out_shape=jax.ShapeDtypeStruct((rows, columns), kind),
        compiler_params=params,
        cost_estimate=small_cost,
    )(left, right)


def upstream(even, odd, slope_even, slope_odd):
    up = lax.dot_general(even[...], slope_even[...], over_columns, preferred_element_type=full)
    return up + lax.dot_general(odd[...], slope_odd[...], over_columns, preferred_element_type=full)


def part_kernel(even, odd, slope_even, slope_odd, out):
    out[...] = upstream(even, odd, slope_even, slope_odd)


def grad_kernel(even, odd, slope_even, slope_odd, part, view, stats, out):
    up = part[...] + upstream(even, odd, slope_even, slope_odd)
    inverse = stats[1:2]
    norm = (view[...].astype(full) - stats[0:1]) * inverse
    out[...] = (inverse * (up - stats[3:4] - norm * stats[2:3])).astype(low)


def up_a_call(half, low_even, low_odd, slope_even, slope_odd, *more):
    rows = low_even.shape[0]
    width = slope_even.shape[0]
    left = pl.BlockSpec((256, width), lambda i: (i, half))
    tile = pl.BlockSpec((256, width), lambda i: (i, 0))
    square = whole(width, width)
    return pl.pallas_call(
        grad_kernel if more else part_kernel,
        grid=(rows // 256,),
        in_specs=[left, left, square, square] + ([tile, tile, whole(8, width)] if more else []),
        out_specs=tile,
        out_shape=jax.ShapeDtypeStruct((rows, width), low if more else full),
        compiler_params=params,
        cost_estimate=small_cost,
    )(low_even, low_odd, slope_even, slope_odd, *more)


def grad_b_kernel(own, near, across, view, stats, out):
    up = own[...] + near[...].astype(full) + across[...].astype(full)
    inverse = stats[1:2]
    norm = (view[...].astype(full) - stats[0:1]) * inverse
    out[...] = (inverse * (up - stats[3:4] - norm * stats[2:3])).astype(low)


def grad_b_call(own, near, across, view, stats):
    rows, width = own.shape
    tile = pl.BlockSpec((128, width), lambda i: (i, 0))
    return pl.pallas_call(
        grad_b_kernel,
        grid=(rows // 128,),
        in_specs=[tile] * 4 + [whole(8, width)],
        out_specs=tile,
        out_shape=jax.ShapeDtypeStruct((rows, width), low),
        compiler_params=params,
        cost_estimate=small_cost,
    )(own, near, across, view, stats)


def terms_kernel(slope, weights, means, diagonal_slope, columns, rows, *fixed):
    step = pl.program_id(0)

    @pl.when(step == 0)
    def _():
        columns[...] = jnp.zeros_like(columns)

    values = slope[...]
    if fixed:
        shape = values.shape
        on_diagonal = lax.broadcasted_iota(
            jnp.int32, shape, 1
        ) == step * 256 + lax.broadcasted_iota(jnp.int32, shape, 0)
        wide = values.astype(full)
        columns[2:3] += jnp.sum(jnp.where(on_diagonal, wide, 0.0), axis=0, keepdims=True)
        off = jnp.where(on_diagonal, 0.0, wide)
        values = jnp.where(on_diagonal, diagonal_slope[0:1], wide).astype(low)
        fixed[0][...] = values
    else:
        off = values.astype(full)
    squares = off * off * (0.5 / off_weight)
    columns[0:1] += jnp.sum(squares, axis=0, keepdims=True)
    columns[1:2] += jnp.dot(weights[...], values, preferred_element_type=full)[0:1]
    high = squares.astype(low)
    rest = (squares - high.astype(full)).astype(low)
    ones = jnp.ones((8, values.shape[1]), low)
    rows[0:1] = (
        lax.dot_general(ones, high, over_columns, preferred_element_type=full)
        + lax.dot_general(ones, rest, over_columns, preferred_element_type=full)
    )[0:1]
    rows[1:2] = lax.dot_general(means[...], values, over_columns, preferred_element_type=full)[0:1]
    rows[2:8] = jnp.zeros((6, 256), full)


def slope_terms(slope, weights, means, diagonal_slope=None):
    width = slope.shape[0]
    fix = diagonal_slope is not None
    tile = pl.BlockSpec((256, width), lambda i: (i, 0))
    outs = [jax.ShapeDtypeStruct((8, width), full)] * 2
    return pl.pallas_call(
        terms_kernel,
        grid=(4,),
        in_specs=[
            tile,
            pl.BlockSpec((16, 256), lambda i: (0, i)),
            whole(16, width),
            whole(8, width),
        ],
        out_specs=[whole(8, width), pl.BlockSpec((8, 256), lambda i: (0, i))] + [tile] * fix,
        out_shape=outs + [jax.ShapeDtypeStruct(slope.shape, low)] * fix,
        input_output_aliases={0: 2} if fix else {},
        compiler_params=params,
        cost_estimate=small_cost,
    )(slope, weights, means, diagonal_slope if fix else jnp.zeros((8, width), full))


def assemble_kernel(position, *refs):
    step = pl.program_id(0)
    for index in range(4):

        @pl.when(step == index)
        def _():
            refs[4][...] = refs[index][...]


def add(one, other):
    return one.astype(full) + other.astype(full)


def pick(stack, index, axis):
    return lax.dynamic_index_in_dim(stack, index, axis, keepdims=False)


def put(stack, part, start):
    return lax.dynamic_update_slice_in_dim(stack, part, start, 0)


def around(block, place):
    return [(block, place(step)) for step in (2, 1, 3)]


def assemble(block, others, position):
    rows, columns = block.shape
    return pl.pallas_call(
        assemble_kernel,
        grid_spec=pltpu.PrefetchScalarGridSpec(
            num_scalar_prefetch=1,
            grid=(4,),
            in_specs=[pl.BlockSpec((rows, columns), lambda k, p: (0, 0))] * 4,
            out_specs=pl.BlockSpec(
                (rows, columns),
                lambda k, p: ((p[0] - (k == 1) * 2 - (k == 2) * 1 - (k == 3) * 3) & 3, 0),
            ),
        ),
        out_shape=jax.ShapeDtypeStruct((4 * rows, columns), block.dtype),
        compiler_params=pltpu.CompilerParams(vmem_limit_bytes=32 * 2**20),
    )(position.astype(jnp.int32).reshape(1), block, *others)


def on_device(view_a, view_b):
    dp_count = lax.axis_size("dp")
    rows, width = view_a.shape
    pairs = rows * dp_count
    dp_index = lax.axis_index("dp")
    xi, yi, zi = dp_index >> 4, (dp_index >> 2) & 3, dp_index & 3
    view_c = stage([(view_b, chip)])[0]
    first = view_a.astype(full)
    second = view_b.astype(full)
    means = jnp.stack((jnp.mean(first, axis=0), jnp.mean(second, axis=0)))
    rest_a, rest_b = first - means[0], second - means[1]
    products = jnp.stack(
        (
            jnp.sum(rest_a * rest_a, axis=0),
            jnp.sum(rest_b * rest_b, axis=0),
            jnp.sum(rest_a * rest_b, axis=0),
        )
    )
    half_groups = [[16 * x + i for i in range(16)] for x in range(2)]
    shared = share(jnp.concatenate((means, products)).reshape(-1, 128), half_groups)
    shared = shared.reshape(16, 5, width)
    mean, products = combine(shared[:, :2], shared[:, 2:], rows)
    parts = jnp.concatenate((mean, products))
    part_b = jnp.stack((mean[1], products[1]))
    parts, part_b, view_c = lax.optimization_barrier((parts, part_b, view_c))
    other, part_c, part_d = stage(
        [(parts, flip(16)), (part_b, chip), (part_b, (("dp", "feat"), across_both))]
    )
    both = jnp.stack((parts, other))
    mean, products = combine(both[:, :2], both[:, 2:], pairs // 2)
    inverse = lax.rsqrt(products[:2] / pairs + epsilon)
    inv_a, inv_b = inverse
    diagonal = products[2] / pairs * inv_a * inv_b
    mean_c = 0.5 * (part_c[0] + part_d[0])
    products_c = part_c[1] + part_d[1] + (pairs // 4) * (part_c[0] - part_d[0]) ** 2
    inv_c = lax.rsqrt(products_c / pairs + epsilon)
    stats = jnp.concatenate(
        (jnp.stack((mean[1], inv_b, mean_c, inv_c)), jnp.zeros((4, width), full))
    )
    norm_a = (first - mean[0]) * inv_a
    low_a = norm_a.astype(low)

    low_even = normalise(view_b, view_c, stats)
    low_odd = stage([(low_even, core)])[0]
    ways = ((low_even, at_z, zi), (low_odd, at_y, yi))

    def product(right, start, size):
        columns = lax.dynamic_slice_in_dim(low_a, start, size, 1)
        return lax.dot_general(
            columns, right, (((0,), (0,)), ((), ())), preferred_element_type=full
        )

    sends = []
    for right, place, position in ways:
        start = ((position + 2) & 3) * 256
        sends.append((product(right, start, 128).astype(low), place(1)))
        sends.append((product(right, start + 128, 128).astype(low), place(3)))
    nears = [
        product(right, ((position + step) & 3) * 256, 256).astype(low)
        for right, _, position in ways
        for step in (1, 3)
    ]
    got = together(sends)
    nears = add_halves(nears, got)
    sends = [
        (near, place(step))
        for near, (place, step) in zip(nears, ((at_z, 1), (at_z, 3), (at_y, 1), (at_y, 3)))
    ]
    local = jnp.concatenate(
        (
            jnp.sum(low_a.astype(full), axis=0),
            jnp.sum(low_even.astype(full), axis=0),
            jnp.sum(low_odd.astype(full), axis=0),
        )
    )
    local = share(local.reshape(-1, 128))
    local, got = lax.optimization_barrier((local, tuple(stage(sends))))
    low_means = jnp.sum(local, axis=0).reshape(5, width) / pairs
    sums = [
        product(right, position * 256, 256) + add(got[2 * index], got[2 * index + 1])
        for index, (right, _, position) in enumerate(ways)
    ]

    others = ((at_y, yi), (at_z, zi))
    blocks = [part.reshape(4, 64, 2 * width) for part in sums]
    sends = [
        (pick(part, (position + step) & 3, 0).astype(low), place(step))
        for step in (2, 1, 3)
        for part, (place, position) in zip(blocks, others)
    ]
    got = together(sends)
    halves = jnp.stack(
        [
            sum((other.astype(full) for other in got[index::2]), pick(part, position, 0))
            for index, (part, (_, position)) in enumerate(zip(blocks, others))
        ]
    ).reshape(2, 2, 32, 2 * width)
    got = stage([(pick(halves, 1 - xi, 1).astype(low), flip(16))])[0]
    own = zi * 256 + yi * 64 + xi * 32
    place = jnp.stack((own, xi)).astype(jnp.int32)
    tiles = slope_tiles(place, halves, got, diagonal[None], pairs)

    got = stage([(tiles, flip(16))])[0]
    both = jnp.where(
        xi == 0,
        jnp.concatenate((tiles, got), axis=1),
        jnp.concatenate((got, tiles), axis=1),
    )
    got = together(
        [(both[index], place(step)) for step in (2, 1, 3) for index, (place, _) in enumerate(others)]
    )
    blocks = [
        assemble(both[index], got[index::2], position) for index, (_, position) in enumerate(others)
    ]

    diagonal_slope = (-2.0 * (1.0 - diagonal)).astype(low).astype(full)
    wide_slope = jnp.broadcast_to(diagonal_slope, (8, width))
    weights, *means = (jnp.broadcast_to(mean, (16, width)).astype(low) for mean in low_means)
    near_even, near_odd = blocks[0][:, width:], blocks[1][:, width:]
    got = together(around(near_even, at_z) + around(near_odd, at_y))
    slope_d = assemble(near_odd, got[3:], yi)
    slope_c = assemble(near_even, got[:3], zi)
    product_d = stage([(times(low_a, slope_d, low), core)])[0]
    across = add(times(low_a, slope_c, full), product_d).astype(low)
    near_even, near_odd = blocks[0][:, :width], blocks[1][:, :width]
    across, near_even, near_odd = lax.optimization_barrier((across, near_even, near_odd))
    across = stage([(across, chip)])[0]
    columns_c, rows_c = slope_terms(slope_c, weights, means[1])
    columns_d, rows_d = slope_terms(slope_d, weights, means[3])
    part_a = up_a_call(1, low_even, low_odd, slope_c, slope_d)
    got = together(around(near_even, at_z) + around(near_odd, at_y))
    slope_e = assemble(near_odd, got[3:], yi)
    slope_b = assemble(near_even, got[:3], zi)
    near = times(low_a, slope_e, low)
    columns_b, rows_b, slope_b = slope_terms(slope_b, weights, means[0], wide_slope)
    columns_e, rows_e = slope_terms(slope_e, weights, means[2])
    loss = jnp.sum(columns_b[2].reshape(32, 32)[:, :3])
    loss_row = jnp.full((1, width), loss)
    small = jnp.concatenate((columns_e[:2], columns_d[:2], loss_row))
    across, near, small = lax.optimization_barrier((across, near, small))
    near, small = stage([(near, core), (small, core)])
    distant = stage([(jnp.concatenate((columns_c[:2] + small[2:4], loss_row + small[4:5])), chip)])[0]
    loss = loss + small[4, 0] + distant[2, 0]
    zeros = jnp.zeros((4, width), full)
    diagonal_term = diagonal_slope * diagonal
    rows_a = rows_b[:2] + rows_c[:2] + rows_d[:2] + rows_e[:2]
    rows_a = jnp.concatenate(((rows_a[0] + diagonal_term)[None], rows_a[1:2]))
    stats_a = jnp.concatenate((mean[0:1], inv_a[None], rows_a, zeros))
    grad_a = up_a_call(0, low_even, low_odd, slope_b, slope_e, part_a, view_a, stats_a)
    columns = columns_b[:2] + small[0:2] + distant[0:2]
    columns = jnp.concatenate(((columns[0] + diagonal_term)[None], columns[1:2]))
    stats_b = jnp.concatenate((mean[1:2], inv_b[None], columns, zeros))
    grad_b = grad_b_call(times(low_a, slope_b, full), near, across, view_b, stats_b)
    return (loss, grad_a, grad_b)


def solution(mesh):
    in_specs = (P("dp", "feat"), P("dp", "feat"))
    out_specs = (P(), P("dp", "feat"), P("dp", "feat"))
    return jax.shard_map(
        on_device, mesh=mesh, in_specs=in_specs, out_specs=out_specs, check_vma=False
    )
```

```python
import functools

import jax
import jax.numpy as jnp
from jax import lax
from jax.experimental import pallas as pl
from jax.experimental.pallas import tpu as pltpu
from jax.sharding import PartitionSpec as P

epsilon = 1e-05
off_weight = 0.0051
low = jnp.bfloat16
full = jnp.float32


def at_z(step):
    return "dp", lambda d: d // 4 * 4 + (d + step) % 4


def at_y(step):
    return "dp", lambda d: d // 16 * 16 + (d // 4 + step) % 4 * 4 + d % 4


def flip(bits):
    return "dp", lambda d: d ^ bits


def across_both(member):
    return member ^ (16 * 4 + 2)


core = ("feat", lambda f: f ^ 1)
chip = ("feat", lambda f: f ^ 2)


def stage(sends, after=()):
    held = lax.optimization_barrier(tuple(values for values, _ in sends) + tuple(after))
    received = []
    for values, (_, (axis, place)) in zip(held, sends):
        count = 128 if isinstance(axis, tuple) else lax.axis_size(axis)
        received.append(lax.ppermute(values, axis, [(d, place(d)) for d in range(count)]))
    return received


def together(sends):
    return list(lax.optimization_barrier(tuple(stage(sends))))


def share(values, groups=None):
    count = len(groups[0]) if groups else lax.axis_size("dp")
    pieces = jnp.broadcast_to(values[None], (count,) + values.shape)
    return lax.all_to_all(pieces, "dp", 0, 0, tiled=True, axis_index_groups=groups)


def combine(means, products, rows):
    mean = jnp.mean(means, axis=0)
    shift = means - mean
    shifts = jnp.stack((shift[:, 0] ** 2, shift[:, 1] ** 2, shift[:, 0] * shift[:, 1]), axis=1)
    return mean, jnp.sum(products + rows * shifts, axis=0)


def normalise_kernel(view_b, view_c, stats, out):
    width = view_b.shape[1]
    for index, view in enumerate((view_b, view_c)):
        mean = stats[2 * index : 2 * index + 1, :]
        inverse = stats[2 * index + 1 : 2 * index + 2, :]
        values = (view[...].astype(full) - mean) * inverse
        out[:, index * width : (index + 1) * width] = values.astype(low)


def normalise(view_b, view_c, stats):
    rows, width = view_b.shape
    return pl.pallas_call(
        normalise_kernel,
        grid=(rows // 256,),
        in_specs=[
            pl.BlockSpec((256, width), lambda i: (i, 0)),
            pl.BlockSpec((256, width), lambda i: (i, 0)),
            pl.BlockSpec((8, width), lambda i: (0, 0)),
        ],
        out_specs=pl.BlockSpec((256, 2 * width), lambda i: (i, 0)),
        out_shape=jax.ShapeDtypeStruct((rows, 2 * width), low),
        compiler_params=pltpu.CompilerParams(vmem_limit_bytes=32 * 2**20),
    )(view_b, view_c, stats)


def add_kernel(*refs):
    for index in range(4):
        refs[8 + index][...] = (
            refs[index][...].astype(full) + refs[4 + index][...].astype(full)
        ).astype(low)


def add_halves(blocks, received):
    rows, columns = received[0].shape
    halves = [pl.BlockSpec((rows, 512), lambda i, h=h: (h, i)) for h in (0, 1, 0, 1)]
    return pl.pallas_call(
        add_kernel,
        grid=(columns // 512,),
        in_specs=halves + [pl.BlockSpec((rows, 512), lambda i: (0, i))] * 4,
        out_specs=halves,
        out_shape=[jax.ShapeDtypeStruct(block.shape, low) for block in blocks],
        input_output_aliases={index: index for index in range(4)},
        compiler_params=pltpu.CompilerParams(vmem_limit_bytes=32 * 2**20),
    )(*blocks, *received)


small_cost = pl.CostEstimate(flops=1, bytes_accessed=1, transcendentals=0)
params = pltpu.CompilerParams(vmem_limit_bytes=48 * 2**20)
over_columns = (((1,), (1,)), ((), ()))


def whole(*shape):
    return pl.BlockSpec(shape, lambda *_: (0,) * len(shape))


def slope_kernel(place, total, received, diagonal, out, *, pairs):
    corr = (total[:, 0] + received[...].astype(full)) / pairs
    shape = corr.shape
    own = place[0]
    row = lax.broadcasted_iota(jnp.int32, shape, 1)
    on_diagonal = (lax.broadcasted_iota(jnp.int32, shape, 2) == own + row) & (
        lax.broadcasted_iota(jnp.int32, shape, 0) == 0
    )
    lane = lax.broadcasted_iota(jnp.int32, diagonal.shape, 1)
    rest = 1.0 - diagonal[...]
    rest = jnp.where((lane >= own) & (lane < own + 32), rest * rest, 0.0)
    loss = jnp.sum(jnp.where(on_diagonal, 0.0, off_weight * corr * corr)) + jnp.sum(rest)
    loss = jnp.full((1, 1, 128), loss)
    high = loss.astype(low).astype(full)
    middle = (loss - high).astype(low).astype(full)
    slots = jnp.zeros(shape, full)
    for index, part in enumerate((high, middle, loss - high - middle)):
        slots = jnp.where(row == index, jnp.max(part), slots)
    out[...] = jnp.where(on_diagonal, slots, 2.0 * off_weight * corr).astype(low)


def slope_tiles(place, halves, received, diagonal, pairs):
    shape = received.shape
    block = (2, 1) + shape[1:]
    return pl.pallas_call(
        functools.partial(slope_kernel, pairs=pairs),
        grid_spec=pltpu.PrefetchScalarGridSpec(
            num_scalar_prefetch=1,
            grid=(1,),
            in_specs=[
                pl.BlockSpec(block, lambda i, p: (0, p[1], 0, 0)),
                whole(*shape),
                whole(1, diagonal.shape[1]),
            ],
            out_specs=whole(*shape),
        ),
        out_shape=jax.ShapeDtypeStruct(shape, low),
        compiler_params=params,
    )(place, halves, received, diagonal)


def product_kernel(left, right, out):
    out[...] = jnp.dot(left[...], right[...], preferred_element_type=full).astype(out.dtype)


def times(left, right, kind):
    rows, depth = left.shape
    columns = right.shape[1]
    return pl.pallas_call(
        product_kernel,
        grid=(rows // 256,),
        in_specs=[pl.BlockSpec((256, depth), lambda i: (i, 0)), whole(depth, columns)],
        out_specs=pl.BlockSpec((256, columns), lambda i: (i, 0)),
        out_shape=jax.ShapeDtypeStruct((rows, columns), kind),
        compiler_params=params,
        cost_estimate=small_cost,
    )(left, right)


def upstream(even, odd, slope_even, slope_odd):
    up = lax.dot_general(even[...], slope_even[...], over_columns, preferred_element_type=full)
    return up + lax.dot_general(odd[...], slope_odd[...], over_columns, preferred_element_type=full)


def part_kernel(even, odd, slope_even, slope_odd, out):
    out[...] = upstream(even, odd, slope_even, slope_odd)


def grad_kernel(even, odd, slope_even, slope_odd, part, view, stats, out):
    up = part[...] + upstream(even, odd, slope_even, slope_odd)
    inverse = stats[1:2]
    norm = (view[...].astype(full) - stats[0:1]) * inverse
    out[...] = (inverse * (up - stats[3:4] - norm * stats[2:3])).astype(low)


def up_a_call(half, low_even, low_odd, slope_even, slope_odd, *more):
    rows = low_even.shape[0]
    width = slope_even.shape[0]
    left = pl.BlockSpec((256, width), lambda i: (i, half))
    tile = pl.BlockSpec((256, width), lambda i: (i, 0))
    square = whole(width, width)
    return pl.pallas_call(
        grad_kernel if more else part_kernel,
        grid=(rows // 256,),
        in_specs=[left, left, square, square] + ([tile, tile, whole(8, width)] if more else []),
        out_specs=tile,
        out_shape=jax.ShapeDtypeStruct((rows, width), low if more else full),
        compiler_params=params,
        cost_estimate=small_cost,
    )(low_even, low_odd, slope_even, slope_odd, *more)


def grad_b_kernel(left, slope, near, across, view, stats, out):
    up = jnp.dot(left[...], slope[...], preferred_element_type=full)
    up = up + near[...].astype(full) + across[...].astype(full)
    inverse = stats[1:2]
    norm = (view[...].astype(full) - stats[0:1]) * inverse
    out[...] = (inverse * (up - stats[3:4] - norm * stats[2:3])).astype(low)


def grad_b_call(left, slope, near, across, view, stats):
    rows, width = view.shape
    tile = pl.BlockSpec((256, width), lambda i: (i, 0))
    return pl.pallas_call(
        grad_b_kernel,
        grid=(rows // 256,),
        in_specs=[tile, whole(*slope.shape)] + [tile] * 3 + [whole(8, width)],
        out_specs=tile,
        out_shape=jax.ShapeDtypeStruct((rows, width), low),
        compiler_params=params,
        cost_estimate=small_cost,
    )(left, slope, near, across, view, stats)


def split_kernel(places, *refs):
    step = pl.program_id(0)
    for index in range(2):
        own, first, second = refs[3 * index : 3 * index + 3]
        total = own[...] + first[...].astype(full) + second[...].astype(full)
        for place in range(4):
            out = refs[6 + 4 * index + place]

            @pl.when(step == place)
            def _(out=out, total=total):
                out[...] = total.astype(out.dtype)


def split_sums(places, even, odd):
    rows, columns = even[0].shape
    size = rows // 4

    def block(index):
        return pl.BlockSpec((size, columns), lambda k, p: ((p[index] + k) & 3, 0))

    kinds = [full, low, low, low] * 2
    return pl.pallas_call(
        split_kernel,
        grid_spec=pltpu.PrefetchScalarGridSpec(
            num_scalar_prefetch=1,
            grid=(4,),
            in_specs=[block(0)] * 3 + [block(1)] * 3,
            out_specs=[whole(size, columns)] * 8,
        ),
        out_shape=[jax.ShapeDtypeStruct((size, columns), kind) for kind in kinds],
        compiler_params=params,
    )(places, *even, *odd)


def terms_kernel(slope, weights, means, diagonal_slope, columns, rows, *fixed):
    step = pl.program_id(0)

    @pl.when(step == 0)
    def _():
        columns[...] = jnp.zeros_like(columns)

    values = slope[...]
    if fixed:
        shape = values.shape
        on_diagonal = lax.broadcasted_iota(
            jnp.int32, shape, 1
        ) == step * 256 + lax.broadcasted_iota(jnp.int32, shape, 0)
        wide = values.astype(full)
        columns[2:3] += jnp.sum(jnp.where(on_diagonal, wide, 0.0), axis=0, keepdims=True)
        off = jnp.where(on_diagonal, 0.0, wide)
        values = jnp.where(on_diagonal, diagonal_slope[0:1], wide).astype(low)
        fixed[0][...] = values
    else:
        off = values.astype(full)
    squares = off * off * (0.5 / off_weight)
    columns[0:1] += jnp.sum(squares, axis=0, keepdims=True)
    columns[1:2] += jnp.dot(weights[...], values, preferred_element_type=full)[0:1]
    high = squares.astype(low)
    rest = (squares - high.astype(full)).astype(low)
    ones = jnp.ones((8, values.shape[1]), low)
    rows[0:1] = (
        lax.dot_general(ones, high, over_columns, preferred_element_type=full)
        + lax.dot_general(ones, rest, over_columns, preferred_element_type=full)
    )[0:1]
    rows[1:2] = lax.dot_general(means[...], values, over_columns, preferred_element_type=full)[0:1]
    rows[2:8] = jnp.zeros((6, 256), full)


def slope_terms(slope, weights, means, diagonal_slope=None):
    width = slope.shape[0]
    fix = diagonal_slope is not None
    tile = pl.BlockSpec((256, width), lambda i: (i, 0))
    outs = [jax.ShapeDtypeStruct((8, width), full)] * 2
    return pl.pallas_call(
        terms_kernel,
        grid=(4,),
        in_specs=[
            tile,
            pl.BlockSpec((16, 256), lambda i: (0, i)),
            whole(16, width),
            whole(8, width),
        ],
        out_specs=[whole(8, width), pl.BlockSpec((8, 256), lambda i: (0, i))] + [tile] * fix,
        out_shape=outs + [jax.ShapeDtypeStruct(slope.shape, low)] * fix,
        input_output_aliases={0: 2} if fix else {},
        compiler_params=params,
        cost_estimate=small_cost,
    )(slope, weights, means, diagonal_slope if fix else jnp.zeros((8, width), full))


def assemble_kernel(position, *refs):
    step = pl.program_id(0)
    out = refs[-1]
    halves = len(refs) == 6
    half = out.shape[0] // 2
    for index in range(4):

        @pl.when(step == index)
        def _(index=index):
            if halves and index == 1:
                out[:half] = refs[1][...]
                out[half:] = refs[2][...]
            else:
                out[...] = refs[index + halves * (index > 1)][...]


def add(one, other):
    return one.astype(full) + other.astype(full)


def pick(stack, index, axis):
    return lax.dynamic_index_in_dim(stack, index, axis, keepdims=False)


def put(stack, part, start):
    return lax.dynamic_update_slice_in_dim(stack, part, start, 0)


def around(block, place):
    return [(block, place(step)) for step in (2, 1, 3)]


def assemble(block, others, position):
    rows, columns = block.shape
    return pl.pallas_call(
        assemble_kernel,
        grid_spec=pltpu.PrefetchScalarGridSpec(
            num_scalar_prefetch=1,
            grid=(4,),
            in_specs=[whole(*part.shape) for part in (block, *others)],
            out_specs=pl.BlockSpec(
                (rows, columns),
                lambda k, p: ((p[0] - (k == 1) * 2 - (k == 2) * 1 - (k == 3) * 3) & 3, 0),
            ),
        ),
        out_shape=jax.ShapeDtypeStruct((4 * rows, columns), block.dtype),
        compiler_params=pltpu.CompilerParams(vmem_limit_bytes=32 * 2**20),
    )(position.astype(jnp.int32).reshape(1), block, *others)


def on_device(view_a, view_b):
    dp_count = lax.axis_size("dp")
    rows, width = view_a.shape
    pairs = rows * dp_count
    dp_index = lax.axis_index("dp")
    xi, yi, zi = dp_index >> 4, (dp_index >> 2) & 3, dp_index & 3
    view_c = stage([(view_b, chip)])[0]
    first = view_a.astype(full)
    second = view_b.astype(full)
    means = jnp.stack((jnp.mean(first, axis=0), jnp.mean(second, axis=0)))
    rest_a, rest_b = first - means[0], second - means[1]
    products = jnp.stack(
        (
            jnp.sum(rest_a * rest_a, axis=0),
            jnp.sum(rest_b * rest_b, axis=0),
            jnp.sum(rest_a * rest_b, axis=0),
        )
    )
    half_groups = [[16 * x + i for i in range(16)] for x in range(2)]
    shared = share(jnp.concatenate((means, products)).reshape(-1, 128), half_groups)
    shared = shared.reshape(16, 5, width)
    mean, products = combine(shared[:, :2], shared[:, 2:], rows)
    parts = jnp.concatenate((mean, products))
    part_b = jnp.stack((mean[1], products[1]))
    parts, part_b, view_c = lax.optimization_barrier((parts, part_b, view_c))
    other, part_c, part_d = stage(
        [(parts, flip(16)), (part_b, chip), (part_b, (("dp", "feat"), across_both))]
    )
    both = jnp.stack((parts, other))
    mean, products = combine(both[:, :2], both[:, 2:], pairs // 2)
    inverse = lax.rsqrt(products[:2] / pairs + epsilon)
    inv_a, inv_b = inverse
    diagonal = products[2] / pairs * inv_a * inv_b
    mean_c = 0.5 * (part_c[0] + part_d[0])
    products_c = part_c[1] + part_d[1] + (pairs // 4) * (part_c[0] - part_d[0]) ** 2
    inv_c = lax.rsqrt(products_c / pairs + epsilon)
    stats = jnp.concatenate(
        (jnp.stack((mean[1], inv_b, mean_c, inv_c)), jnp.zeros((4, width), full))
    )
    norm_a = (first - mean[0]) * inv_a
    low_a = norm_a.astype(low)

    low_even = normalise(view_b, view_c, stats)
    low_odd = stage([(low_even, core)])[0]
    ways = ((low_even, at_z, zi), (low_odd, at_y, yi))

    def product(right, start, size):
        columns = lax.dynamic_slice_in_dim(low_a, start, size, 1)
        return lax.dot_general(
            columns, right, (((0,), (0,)), ((), ())), preferred_element_type=full
        )

    sends = []
    for right, place, position in ways:
        start = ((position + 2) & 3) * 256
        sends.append((product(right, start, 128).astype(low), place(1)))
        sends.append((product(right, start + 128, 128).astype(low), place(3)))
    nears = [
        product(right, ((position + step) & 3) * 256, 256).astype(low)
        for right, _, position in ways
        for step in (1, 3)
    ]
    got = together(sends)
    nears = add_halves(nears, got)
    sends = [
        (near, place(step))
        for near, (place, step) in zip(nears, ((at_z, 1), (at_z, 3), (at_y, 1), (at_y, 3)))
    ]
    local = jnp.concatenate(
        (
            jnp.sum(low_a.astype(full), axis=0),
            jnp.sum(low_even.astype(full), axis=0),
            jnp.sum(low_odd.astype(full), axis=0),
        )
    )
    local = share(local.reshape(-1, 128))
    owns = [product(right, position * 256, 256) for right, _, position in ways]
    local, owns, got = lax.optimization_barrier((local, owns, tuple(stage(sends))))
    low_means = jnp.sum(local, axis=0).reshape(5, width) / pairs

    others = ((at_y, yi), (at_z, zi))
    blocks = split_sums(
        jnp.stack((yi, zi)).astype(jnp.int32), (owns[0], *got[:2]), (owns[1], *got[2:])
    )
    got = together(
        [
            (blocks[4 * index + step], place(step))
            for step in (2, 1, 3)
            for index, (place, _) in enumerate(others)
        ]
    )
    halves = jnp.stack(
        [
            sum((other.astype(full) for other in got[index::2]), blocks[4 * index])
            for index in range(2)
        ]
    ).reshape(2, 2, 32, 2 * width)
    got = stage([(pick(halves, 1 - xi, 1).astype(low), flip(16))])[0]
    own = zi * 256 + yi * 64 + xi * 32
    place = jnp.stack((own, xi)).astype(jnp.int32)
    tiles = slope_tiles(place, halves, got, diagonal[None], pairs)

    got = stage([(tiles, flip(16))])[0]
    both = jnp.where(
        xi == 0,
        jnp.concatenate((tiles, got), axis=1),
        jnp.concatenate((got, tiles), axis=1),
    )
    got = together(
        [(both[index], place(step)) for step in (2, 1, 3) for index, (place, _) in enumerate(others)]
    )
    blocks = [
        assemble(both[index], got[index::2], position) for index, (_, position) in enumerate(others)
    ]

    diagonal_slope = (-2.0 * (1.0 - diagonal)).astype(low).astype(full)
    wide_slope = jnp.broadcast_to(diagonal_slope, (8, width))
    weights, *means = (jnp.broadcast_to(mean, (16, width)).astype(low) for mean in low_means)
    near_even, near_odd = blocks[0][:, width:], blocks[1][:, width:]
    got = together(around(near_even, at_z) + around(near_odd, at_y))
    slope_d = assemble(near_odd, got[3:], yi)
    slope_c = assemble(near_even, got[:3], zi)
    product_d = stage([(times(low_a, slope_d, low), core)])[0]
    across = add(times(low_a, slope_c, full), product_d).astype(low)
    near_even, near_odd = blocks[0][:, :width], blocks[1][:, :width]
    across, near_even, near_odd = lax.optimization_barrier((across, near_even, near_odd))
    across = stage([(across, chip)])[0]
    columns_c, rows_c = slope_terms(slope_c, weights, means[1])
    columns_d, rows_d = slope_terms(slope_d, weights, means[3])
    part_a = up_a_call(1, low_even, low_odd, slope_c, slope_d)
    got = stage(
        [(near_even, at_z(1)), (near_even, at_z(3)), (near_odd, at_y(1)), (near_odd, at_y(3))]
    )
    got, (columns_c, rows_c, columns_d, rows_d) = lax.optimization_barrier(
        (got, (columns_c, rows_c, columns_d, rows_d))
    )
    half = near_even.shape[0] // 2
    sends = [
        (got[0][:half], at_z(1)),
        (got[1][half:], at_z(3)),
        (got[2][:half], at_y(1)),
        (got[3][half:], at_y(3)),
    ]
    far, part_a = lax.optimization_barrier((tuple(stage(sends)), part_a))
    slope_e = assemble(near_odd, [*far[2:], *got[2:]], yi)
    slope_b = assemble(near_even, [*far[:2], *got[:2]], zi)
    near = times(low_a, slope_e, low)
    columns_b, rows_b, slope_b = slope_terms(slope_b, weights, means[0], wide_slope)
    columns_e, rows_e = slope_terms(slope_e, weights, means[2])
    loss = jnp.sum(columns_b[2].reshape(32, 32)[:, :3])
    loss_row = jnp.full((1, width), loss)
    small = jnp.concatenate((columns_e[:2], columns_d[:2], loss_row))
    across, near, small = lax.optimization_barrier((across, near, small))
    near, small = stage([(near, core), (small, core)])
    distant = stage([(jnp.concatenate((columns_c[:2] + small[2:4], loss_row + small[4:5])), chip)])[0]
    loss = loss + small[4, 0] + distant[2, 0]
    zeros = jnp.zeros((4, width), full)
    diagonal_term = diagonal_slope * diagonal
    rows_a = rows_b[:2] + rows_c[:2] + rows_d[:2] + rows_e[:2]
    rows_a = jnp.concatenate(((rows_a[0] + diagonal_term)[None], rows_a[1:2]))
    stats_a = jnp.concatenate((mean[0:1], inv_a[None], rows_a, zeros))
    grad_a = up_a_call(0, low_even, low_odd, slope_b, slope_e, part_a, view_a, stats_a)
    columns = columns_b[:2] + small[0:2] + distant[0:2]
    columns = jnp.concatenate(((columns[0] + diagonal_term)[None], columns[1:2]))
    stats_b = jnp.concatenate((mean[1:2], inv_b[None], columns, zeros))
    grad_b = grad_b_call(low_a, slope_b, near, across, view_b, stats_b)
    return (loss, grad_a, grad_b)


def solution(mesh):
    in_specs = (P("dp", "feat"), P("dp", "feat"))
    out_specs = (P(), P("dp", "feat"), P("dp", "feat"))
    return jax.shard_map(
        on_device, mesh=mesh, in_specs=in_specs, out_specs=out_specs, check_vma=False
    )
```

```python
import functools

import jax
import jax.numpy as jnp
from jax import lax
from jax.experimental import pallas as pl
from jax.experimental.pallas import tpu as pltpu
from jax.sharding import PartitionSpec as P

epsilon = 1e-05
off_weight = 0.0051
low = jnp.bfloat16
full = jnp.float32


def at_z(step):
    return "dp", lambda d: d // 4 * 4 + (d + step) % 4


def at_y(step):
    return "dp", lambda d: d // 16 * 16 + (d // 4 + step) % 4 * 4 + d % 4


def flip(bits):
    return "dp", lambda d: d ^ bits


def across_both(member):
    return member ^ (16 * 4 + 2)


core = ("feat", lambda f: f ^ 1)
chip = ("feat", lambda f: f ^ 2)


def stage(sends, after=()):
    held = lax.optimization_barrier(tuple(values for values, _ in sends) + tuple(after))
    received = []
    for values, (_, (axis, place)) in zip(held, sends):
        count = 128 if isinstance(axis, tuple) else lax.axis_size(axis)
        received.append(lax.ppermute(values, axis, [(d, place(d)) for d in range(count)]))
    return received


def together(sends):
    return list(lax.optimization_barrier(tuple(stage(sends))))


def share(values, groups=None):
    count = len(groups[0]) if groups else lax.axis_size("dp")
    pieces = jnp.broadcast_to(values[None], (count,) + values.shape)
    return lax.all_to_all(pieces, "dp", 0, 0, tiled=True, axis_index_groups=groups)


def combine(means, products, rows):
    mean = jnp.mean(means, axis=0)
    shift = means - mean
    shifts = jnp.stack((shift[:, 0] ** 2, shift[:, 1] ** 2, shift[:, 0] * shift[:, 1]), axis=1)
    return mean, jnp.sum(products + rows * shifts, axis=0)


def normalise_kernel(view_b, view_c, stats, out):
    width = view_b.shape[1]
    for index, view in enumerate((view_b, view_c)):
        mean = stats[2 * index : 2 * index + 1, :]
        inverse = stats[2 * index + 1 : 2 * index + 2, :]
        values = (view[...].astype(full) - mean) * inverse
        out[:, index * width : (index + 1) * width] = values.astype(low)


def normalise(view_b, view_c, stats):
    rows, width = view_b.shape
    return pl.pallas_call(
        normalise_kernel,
        grid=(rows // 256,),
        in_specs=[
            pl.BlockSpec((256, width), lambda i: (i, 0)),
            pl.BlockSpec((256, width), lambda i: (i, 0)),
            pl.BlockSpec((8, width), lambda i: (0, 0)),
        ],
        out_specs=pl.BlockSpec((256, 2 * width), lambda i: (i, 0)),
        out_shape=jax.ShapeDtypeStruct((rows, 2 * width), low),
        compiler_params=pltpu.CompilerParams(vmem_limit_bytes=32 * 2**20),
    )(view_b, view_c, stats)


def add_kernel(*refs):
    for index in range(4):
        refs[8 + index][...] = (
            refs[index][...].astype(full) + refs[4 + index][...].astype(full)
        ).astype(low)


def add_halves(blocks, received):
    rows, columns = received[0].shape
    halves = [pl.BlockSpec((rows, 512), lambda i, h=h: (h, i)) for h in (0, 1, 0, 1)]
    return pl.pallas_call(
        add_kernel,
        grid=(columns // 512,),
        in_specs=halves + [pl.BlockSpec((rows, 512), lambda i: (0, i))] * 4,
        out_specs=halves,
        out_shape=[jax.ShapeDtypeStruct(block.shape, low) for block in blocks],
        input_output_aliases={index: index for index in range(4)},
        compiler_params=pltpu.CompilerParams(vmem_limit_bytes=32 * 2**20),
    )(*blocks, *received)


small_cost = pl.CostEstimate(flops=1, bytes_accessed=1, transcendentals=0)
params = pltpu.CompilerParams(vmem_limit_bytes=48 * 2**20)
over_columns = (((1,), (1,)), ((), ()))


def whole(*shape):
    return pl.BlockSpec(shape, lambda *_: (0,) * len(shape))


def slope_kernel(place, total, received, diagonal, out, *, pairs):
    corr = add(total[...], received[...]) / pairs
    shape = corr.shape
    own = place[0]
    row = lax.broadcasted_iota(jnp.int32, shape, 1)
    on_diagonal = (lax.broadcasted_iota(jnp.int32, shape, 2) == own + row) & (
        lax.broadcasted_iota(jnp.int32, shape, 0) == 0
    )
    lane = lax.broadcasted_iota(jnp.int32, diagonal.shape, 1)
    rest = 1.0 - diagonal[...]
    rest = jnp.where((lane >= own) & (lane < own + shape[1]), rest * rest, 0.0)
    loss = jnp.sum(jnp.where(on_diagonal, 0.0, off_weight * corr * corr)) + jnp.sum(rest)
    loss = jnp.full((1, 1, 128), loss)
    high = loss.astype(low).astype(full)
    middle = (loss - high).astype(low).astype(full)
    slots = jnp.zeros(shape, full)
    for index, part in enumerate((high, middle, loss - high - middle)):
        slots = jnp.where(row == index, jnp.max(part), slots)
    out[...] = jnp.where(on_diagonal, slots, 2.0 * off_weight * corr).astype(low)


def slope_tiles(place, total, received, diagonal, pairs):
    shape = received.shape
    return pl.pallas_call(
        functools.partial(slope_kernel, pairs=pairs),
        grid_spec=pltpu.PrefetchScalarGridSpec(
            num_scalar_prefetch=1,
            grid=(1,),
            in_specs=[whole(*shape), whole(*shape), whole(1, diagonal.shape[1])],
            out_specs=whole(*shape),
        ),
        out_shape=jax.ShapeDtypeStruct(shape, low),
        compiler_params=params,
    )(place, total, received, diagonal)


def far_kernel(position, left, right, top, bottom):
    columns = left[:, pl.ds(pl.multiple_of(position[0] * 256, 256), 256)]
    part = lax.dot_general(
        columns, right[...], (((0,), (0,)), ((), ())), preferred_element_type=full
    ).astype(low)
    top[...] = part[:128]
    bottom[...] = part[128:]


def far_chunk(position, left, right):
    rows, width = left.shape
    columns = right.shape[1]
    return pl.pallas_call(
        far_kernel,
        grid_spec=pltpu.PrefetchScalarGridSpec(
            num_scalar_prefetch=1,
            grid=(columns // 512,),
            in_specs=[whole(rows, width), pl.BlockSpec((rows, 512), lambda i, p: (0, i))],
            out_specs=[pl.BlockSpec((128, 512), lambda i, p: (0, i))] * 2,
        ),
        out_shape=[jax.ShapeDtypeStruct((128, columns), low)] * 2,
        compiler_params=params,
    )(position.astype(jnp.int32).reshape(1), left, right)


def product_kernel(left, right, out):
    out[...] = jnp.dot(left[...], right[...], preferred_element_type=full).astype(out.dtype)


def times(left, right, kind):
    rows, depth = left.shape
    columns = right.shape[1]
    return pl.pallas_call(
        product_kernel,
        grid=(rows // 256,),
        in_specs=[pl.BlockSpec((256, depth), lambda i: (i, 0)), whole(depth, columns)],
        out_specs=pl.BlockSpec((256, columns), lambda i: (i, 0)),
        out_shape=jax.ShapeDtypeStruct((rows, columns), kind),
        compiler_params=params,
        cost_estimate=small_cost,
    )(left, right)


def upstream(even, odd, slope_even, slope_odd):
    up = lax.dot_general(even[...], slope_even[...], over_columns, preferred_element_type=full)
    return up + lax.dot_general(odd[...], slope_odd[...], over_columns, preferred_element_type=full)


def part_kernel(even, odd, slope_even, slope_odd, out):
    out[...] = upstream(even, odd, slope_even, slope_odd)


def grad_kernel(even, odd, slope_even, slope_odd, part, view, stats, out):
    up = part[...] + upstream(even, odd, slope_even, slope_odd)
    inverse = stats[1:2]
    norm = (view[...].astype(full) - stats[0:1]) * inverse
    out[...] = (inverse * (up - stats[3:4] - norm * stats[2:3])).astype(low)


def up_a_call(half, low_even, low_odd, slope_even, slope_odd, *more):
    rows = low_even.shape[0]
    width = slope_even.shape[0]
    left = pl.BlockSpec((256, width), lambda i: (i, half))
    tile = pl.BlockSpec((256, width), lambda i: (i, 0))
    square = whole(width, width)
    return pl.pallas_call(
        grad_kernel if more else part_kernel,
        grid=(rows // 256,),
        in_specs=[left, left, square, square] + ([tile, tile, whole(8, width)] if more else []),
        out_specs=tile,
        out_shape=jax.ShapeDtypeStruct((rows, width), low if more else full),
        compiler_params=params,
        cost_estimate=small_cost,
    )(low_even, low_odd, slope_even, slope_odd, *more)


def grad_b_kernel(left, slope, near, across, view, stats, out):
    up = jnp.dot(left[...], slope[...], preferred_element_type=full)
    up = up + near[...].astype(full) + across[...].astype(full)
    inverse = stats[1:2]
    norm = (view[...].astype(full) - stats[0:1]) * inverse
    out[...] = (inverse * (up - stats[3:4] - norm * stats[2:3])).astype(low)


def grad_b_call(left, slope, near, across, view, stats):
    rows, width = view.shape
    tile = pl.BlockSpec((256, width), lambda i: (i, 0))
    return pl.pallas_call(
        grad_b_kernel,
        grid=(rows // 256,),
        in_specs=[tile, whole(*slope.shape)] + [tile] * 3 + [whole(8, width)],
        out_specs=tile,
        out_shape=jax.ShapeDtypeStruct((rows, width), low),
        compiler_params=params,
        cost_estimate=small_cost,
    )(left, slope, near, across, view, stats)


def split_kernel(places, *refs):
    step = pl.program_id(0)
    for index in range(2):
        own, first, second = refs[3 * index : 3 * index + 3]
        total = own[...] + first[...].astype(full) + second[...].astype(full)
        for place in range(4):
            out = refs[6 + 4 * index + place]

            @pl.when(step == place)
            def _(out=out, total=total):
                out[...] = total.astype(out.dtype)


def split_sums(places, even, odd):
    rows, columns = even[0].shape
    size = rows // 4

    def block(index):
        return pl.BlockSpec((size, columns), lambda k, p: ((p[index] + k) & 3, 0))

    kinds = [full, low, low, low] * 2
    return pl.pallas_call(
        split_kernel,
        grid_spec=pltpu.PrefetchScalarGridSpec(
            num_scalar_prefetch=1,
            grid=(4,),
            in_specs=[block(0)] * 3 + [block(1)] * 3,
            out_specs=[whole(size, columns)] * 8,
        ),
        out_shape=[jax.ShapeDtypeStruct((size, columns), kind) for kind in kinds],
        compiler_params=params,
    )(places, *even, *odd)


def terms_kernel(slope, weights, means, diagonal_slope, columns, rows, *fixed):
    step = pl.program_id(0)

    @pl.when(step == 0)
    def _():
        columns[...] = jnp.zeros_like(columns)

    values = slope[...]
    if fixed:
        shape = values.shape
        on_diagonal = lax.broadcasted_iota(
            jnp.int32, shape, 1
        ) == step * 256 + lax.broadcasted_iota(jnp.int32, shape, 0)
        wide = values.astype(full)
        columns[2:3] += jnp.sum(jnp.where(on_diagonal, wide, 0.0), axis=0, keepdims=True)
        off = jnp.where(on_diagonal, 0.0, wide)
        values = jnp.where(on_diagonal, diagonal_slope[0:1], wide).astype(low)
        fixed[0][...] = values
    else:
        off = values.astype(full)
    squares = off * off * (0.5 / off_weight)
    columns[0:1] += jnp.sum(squares, axis=0, keepdims=True)
    columns[1:2] += jnp.dot(weights[...], values, preferred_element_type=full)[0:1]
    high = squares.astype(low)
    rest = (squares - high.astype(full)).astype(low)
    ones = jnp.ones((8, values.shape[1]), low)
    rows[0:1] = (
        lax.dot_general(ones, high, over_columns, preferred_element_type=full)
        + lax.dot_general(ones, rest, over_columns, preferred_element_type=full)
    )[0:1]
    rows[1:2] = lax.dot_general(means[...], values, over_columns, preferred_element_type=full)[0:1]
    rows[2:8] = jnp.zeros((6, 256), full)


def slope_terms(slope, weights, means, diagonal_slope=None):
    width = slope.shape[0]
    fix = diagonal_slope is not None
    tile = pl.BlockSpec((256, width), lambda i: (i, 0))
    outs = [jax.ShapeDtypeStruct((8, width), full)] * 2
    return pl.pallas_call(
        terms_kernel,
        grid=(4,),
        in_specs=[
            tile,
            pl.BlockSpec((16, 256), lambda i: (0, i)),
            whole(16, width),
            whole(8, width),
        ],
        out_specs=[whole(8, width), pl.BlockSpec((8, 256), lambda i: (0, i))] + [tile] * fix,
        out_shape=outs + [jax.ShapeDtypeStruct(slope.shape, low)] * fix,
        input_output_aliases={0: 2} if fix else {},
        compiler_params=params,
        cost_estimate=small_cost,
    )(slope, weights, means, diagonal_slope if fix else jnp.zeros((8, width), full))


def assemble_kernel(position, *refs):
    step = pl.program_id(0)
    out = refs[-1]
    halves = len(refs) == 6
    half = out.shape[0] // 2
    for index in range(4):

        @pl.when(step == index)
        def _(index=index):
            if halves and index == 1:
                out[:half] = refs[1][...]
                out[half:] = refs[2][...]
            else:
                out[...] = refs[index + halves * (index > 1)][...]


def add(one, other):
    return one.astype(full) + other.astype(full)


def pick(stack, index, axis):
    return lax.dynamic_index_in_dim(stack, index, axis, keepdims=False)


def put(stack, part, start):
    return lax.dynamic_update_slice_in_dim(stack, part, start, 0)


def around(block, place):
    return [(block, place(step)) for step in (2, 1, 3)]


def assemble(block, others, position):
    rows, columns = block.shape
    return pl.pallas_call(
        assemble_kernel,
        grid_spec=pltpu.PrefetchScalarGridSpec(
            num_scalar_prefetch=1,
            grid=(4,),
            in_specs=[whole(*part.shape) for part in (block, *others)],
            out_specs=pl.BlockSpec(
                (rows, columns),
                lambda k, p: ((p[0] - (k == 1) * 2 - (k == 2) * 1 - (k == 3) * 3) & 3, 0),
            ),
        ),
        out_shape=jax.ShapeDtypeStruct((4 * rows, columns), block.dtype),
        compiler_params=pltpu.CompilerParams(vmem_limit_bytes=32 * 2**20),
    )(position.astype(jnp.int32).reshape(1), block, *others)


def on_device(view_a, view_b):
    dp_count = lax.axis_size("dp")
    rows, width = view_a.shape
    pairs = rows * dp_count
    dp_index = lax.axis_index("dp")
    xi, yi, zi = dp_index >> 4, (dp_index >> 2) & 3, dp_index & 3
    view_c = stage([(view_b, chip)])[0]
    first = view_a.astype(full)
    second = view_b.astype(full)
    means = jnp.stack((jnp.mean(first, axis=0), jnp.mean(second, axis=0)))
    rest_a, rest_b = first - means[0], second - means[1]
    products = jnp.stack(
        (
            jnp.sum(rest_a * rest_a, axis=0),
            jnp.sum(rest_b * rest_b, axis=0),
            jnp.sum(rest_a * rest_b, axis=0),
        )
    )
    half_groups = [[16 * x + i for i in range(16)] for x in range(2)]
    shared = share(jnp.concatenate((means, products)).reshape(-1, 128), half_groups)
    shared = shared.reshape(16, 5, width)
    mean, products = combine(shared[:, :2], shared[:, 2:], rows)
    parts = jnp.concatenate((mean, products))
    part_b = jnp.stack((mean[1], products[1]))
    parts, part_b, view_c = lax.optimization_barrier((parts, part_b, view_c))
    other, part_c, part_d = stage(
        [(parts, flip(16)), (part_b, chip), (part_b, (("dp", "feat"), across_both))]
    )
    both = jnp.stack((parts, other))
    mean, products = combine(both[:, :2], both[:, 2:], pairs // 2)
    inverse = lax.rsqrt(products[:2] / pairs + epsilon)
    inv_a, inv_b = inverse
    diagonal = products[2] / pairs * inv_a * inv_b
    mean_c = 0.5 * (part_c[0] + part_d[0])
    products_c = part_c[1] + part_d[1] + (pairs // 4) * (part_c[0] - part_d[0]) ** 2
    inv_c = lax.rsqrt(products_c / pairs + epsilon)
    stats = jnp.concatenate(
        (jnp.stack((mean[1], inv_b, mean_c, inv_c)), jnp.zeros((4, width), full))
    )
    norm_a = (first - mean[0]) * inv_a
    low_a = norm_a.astype(low)

    low_even = normalise(view_b, view_c, stats)
    low_odd = stage([(low_even, core)])[0]
    ways = ((low_even, at_z, zi), (low_odd, at_y, yi))

    def product(right, start, size):
        columns = lax.dynamic_slice_in_dim(low_a, start, size, 1)
        return lax.dot_general(
            columns, right, (((0,), (0,)), ((), ())), preferred_element_type=full
        )

    sends = []
    for right, place, position in ways:
        top, bottom = far_chunk((position + 2) & 3, low_a, right)
        sends.extend(((top, place(1)), (bottom, place(3))))
    nears = [
        product(right, ((position + step) & 3) * 256, 256).astype(low)
        for right, _, position in ways
        for step in (1, 3)
    ]
    got = together(sends)
    nears = add_halves(nears, got)
    sends = [
        (near, place(step))
        for near, (place, step) in zip(nears, ((at_z, 1), (at_z, 3), (at_y, 1), (at_y, 3)))
    ]
    local = jnp.concatenate(
        (
            jnp.sum(low_a.astype(full), axis=0),
            jnp.sum(low_even.astype(full), axis=0),
            jnp.sum(low_odd.astype(full), axis=0),
        )
    )
    local = share(local.reshape(-1, 128))
    owns = [product(right, position * 256, 256) for right, _, position in ways]
    local, owns, got = lax.optimization_barrier((local, owns, tuple(stage(sends))))
    low_means = jnp.sum(local, axis=0).reshape(5, width) / pairs

    others = ((at_y, yi), (at_z, zi))
    blocks = split_sums(
        jnp.stack((yi, zi)).astype(jnp.int32), (owns[0], *got[:2]), (owns[1], *got[2:])
    )
    got = together(
        [
            (blocks[4 * index + step], place(step))
            for step in (2, 1, 3)
            for index, (place, _) in enumerate(others)
        ]
    )
    totals = jnp.stack(
        [
            sum((other.astype(full) for other in got[index::2]), blocks[4 * index]).astype(low)
            for index in range(2)
        ]
    )
    got = stage([(totals, flip(16))])[0]
    place = (zi * 256 + yi * 64).astype(jnp.int32).reshape(1)
    both = slope_tiles(place, totals, got, diagonal[None], pairs)
    got = together(
        [(both[index], place(step)) for step in (2, 1, 3) for index, (place, _) in enumerate(others)]
    )
    blocks = [
        assemble(both[index], got[index::2], position) for index, (_, position) in enumerate(others)
    ]

    diagonal_slope = (-2.0 * (1.0 - diagonal)).astype(low).astype(full)
    wide_slope = jnp.broadcast_to(diagonal_slope, (8, width))
    weights, *means = (jnp.broadcast_to(mean, (16, width)).astype(low) for mean in low_means)
    near_even, near_odd = blocks[0][:, width:], blocks[1][:, width:]
    got = together(around(near_even, at_z) + around(near_odd, at_y))
    slope_d = assemble(near_odd, got[3:], yi)
    slope_c = assemble(near_even, got[:3], zi)
    product_d = stage([(times(low_a, slope_d, low), core)])[0]
    across = add(times(low_a, slope_c, full), product_d).astype(low)
    near_even, near_odd = blocks[0][:, :width], blocks[1][:, :width]
    across, near_even, near_odd = lax.optimization_barrier((across, near_even, near_odd))
    across = stage([(across, chip)])[0]
    columns_c, rows_c = slope_terms(slope_c, weights, means[1])
    columns_d, rows_d = slope_terms(slope_d, weights, means[3])
    part_a = up_a_call(1, low_even, low_odd, slope_c, slope_d)
    got = stage(
        [(near_even, at_z(1)), (near_even, at_z(3)), (near_odd, at_y(1)), (near_odd, at_y(3))]
    )
    got, (columns_c, rows_c, columns_d, rows_d) = lax.optimization_barrier(
        (got, (columns_c, rows_c, columns_d, rows_d))
    )
    half = near_even.shape[0] // 2
    sends = [
        (got[0][:half], at_z(1)),
        (got[1][half:], at_z(3)),
        (got[2][:half], at_y(1)),
        (got[3][half:], at_y(3)),
    ]
    far, part_a = lax.optimization_barrier((tuple(stage(sends)), part_a))
    slope_e = assemble(near_odd, [*far[2:], *got[2:]], yi)
    slope_b = assemble(near_even, [*far[:2], *got[:2]], zi)
    near = times(low_a, slope_e, low)
    columns_b, rows_b, slope_b = slope_terms(slope_b, weights, means[0], wide_slope)
    columns_e, rows_e = slope_terms(slope_e, weights, means[2])
    loss = jnp.sum(columns_b[2].reshape(16, 64)[:, :3])
    loss_row = jnp.full((1, width), loss)
    small = jnp.concatenate((columns_e[:2], columns_d[:2], loss_row))
    across, near, small = lax.optimization_barrier((across, near, small))
    diagonal_term = diagonal_slope * diagonal
    near, small = stage([(near, core), (small, core)])
    distant = stage([(jnp.concatenate((columns_c[:2] + small[2:4], loss_row + small[4:5])), chip)])[0]
    rows_a = rows_b[:2] + rows_c[:2] + rows_d[:2] + rows_e[:2]
    rows_a = jnp.concatenate(((rows_a[0] + diagonal_term)[None], rows_a[1:2]))
    stats_a = jnp.concatenate((mean[0:1], inv_a[None], rows_a, jnp.zeros((4, width), full)))
    grad_a = up_a_call(0, low_even, low_odd, slope_b, slope_e, part_a, view_a, stats_a)
    grad_a, distant = lax.optimization_barrier((grad_a, distant))
    loss = loss + small[4, 0] + distant[2, 0]
    zeros = jnp.zeros((4, width), full)
    columns = columns_b[:2] + small[0:2] + distant[0:2]
    columns = jnp.concatenate(((columns[0] + diagonal_term)[None], columns[1:2]))
    stats_b = jnp.concatenate((mean[1:2], inv_b[None], columns, zeros))
    grad_b = grad_b_call(low_a, slope_b, near, across, view_b, stats_b)
    return (loss, grad_a, grad_b)


def solution(mesh):
    in_specs = (P("dp", "feat"), P("dp", "feat"))
    out_specs = (P(), P("dp", "feat"), P("dp", "feat"))
    return jax.shard_map(
        on_device, mesh=mesh, in_specs=in_specs, out_specs=out_specs, check_vma=False
    )
```

```python
import functools

import jax
import jax.numpy as jnp
from jax import lax
from jax.experimental import pallas as pl
from jax.experimental.pallas import tpu as pltpu
from jax.sharding import PartitionSpec as P

epsilon = 1e-05
off_weight = 0.0051
low = jnp.bfloat16
full = jnp.float32


def at_z(step):
    return "dp", lambda d: d // 4 * 4 + (d + step) % 4


def at_y(step):
    return "dp", lambda d: d // 16 * 16 + (d // 4 + step) % 4 * 4 + d % 4


def flip(bits):
    return "dp", lambda d: d ^ bits


def across_both(member):
    return member ^ (16 * 4 + 2)


core = ("feat", lambda f: f ^ 1)
chip = ("feat", lambda f: f ^ 2)


def stage(sends, after=()):
    held = lax.optimization_barrier(tuple(values for values, _ in sends) + tuple(after))
    received = []
    for values, (_, (axis, place)) in zip(held, sends):
        count = 128 if isinstance(axis, tuple) else lax.axis_size(axis)
        received.append(lax.ppermute(values, axis, [(d, place(d)) for d in range(count)]))
    return received


def together(sends):
    return list(lax.optimization_barrier(tuple(stage(sends))))


def share(values, groups=None):
    count = len(groups[0]) if groups else lax.axis_size("dp")
    pieces = jnp.broadcast_to(values[None], (count,) + values.shape)
    return lax.all_to_all(pieces, "dp", 0, 0, tiled=True, axis_index_groups=groups)


def combine(means, products, rows):
    mean = jnp.mean(means, axis=0)
    shift = means - mean
    shifts = jnp.stack((shift[:, 0] ** 2, shift[:, 1] ** 2, shift[:, 0] * shift[:, 1]), axis=1)
    return mean, jnp.sum(products + rows * shifts, axis=0)


def normalise_kernel(view_b, view_c, stats, out):
    width = view_b.shape[1]
    for index, view in enumerate((view_b, view_c)):
        mean = stats[2 * index : 2 * index + 1, :]
        inverse = stats[2 * index + 1 : 2 * index + 2, :]
        values = (view[...].astype(full) - mean) * inverse
        out[:, index * width : (index + 1) * width] = values.astype(low)


def normalise(view_b, view_c, stats):
    rows, width = view_b.shape
    return pl.pallas_call(
        normalise_kernel,
        grid=(rows // 256,),
        in_specs=[
            pl.BlockSpec((256, width), lambda i: (i, 0)),
            pl.BlockSpec((256, width), lambda i: (i, 0)),
            pl.BlockSpec((8, width), lambda i: (0, 0)),
        ],
        out_specs=pl.BlockSpec((256, 2 * width), lambda i: (i, 0)),
        out_shape=jax.ShapeDtypeStruct((rows, 2 * width), low),
        compiler_params=pltpu.CompilerParams(vmem_limit_bytes=32 * 2**20),
    )(view_b, view_c, stats)


def add_kernel(*refs):
    for index in range(4):
        refs[8 + index][...] = (
            refs[index][...].astype(full) + refs[4 + index][...].astype(full)
        ).astype(low)


def add_halves(blocks, received):
    rows, columns = received[0].shape
    halves = [pl.BlockSpec((rows, 512), lambda i, h=h: (h, i)) for h in (0, 1, 0, 1)]
    return pl.pallas_call(
        add_kernel,
        grid=(columns // 512,),
        in_specs=halves + [pl.BlockSpec((rows, 512), lambda i: (0, i))] * 4,
        out_specs=halves,
        out_shape=[jax.ShapeDtypeStruct(block.shape, low) for block in blocks],
        input_output_aliases={index: index for index in range(4)},
        compiler_params=pltpu.CompilerParams(vmem_limit_bytes=32 * 2**20),
    )(*blocks, *received)


small_cost = pl.CostEstimate(flops=1, bytes_accessed=1, transcendentals=0)
params = pltpu.CompilerParams(vmem_limit_bytes=48 * 2**20)
over_columns = (((1,), (1,)), ((), ()))


def whole(*shape):
    return pl.BlockSpec(shape, lambda *_: (0,) * len(shape))


def slope_kernel(place, total, received, diagonal, out, *, pairs):
    corr = add(total[...], received[...]) / pairs
    shape = corr.shape
    own = place[0]
    row = lax.broadcasted_iota(jnp.int32, shape, 1)
    on_diagonal = (lax.broadcasted_iota(jnp.int32, shape, 2) == own + row) & (
        lax.broadcasted_iota(jnp.int32, shape, 0) == 0
    )
    lane = lax.broadcasted_iota(jnp.int32, diagonal.shape, 1)
    rest = 1.0 - diagonal[...]
    rest = jnp.where((lane >= own) & (lane < own + shape[1]), rest * rest, 0.0)
    loss = jnp.sum(jnp.where(on_diagonal, 0.0, off_weight * corr * corr)) + jnp.sum(rest)
    loss = jnp.full((1, 1, 128), loss)
    high = loss.astype(low).astype(full)
    middle = (loss - high).astype(low).astype(full)
    slots = jnp.zeros(shape, full)
    for index, part in enumerate((high, middle, loss - high - middle)):
        slots = jnp.where(row == index, jnp.max(part), slots)
    out[...] = jnp.where(on_diagonal, slots, 2.0 * off_weight * corr).astype(low)


def slope_tiles(place, total, received, diagonal, pairs):
    shape = received.shape
    return pl.pallas_call(
        functools.partial(slope_kernel, pairs=pairs),
        grid_spec=pltpu.PrefetchScalarGridSpec(
            num_scalar_prefetch=1,
            grid=(1,),
            in_specs=[whole(*shape), whole(*shape), whole(1, diagonal.shape[1])],
            out_specs=whole(*shape),
        ),
        out_shape=jax.ShapeDtypeStruct(shape, low),
        compiler_params=params,
    )(place, total, received, diagonal)


def far_kernel(position, left, right, top, bottom):
    columns = left[:, pl.ds(pl.multiple_of(position[0] * 256, 256), 256)]
    part = lax.dot_general(
        columns, right[...], (((0,), (0,)), ((), ())), preferred_element_type=full
    ).astype(low)
    top[...] = part[:128]
    bottom[...] = part[128:]


def near_kernel(position, left, right, above, below):
    for step, out in ((1, above), (3, below)):
        start = pl.multiple_of(((position[0] + step) & 3) * 256, 256)
        out[...] = lax.dot_general(
            left[:, pl.ds(start, 256)],
            right[...],
            (((0,), (0,)), ((), ())),
            preferred_element_type=full,
        ).astype(low)


def near_chunks(position, left, right):
    rows, width = left.shape
    columns = right.shape[1]
    return pl.pallas_call(
        near_kernel,
        grid_spec=pltpu.PrefetchScalarGridSpec(
            num_scalar_prefetch=1,
            grid=(columns // 512,),
            in_specs=[whole(rows, width), pl.BlockSpec((rows, 512), lambda i, p: (0, i))],
            out_specs=[pl.BlockSpec((256, 512), lambda i, p: (0, i))] * 2,
        ),
        out_shape=[jax.ShapeDtypeStruct((256, columns), low)] * 2,
        compiler_params=params,
    )(position.astype(jnp.int32).reshape(1), left, right)


def far_chunk(position, left, right):
    rows, width = left.shape
    columns = right.shape[1]
    return pl.pallas_call(
        far_kernel,
        grid_spec=pltpu.PrefetchScalarGridSpec(
            num_scalar_prefetch=1,
            grid=(columns // 512,),
            in_specs=[whole(rows, width), pl.BlockSpec((rows, 512), lambda i, p: (0, i))],
            out_specs=[pl.BlockSpec((128, 512), lambda i, p: (0, i))] * 2,
        ),
        out_shape=[jax.ShapeDtypeStruct((128, columns), low)] * 2,
        compiler_params=params,
    )(position.astype(jnp.int32).reshape(1), left, right)


def product_kernel(left, right, out):
    out[...] = jnp.dot(left[...], right[...], preferred_element_type=full).astype(out.dtype)


def times(left, right, kind):
    rows, depth = left.shape
    columns = right.shape[1]
    return pl.pallas_call(
        product_kernel,
        grid=(rows // 256,),
        in_specs=[pl.BlockSpec((256, depth), lambda i: (i, 0)), whole(depth, columns)],
        out_specs=pl.BlockSpec((256, columns), lambda i: (i, 0)),
        out_shape=jax.ShapeDtypeStruct((rows, columns), kind),
        compiler_params=params,
        cost_estimate=small_cost,
    )(left, right)


def upstream(even, odd, slope_even, slope_odd):
    up = lax.dot_general(even[...], slope_even[...], over_columns, preferred_element_type=full)
    return up + lax.dot_general(odd[...], slope_odd[...], over_columns, preferred_element_type=full)


def part_kernel(even, odd, slope_even, slope_odd, out):
    out[...] = upstream(even, odd, slope_even, slope_odd)


def grad_kernel(even, odd, slope_even, slope_odd, part, view, stats, out):
    up = part[...] + upstream(even, odd, slope_even, slope_odd)
    inverse = stats[1:2]
    norm = (view[...].astype(full) - stats[0:1]) * inverse
    out[...] = (inverse * (up - stats[3:4] - norm * stats[2:3])).astype(low)


def up_a_call(half, low_even, low_odd, slope_even, slope_odd, *more):
    rows = low_even.shape[0]
    width = slope_even.shape[0]
    left = pl.BlockSpec((rows, width), lambda i: (0, half))
    right = pl.BlockSpec((256, width), lambda i: (i, 0))
    tile = pl.BlockSpec((rows, 256), lambda i: (0, i))
    line = pl.BlockSpec((8, 256), lambda i: (0, i))
    return pl.pallas_call(
        grad_kernel if more else part_kernel,
        grid=(width // 256,),
        in_specs=[left, left, right, right] + ([tile, tile, line] if more else []),
        out_specs=tile,
        out_shape=jax.ShapeDtypeStruct((rows, width), low if more else full),
        compiler_params=params,
        cost_estimate=small_cost,
    )(low_even, low_odd, slope_even, slope_odd, *more)


def halves_kernel(*refs):
    for index in range(4):
        refs[4 + index][...] = refs[index][...]


def halves(blocks):
    rows, columns = blocks[0].shape
    return pl.pallas_call(
        halves_kernel,
        grid=(2,),
        in_specs=[
            pl.BlockSpec((rows // 2, columns // 2), lambda i, h=h: (h, i)) for h in (0, 1, 0, 1)
        ],
        out_specs=[pl.BlockSpec((rows // 2, columns // 2), lambda i: (0, i))] * 4,
        out_shape=[jax.ShapeDtypeStruct((rows // 2, columns), low)] * 4,
        compiler_params=params,
    )(*blocks)


def grad_b_kernel(left, slope, near, across, view, stats, out):
    up = jnp.dot(left[...], slope[...], preferred_element_type=full)
    up = up + near[...].astype(full) + across[...].astype(full)
    inverse = stats[1:2]
    norm = (view[...].astype(full) - stats[0:1]) * inverse
    out[...] = (inverse * (up - stats[3:4] - norm * stats[2:3])).astype(low)


def grad_b_call(left, slope, near, across, view, stats):
    rows, width = view.shape
    tile = pl.BlockSpec((256, width), lambda i: (i, 0))
    return pl.pallas_call(
        grad_b_kernel,
        grid=(rows // 256,),
        in_specs=[tile, whole(*slope.shape)] + [tile] * 3 + [whole(8, width)],
        out_specs=tile,
        out_shape=jax.ShapeDtypeStruct((rows, width), low),
        compiler_params=params,
        cost_estimate=small_cost,
    )(left, slope, near, across, view, stats)


def split_kernel(places, *refs):
    step = pl.program_id(0)
    for index in range(2):
        own, first, second = refs[3 * index : 3 * index + 3]
        total = own[...] + first[...].astype(full) + second[...].astype(full)
        for place in range(4):
            out = refs[6 + 4 * index + place]

            @pl.when(step == place)
            def _(out=out, total=total):
                out[...] = total.astype(out.dtype)


def split_sums(places, even, odd):
    rows, columns = even[0].shape
    size = rows // 4

    def block(index):
        return pl.BlockSpec((size, columns), lambda k, p: ((p[index] + k) & 3, 0))

    kinds = [full, low, low, low] * 2
    return pl.pallas_call(
        split_kernel,
        grid_spec=pltpu.PrefetchScalarGridSpec(
            num_scalar_prefetch=1,
            grid=(4,),
            in_specs=[block(0)] * 3 + [block(1)] * 3,
            out_specs=[whole(size, columns)] * 8,
        ),
        out_shape=[jax.ShapeDtypeStruct((size, columns), kind) for kind in kinds],
        compiler_params=params,
    )(places, *even, *odd)


def terms_kernel(slope, weights, means, diagonal_slope, columns, rows, *fixed):
    step = pl.program_id(0)

    @pl.when(step == 0)
    def _():
        columns[...] = jnp.zeros_like(columns)

    values = slope[...]
    if fixed:
        shape = values.shape
        on_diagonal = lax.broadcasted_iota(
            jnp.int32, shape, 1
        ) == step * 256 + lax.broadcasted_iota(jnp.int32, shape, 0)
        wide = values.astype(full)
        columns[2:3] += jnp.sum(jnp.where(on_diagonal, wide, 0.0), axis=0, keepdims=True)
        off = jnp.where(on_diagonal, 0.0, wide)
        values = jnp.where(on_diagonal, diagonal_slope[0:1], wide).astype(low)
        fixed[0][...] = values
    else:
        off = values.astype(full)
    squares = off * off * (0.5 / off_weight)
    columns[0:1] += jnp.sum(squares, axis=0, keepdims=True)
    columns[1:2] += jnp.dot(weights[...], values, preferred_element_type=full)[0:1]
    high = squares.astype(low)
    rest = (squares - high.astype(full)).astype(low)
    ones = jnp.ones((8, values.shape[1]), low)
    rows[0:1] = (
        lax.dot_general(ones, high, over_columns, preferred_element_type=full)
        + lax.dot_general(ones, rest, over_columns, preferred_element_type=full)
    )[0:1]
    rows[1:2] = lax.dot_general(means[...], values, over_columns, preferred_element_type=full)[0:1]
    rows[2:8] = jnp.zeros((6, 256), full)


def slope_terms(slope, weights, means, diagonal_slope=None):
    width = slope.shape[0]
    fix = diagonal_slope is not None
    tile = pl.BlockSpec((256, width), lambda i: (i, 0))
    outs = [jax.ShapeDtypeStruct((8, width), full)] * 2
    return pl.pallas_call(
        terms_kernel,
        grid=(4,),
        in_specs=[
            tile,
            pl.BlockSpec((16, 256), lambda i: (0, i)),
            whole(16, width),
            whole(8, width),
        ],
        out_specs=[whole(8, width), pl.BlockSpec((8, 256), lambda i: (0, i))] + [tile] * fix,
        out_shape=outs + [jax.ShapeDtypeStruct(slope.shape, low)] * fix,
        input_output_aliases={0: 2} if fix else {},
        compiler_params=params,
        cost_estimate=small_cost,
    )(slope, weights, means, diagonal_slope if fix else jnp.zeros((8, width), full))


def assemble_kernel(position, *refs):
    step = pl.program_id(0)
    out = refs[-1]
    halves = len(refs) == 6
    half = out.shape[0] // 2
    for index in range(4):

        @pl.when(step == index)
        def _(index=index):
            if halves and index == 1:
                out[:half] = refs[1][...]
                out[half:] = refs[2][...]
            else:
                out[...] = refs[index + halves * (index > 1)][...]


def add(one, other):
    return one.astype(full) + other.astype(full)


def pick(stack, index, axis):
    return lax.dynamic_index_in_dim(stack, index, axis, keepdims=False)


def put(stack, part, start):
    return lax.dynamic_update_slice_in_dim(stack, part, start, 0)


def around(block, place):
    return [(block, place(step)) for step in (2, 1, 3)]


def assemble(block, others, position):
    rows, columns = block.shape
    return pl.pallas_call(
        assemble_kernel,
        grid_spec=pltpu.PrefetchScalarGridSpec(
            num_scalar_prefetch=1,
            grid=(4,),
            in_specs=[whole(*part.shape) for part in (block, *others)],
            out_specs=pl.BlockSpec(
                (rows, columns),
                lambda k, p: ((p[0] - (k == 1) * 2 - (k == 2) * 1 - (k == 3) * 3) & 3, 0),
            ),
        ),
        out_shape=jax.ShapeDtypeStruct((4 * rows, columns), block.dtype),
        compiler_params=pltpu.CompilerParams(vmem_limit_bytes=32 * 2**20),
    )(position.astype(jnp.int32).reshape(1), block, *others)


def on_device(view_a, view_b):
    dp_count = lax.axis_size("dp")
    rows, width = view_a.shape
    pairs = rows * dp_count
    dp_index = lax.axis_index("dp")
    xi, yi, zi = dp_index >> 4, (dp_index >> 2) & 3, dp_index & 3
    view_c = stage([(view_b, chip)])[0]
    first = view_a.astype(full)
    second = view_b.astype(full)
    means = jnp.stack((jnp.mean(first, axis=0), jnp.mean(second, axis=0)))
    rest_a, rest_b = first - means[0], second - means[1]
    products = jnp.stack(
        (
            jnp.sum(rest_a * rest_a, axis=0),
            jnp.sum(rest_b * rest_b, axis=0),
            jnp.sum(rest_a * rest_b, axis=0),
        )
    )
    half_groups = [[16 * x + i for i in range(16)] for x in range(2)]
    shared = share(jnp.concatenate((means, products)).reshape(-1, 128), half_groups)
    shared = shared.reshape(16, 5, width)
    mean, products = combine(shared[:, :2], shared[:, 2:], rows)
    parts = jnp.concatenate((mean, products))
    part_b = jnp.stack((mean[1], products[1]))
    view_d = stage([(view_b, core)])[0]
    parts, part_b, view_c, view_d = lax.optimization_barrier((parts, part_b, view_c, view_d))
    other, part_c, part_d, view_e = together(
        [
            (parts, flip(16)),
            (part_b, chip),
            (part_b, (("dp", "feat"), across_both)),
            (view_c, core),
        ]
    )
    both = jnp.stack((parts, other))
    mean, products = combine(both[:, :2], both[:, 2:], pairs // 2)
    inverse = lax.rsqrt(products[:2] / pairs + epsilon)
    inv_a, inv_b = inverse
    diagonal = products[2] / pairs * inv_a * inv_b
    mean_c = 0.5 * (part_c[0] + part_d[0])
    products_c = part_c[1] + part_d[1] + (pairs // 4) * (part_c[0] - part_d[0]) ** 2
    inv_c = lax.rsqrt(products_c / pairs + epsilon)
    stats = jnp.concatenate(
        (jnp.stack((mean[1], inv_b, mean_c, inv_c)), jnp.zeros((4, width), full))
    )
    norm_a = (first - mean[0]) * inv_a
    low_a = norm_a.astype(low)

    low_even = normalise(view_b, view_c, stats)
    low_odd = normalise(view_d, view_e, stage([(stats, core)])[0])
    ways = ((low_even, at_z, zi), (low_odd, at_y, yi))

    def product(right, start, size):
        columns = lax.dynamic_slice_in_dim(low_a, start, size, 1)
        return lax.dot_general(
            columns, right, (((0,), (0,)), ((), ())), preferred_element_type=full
        )

    sends = []
    for right, place, position in ways:
        top, bottom = far_chunk((position + 2) & 3, low_a, right)
        sends.extend(((top, place(1)), (bottom, place(3))))
    nears = [
        near for right, _, position in ways for near in near_chunks(position, low_a, right)
    ]
    got = together(sends)
    nears = add_halves(nears, got)
    sends = [
        (near, place(step))
        for near, (place, step) in zip(nears, ((at_z, 1), (at_z, 3), (at_y, 1), (at_y, 3)))
    ]
    local = jnp.concatenate(
        (
            jnp.sum(low_a.astype(full), axis=0),
            jnp.sum(low_even.astype(full), axis=0),
            jnp.sum(low_odd.astype(full), axis=0),
        )
    )
    local = share(local.reshape(-1, 128), half_groups)
    owns = [product(right, position * 256, 256) for right, _, position in ways]
    local, owns, got = lax.optimization_barrier((local, owns, tuple(stage(sends))))
    local = jnp.sum(local, axis=0)

    others = ((at_y, yi), (at_z, zi))
    blocks = split_sums(
        jnp.stack((yi, zi)).astype(jnp.int32), (owns[0], *got[:2]), (owns[1], *got[2:])
    )
    got = together(
        [
            (blocks[4 * index + step], place(step))
            for step in (2, 1, 3)
            for index, (place, _) in enumerate(others)
        ]
    )
    totals = jnp.stack(
        [
            sum((other.astype(full) for other in got[index::2]), blocks[4 * index]).astype(low)
            for index in range(2)
        ]
    )
    got, other_local = together([(totals, flip(16)), (local, flip(16))])
    low_means = (local + other_local).reshape(5, width) / pairs
    place = (zi * 256 + yi * 64).astype(jnp.int32).reshape(1)
    both = slope_tiles(place, totals, got, diagonal[None], pairs)
    got = together(
        [(both[index], place(step)) for step in (2, 1, 3) for index, (place, _) in enumerate(others)]
    )
    blocks = [
        assemble(both[index], got[index::2], position) for index, (_, position) in enumerate(others)
    ]

    diagonal_slope = (-2.0 * (1.0 - diagonal)).astype(low).astype(full)
    wide_slope = jnp.broadcast_to(diagonal_slope, (8, width))
    weights, *means = (jnp.broadcast_to(mean, (16, width)).astype(low) for mean in low_means)
    near_even, near_odd = blocks[0][:, width:], blocks[1][:, width:]
    got = together(around(near_even, at_z) + around(near_odd, at_y))
    slope_d = assemble(near_odd, got[3:], yi)
    slope_c = assemble(near_even, got[:3], zi)
    product_d = stage([(times(low_a, slope_d, low), core)])[0]
    across = add(times(low_a, slope_c, full), product_d).astype(low)
    near_even, near_odd = blocks[0][:, :width], blocks[1][:, :width]
    across, near_even, near_odd = lax.optimization_barrier((across, near_even, near_odd))
    across = stage([(across, chip)])[0]
    columns_c, rows_c = slope_terms(slope_c, weights, means[1])
    columns_d, rows_d = slope_terms(slope_d, weights, means[3])
    part_a = up_a_call(1, low_even, low_odd, slope_c, slope_d)
    got = stage(
        [(near_even, at_z(1)), (near_even, at_z(3)), (near_odd, at_y(1)), (near_odd, at_y(3))]
    )
    got, (columns_c, rows_c, columns_d, rows_d) = lax.optimization_barrier(
        (got, (columns_c, rows_c, columns_d, rows_d))
    )
    sends = list(zip(halves(got), (at_z(1), at_z(3), at_y(1), at_y(3))))
    far, part_a = lax.optimization_barrier((tuple(stage(sends)), part_a))
    slope_e = assemble(near_odd, [*far[2:], *got[2:]], yi)
    slope_b = assemble(near_even, [*far[:2], *got[:2]], zi)
    near = times(low_a, slope_e, low)
    columns_b, rows_b, slope_b = slope_terms(slope_b, weights, means[0], wide_slope)
    columns_e, rows_e = slope_terms(slope_e, weights, means[2])
    loss = jnp.sum(columns_b[2].reshape(16, 64)[:, :3])
    loss_row = jnp.full((1, width), loss)
    small = jnp.concatenate((columns_e[:2], columns_d[:2], loss_row))
    across, near, small = lax.optimization_barrier((across, near, small))
    diagonal_term = diagonal_slope * diagonal
    near, small = stage([(near, core), (small, core)])
    distant = stage([(jnp.concatenate((columns_c[:2] + small[2:4], loss_row + small[4:5])), chip)])[0]
    rows_a = rows_b[:2] + rows_c[:2] + rows_d[:2] + rows_e[:2]
    rows_a = jnp.concatenate(((rows_a[0] + diagonal_term)[None], rows_a[1:2]))
    stats_a = jnp.concatenate((mean[0:1], inv_a[None], rows_a, jnp.zeros((4, width), full)))
    grad_a = up_a_call(0, low_even, low_odd, slope_b, slope_e, part_a, view_a, stats_a)
    grad_a, distant = lax.optimization_barrier((grad_a, distant))
    loss = loss + small[4, 0] + distant[2, 0]
    zeros = jnp.zeros((4, width), full)
    columns = columns_b[:2] + small[0:2] + distant[0:2]
    columns = jnp.concatenate(((columns[0] + diagonal_term)[None], columns[1:2]))
    stats_b = jnp.concatenate((mean[1:2], inv_b[None], columns, zeros))
    grad_b = grad_b_call(low_a, slope_b, near, across, view_b, stats_b)
    return (loss, grad_a, grad_b)


def solution(mesh):
    in_specs = (P("dp", "feat"), P("dp", "feat"))
    out_specs = (P(), P("dp", "feat"), P("dp", "feat"))
    return jax.shard_map(
        on_device, mesh=mesh, in_specs=in_specs, out_specs=out_specs, check_vma=False
    )
```

```python
import functools

import jax
import jax.numpy as jnp
from jax import lax
from jax.experimental import pallas as pl
from jax.experimental.pallas import tpu as pltpu
from jax.sharding import PartitionSpec as P

epsilon = 1e-05
off_weight = 0.0051
low = jnp.bfloat16
full = jnp.float32


def at_z(step):
    return "dp", lambda d: d // 4 * 4 + (d + step) % 4


def at_y(step):
    return "dp", lambda d: d // 16 * 16 + (d // 4 + step) % 4 * 4 + d % 4


def flip(bits):
    return "dp", lambda d: d ^ bits


def across_both(member):
    return member ^ (16 * 4 + 2)


core = ("feat", lambda f: f ^ 1)
chip = ("feat", lambda f: f ^ 2)


def stage(sends, after=()):
    held = lax.optimization_barrier(tuple(values for values, _ in sends) + tuple(after))
    received = []
    for values, (_, (axis, place)) in zip(held, sends):
        count = 128 if isinstance(axis, tuple) else lax.axis_size(axis)
        received.append(lax.ppermute(values, axis, [(d, place(d)) for d in range(count)]))
    return received


def together(sends):
    return list(lax.optimization_barrier(tuple(stage(sends))))


def share(values, groups=None):
    count = len(groups[0]) if groups else lax.axis_size("dp")
    pieces = jnp.broadcast_to(values[None], (count,) + values.shape)
    return lax.all_to_all(pieces, "dp", 0, 0, tiled=True, axis_index_groups=groups)


def combine(means, products, rows):
    mean = jnp.mean(means, axis=0)
    shift = means - mean
    shifts = jnp.stack((shift[:, 0] ** 2, shift[:, 1] ** 2, shift[:, 0] * shift[:, 1]), axis=1)
    return mean, jnp.sum(products + rows * shifts, axis=0)


def normalise_kernel(view_b, view_c, stats, out):
    width = view_b.shape[1]
    for index, view in enumerate((view_b, view_c)):
        mean = stats[2 * index : 2 * index + 1, :]
        inverse = stats[2 * index + 1 : 2 * index + 2, :]
        values = (view[...].astype(full) - mean) * inverse
        out[:, index * width : (index + 1) * width] = values.astype(low)


def normalise(view_b, view_c, stats):
    rows, width = view_b.shape
    return pl.pallas_call(
        normalise_kernel,
        grid=(rows // 256,),
        in_specs=[
            pl.BlockSpec((256, width), lambda i: (i, 0)),
            pl.BlockSpec((256, width), lambda i: (i, 0)),
            pl.BlockSpec((8, width), lambda i: (0, 0)),
        ],
        out_specs=pl.BlockSpec((256, 2 * width), lambda i: (i, 0)),
        out_shape=jax.ShapeDtypeStruct((rows, 2 * width), low),
        compiler_params=pltpu.CompilerParams(vmem_limit_bytes=32 * 2**20),
    )(view_b, view_c, stats)


def add_kernel(*refs):
    for index in range(4):
        refs[8 + index][...] = (
            refs[index][...].astype(full) + refs[4 + index][...].astype(full)
        ).astype(low)


def add_halves(blocks, received):
    rows, columns = received[0].shape
    halves = [pl.BlockSpec((rows, 512), lambda i, h=h: (h, i)) for h in (0, 1, 0, 1)]
    return pl.pallas_call(
        add_kernel,
        grid=(columns // 512,),
        in_specs=halves + [pl.BlockSpec((rows, 512), lambda i: (0, i))] * 4,
        out_specs=halves,
        out_shape=[jax.ShapeDtypeStruct(block.shape, low) for block in blocks],
        input_output_aliases={index: index for index in range(4)},
        compiler_params=pltpu.CompilerParams(vmem_limit_bytes=32 * 2**20),
    )(*blocks, *received)


small_cost = pl.CostEstimate(flops=1, bytes_accessed=1, transcendentals=0)
params = pltpu.CompilerParams(vmem_limit_bytes=48 * 2**20)
over_columns = (((1,), (1,)), ((), ()))


def whole(*shape):
    return pl.BlockSpec(shape, lambda *_: (0,) * len(shape))


def slope_kernel(place, total, received, diagonal, out, *, pairs):
    corr = add(total[...], received[...]) / pairs
    shape = corr.shape
    own = place[0]
    row = lax.broadcasted_iota(jnp.int32, shape, 1)
    on_diagonal = (lax.broadcasted_iota(jnp.int32, shape, 2) == own + row) & (
        lax.broadcasted_iota(jnp.int32, shape, 0) == 0
    )
    lane = lax.broadcasted_iota(jnp.int32, diagonal.shape, 1)
    rest = 1.0 - diagonal[...]
    rest = jnp.where((lane >= own) & (lane < own + shape[1]), rest * rest, 0.0)
    loss = jnp.sum(jnp.where(on_diagonal, 0.0, off_weight * corr * corr)) + jnp.sum(rest)
    loss = jnp.full((1, 1, 128), loss)
    high = loss.astype(low).astype(full)
    middle = (loss - high).astype(low).astype(full)
    slots = jnp.zeros(shape, full)
    for index, part in enumerate((high, middle, loss - high - middle)):
        slots = jnp.where(row == index, jnp.max(part), slots)
    out[...] = jnp.where(on_diagonal, slots, 2.0 * off_weight * corr).astype(low)


def slope_tiles(place, total, received, diagonal, pairs):
    shape = received.shape
    return pl.pallas_call(
        functools.partial(slope_kernel, pairs=pairs),
        grid_spec=pltpu.PrefetchScalarGridSpec(
            num_scalar_prefetch=1,
            grid=(1,),
            in_specs=[whole(*shape), whole(*shape), whole(1, diagonal.shape[1])],
            out_specs=whole(*shape),
        ),
        out_shape=jax.ShapeDtypeStruct(shape, low),
        compiler_params=params,
    )(place, total, received, diagonal)


def far_kernel(position, left, right, top, bottom):
    columns = left[:, pl.ds(pl.multiple_of(position[0] * 256, 256), 256)]
    part = lax.dot_general(
        columns, right[...], (((0,), (0,)), ((), ())), preferred_element_type=full
    ).astype(low)
    top[...] = part[:128]
    bottom[...] = part[128:]


def near_kernel(position, left, right, above, below):
    for step, out in ((1, above), (3, below)):
        start = pl.multiple_of(((position[0] + step) & 3) * 256, 256)
        out[...] = lax.dot_general(
            left[:, pl.ds(start, 256)],
            right[...],
            (((0,), (0,)), ((), ())),
            preferred_element_type=full,
        ).astype(low)


def near_chunks(position, left, right):
    rows, width = left.shape
    columns = right.shape[1]
    return pl.pallas_call(
        near_kernel,
        grid_spec=pltpu.PrefetchScalarGridSpec(
            num_scalar_prefetch=1,
            grid=(columns // 512,),
            in_specs=[whole(rows, width), pl.BlockSpec((rows, 512), lambda i, p: (0, i))],
            out_specs=[pl.BlockSpec((256, 512), lambda i, p: (0, i))] * 2,
        ),
        out_shape=[jax.ShapeDtypeStruct((256, columns), low)] * 2,
        compiler_params=params,
    )(position.astype(jnp.int32).reshape(1), left, right)


def far_chunk(position, left, right):
    rows, width = left.shape
    columns = right.shape[1]
    return pl.pallas_call(
        far_kernel,
        grid_spec=pltpu.PrefetchScalarGridSpec(
            num_scalar_prefetch=1,
            grid=(columns // 512,),
            in_specs=[whole(rows, width), pl.BlockSpec((rows, 512), lambda i, p: (0, i))],
            out_specs=[pl.BlockSpec((128, 512), lambda i, p: (0, i))] * 2,
        ),
        out_shape=[jax.ShapeDtypeStruct((128, columns), low)] * 2,
        compiler_params=params,
    )(position.astype(jnp.int32).reshape(1), left, right)


def product_kernel(left, right, out):
    out[...] = jnp.dot(left[...], right[...], preferred_element_type=full).astype(out.dtype)


def times(left, right, kind):
    rows, depth = left.shape
    columns = right.shape[1]
    return pl.pallas_call(
        product_kernel,
        grid=(rows // 256,),
        in_specs=[pl.BlockSpec((256, depth), lambda i: (i, 0)), whole(depth, columns)],
        out_specs=pl.BlockSpec((256, columns), lambda i: (i, 0)),
        out_shape=jax.ShapeDtypeStruct((rows, columns), kind),
        compiler_params=params,
        cost_estimate=small_cost,
    )(left, right)


def upstream(even, odd, slope_even, slope_odd):
    up = lax.dot_general(even[...], slope_even[...], over_columns, preferred_element_type=full)
    return up + lax.dot_general(odd[...], slope_odd[...], over_columns, preferred_element_type=full)


def part_kernel(even, odd, slope_even, slope_odd, out):
    out[...] = upstream(even, odd, slope_even, slope_odd)


def grad_kernel(even, odd, slope_even, slope_odd, part, view, stats, out):
    up = part[...] + upstream(even, odd, slope_even, slope_odd)
    inverse = stats[1:2]
    norm = (view[...].astype(full) - stats[0:1]) * inverse
    out[...] = (inverse * (up - stats[3:4] - norm * stats[2:3])).astype(low)


def up_a_call(half, low_even, low_odd, slope_even, slope_odd, *more):
    rows = low_even.shape[0]
    width = slope_even.shape[0]
    left = pl.BlockSpec((rows, width), lambda i: (0, half))
    right = pl.BlockSpec((256, width), lambda i: (i, 0))
    tile = pl.BlockSpec((rows, 256), lambda i: (0, i))
    line = pl.BlockSpec((8, 256), lambda i: (0, i))
    return pl.pallas_call(
        grad_kernel if more else part_kernel,
        grid=(width // 256,),
        in_specs=[left, left, right, right] + ([tile, tile, line] if more else []),
        out_specs=tile,
        out_shape=jax.ShapeDtypeStruct((rows, width), low if more else full),
        compiler_params=params,
        cost_estimate=small_cost,
    )(low_even, low_odd, slope_even, slope_odd, *more)


def halves_kernel(*refs):
    for index in range(4):
        refs[4 + index][...] = refs[index][...]


def halves(blocks):
    rows, columns = blocks[0].shape
    return pl.pallas_call(
        halves_kernel,
        grid=(2,),
        in_specs=[
            pl.BlockSpec((rows // 2, columns // 2), lambda i, h=h: (h, i)) for h in (0, 1, 0, 1)
        ],
        out_specs=[pl.BlockSpec((rows // 2, columns // 2), lambda i: (0, i))] * 4,
        out_shape=[jax.ShapeDtypeStruct((rows // 2, columns), low)] * 4,
        compiler_params=params,
    )(*blocks)


def grad_b_kernel(left, slope, near, across, view, stats, out):
    up = jnp.dot(left[...], slope[...], preferred_element_type=full)
    up = up + near[...].astype(full) + across[...].astype(full)
    inverse = stats[1:2]
    norm = (view[...].astype(full) - stats[0:1]) * inverse
    out[...] = (inverse * (up - stats[3:4] - norm * stats[2:3])).astype(low)


def grad_b_call(left, slope, near, across, view, stats):
    rows, width = view.shape
    tile = pl.BlockSpec((256, width), lambda i: (i, 0))
    return pl.pallas_call(
        grad_b_kernel,
        grid=(rows // 256,),
        in_specs=[tile, whole(*slope.shape)] + [tile] * 3 + [whole(8, width)],
        out_specs=tile,
        out_shape=jax.ShapeDtypeStruct((rows, width), low),
        compiler_params=params,
        cost_estimate=small_cost,
    )(left, slope, near, across, view, stats)


def split_kernel(places, *refs):
    step = pl.program_id(0)
    for index in range(2):
        own, first, second = refs[3 * index : 3 * index + 3]
        total = own[...] + first[...].astype(full) + second[...].astype(full)
        for place in range(4):
            out = refs[6 + 4 * index + place]

            @pl.when(step == place)
            def _(out=out, total=total):
                out[...] = total.astype(out.dtype)


def split_sums(places, even, odd):
    rows, columns = even[0].shape
    size = rows // 4

    def block(index):
        return pl.BlockSpec((size, columns), lambda k, p: ((p[index] + k) & 3, 0))

    kinds = [full, low, low, low] * 2
    return pl.pallas_call(
        split_kernel,
        grid_spec=pltpu.PrefetchScalarGridSpec(
            num_scalar_prefetch=1,
            grid=(4,),
            in_specs=[block(0)] * 3 + [block(1)] * 3,
            out_specs=[whole(size, columns)] * 8,
        ),
        out_shape=[jax.ShapeDtypeStruct((size, columns), kind) for kind in kinds],
        compiler_params=params,
    )(places, *even, *odd)


def terms_kernel(slope, weights, means, diagonal_slope, columns, rows, *fixed):
    step = pl.program_id(0)

    @pl.when(step == 0)
    def _():
        columns[...] = jnp.zeros_like(columns)

    values = slope[...]
    if fixed:
        shape = values.shape
        on_diagonal = lax.broadcasted_iota(
            jnp.int32, shape, 1
        ) == step * 256 + lax.broadcasted_iota(jnp.int32, shape, 0)
        wide = values.astype(full)
        columns[2:3] += jnp.sum(jnp.where(on_diagonal, wide, 0.0), axis=0, keepdims=True)
        off = jnp.where(on_diagonal, 0.0, wide)
        values = jnp.where(on_diagonal, diagonal_slope[0:1], wide).astype(low)
        fixed[0][...] = values
    else:
        off = values.astype(full)
    squares = off * off * (0.5 / off_weight)
    columns[0:1] += jnp.sum(squares, axis=0, keepdims=True)
    columns[1:2] += jnp.dot(weights[...], values, preferred_element_type=full)[0:1]
    high = squares.astype(low)
    rest = (squares - high.astype(full)).astype(low)
    ones = jnp.ones((8, values.shape[1]), low)
    rows[0:1] = (
        lax.dot_general(ones, high, over_columns, preferred_element_type=full)
        + lax.dot_general(ones, rest, over_columns, preferred_element_type=full)
    )[0:1]
    rows[1:2] = lax.dot_general(means[...], values, over_columns, preferred_element_type=full)[0:1]
    rows[2:8] = jnp.zeros((6, 256), full)


def slope_terms(slope, weights, means, diagonal_slope=None):
    width = slope.shape[0]
    fix = diagonal_slope is not None
    tile = pl.BlockSpec((256, width), lambda i: (i, 0))
    outs = [jax.ShapeDtypeStruct((8, width), full)] * 2
    return pl.pallas_call(
        terms_kernel,
        grid=(4,),
        in_specs=[
            tile,
            pl.BlockSpec((16, 256), lambda i: (0, i)),
            whole(16, width),
            whole(8, width),
        ],
        out_specs=[whole(8, width), pl.BlockSpec((8, 256), lambda i: (0, i))] + [tile] * fix,
        out_shape=outs + [jax.ShapeDtypeStruct(slope.shape, low)] * fix,
        input_output_aliases={0: 2} if fix else {},
        compiler_params=params,
        cost_estimate=small_cost,
    )(slope, weights, means, diagonal_slope if fix else jnp.zeros((8, width), full))


def assemble_kernel(position, *refs):
    step = pl.program_id(0)
    out = refs[-1]
    halves = len(refs) == 6
    half = out.shape[0] // 2
    for index in range(4):

        @pl.when(step == index)
        def _(index=index):
            if halves and index == 1:
                out[:half] = refs[1][...]
                out[half:] = refs[2][...]
            else:
                out[...] = refs[index + halves * (index > 1)][...]


def add(one, other):
    return one.astype(full) + other.astype(full)


def pick(stack, index, axis):
    return lax.dynamic_index_in_dim(stack, index, axis, keepdims=False)


def put(stack, part, start):
    return lax.dynamic_update_slice_in_dim(stack, part, start, 0)


def around(block, place):
    return [(block, place(step)) for step in (2, 1, 3)]


def assemble(block, others, position):
    rows, columns = block.shape
    return pl.pallas_call(
        assemble_kernel,
        grid_spec=pltpu.PrefetchScalarGridSpec(
            num_scalar_prefetch=1,
            grid=(4,),
            in_specs=[whole(*part.shape) for part in (block, *others)],
            out_specs=pl.BlockSpec(
                (rows, columns),
                lambda k, p: ((p[0] - (k == 1) * 2 - (k == 2) * 1 - (k == 3) * 3) & 3, 0),
            ),
        ),
        out_shape=jax.ShapeDtypeStruct((4 * rows, columns), block.dtype),
        compiler_params=pltpu.CompilerParams(vmem_limit_bytes=32 * 2**20),
    )(position.astype(jnp.int32).reshape(1), block, *others)


def on_device(view_a, view_b):
    dp_count = lax.axis_size("dp")
    rows, width = view_a.shape
    pairs = rows * dp_count
    dp_index = lax.axis_index("dp")
    xi, yi, zi = dp_index >> 4, (dp_index >> 2) & 3, dp_index & 3
    view_c = stage([(view_b, chip)])[0]
    first = view_a.astype(full)
    second = view_b.astype(full)
    means = jnp.stack((jnp.mean(first, axis=0), jnp.mean(second, axis=0)))
    rest_a, rest_b = first - means[0], second - means[1]
    products = jnp.stack(
        (
            jnp.sum(rest_a * rest_a, axis=0),
            jnp.sum(rest_b * rest_b, axis=0),
            jnp.sum(rest_a * rest_b, axis=0),
        )
    )
    half_groups = [[16 * x + i for i in range(16)] for x in range(2)]
    shared = share(jnp.concatenate((means, products)).reshape(-1, 128), half_groups)
    shared = shared.reshape(16, 5, width)
    mean, products = combine(shared[:, :2], shared[:, 2:], rows)
    parts = jnp.concatenate((mean, products))
    part_b = jnp.stack((mean[1], products[1]))
    view_d = stage([(view_b, core)])[0]
    parts, part_b, view_c, view_d = lax.optimization_barrier((parts, part_b, view_c, view_d))
    other, part_c, part_d, view_e = together(
        [
            (parts, flip(16)),
            (part_b, chip),
            (part_b, (("dp", "feat"), across_both)),
            (view_c, core),
        ]
    )
    both = jnp.stack((parts, other))
    mean, products = combine(both[:, :2], both[:, 2:], pairs // 2)
    inverse = lax.rsqrt(products[:2] / pairs + epsilon)
    inv_a, inv_b = inverse
    diagonal = products[2] / pairs * inv_a * inv_b
    mean_c = 0.5 * (part_c[0] + part_d[0])
    products_c = part_c[1] + part_d[1] + (pairs // 4) * (part_c[0] - part_d[0]) ** 2
    inv_c = lax.rsqrt(products_c / pairs + epsilon)
    stats = jnp.concatenate(
        (jnp.stack((mean[1], inv_b, mean_c, inv_c)), jnp.zeros((4, width), full))
    )
    norm_a = (first - mean[0]) * inv_a
    low_a = norm_a.astype(low)

    low_even = normalise(view_b, view_c, stats)
    low_odd = normalise(view_d, view_e, stage([(stats, core)])[0])
    ways = ((low_even, at_z, zi), (low_odd, at_y, yi))

    def product(right, start, size):
        columns = lax.dynamic_slice_in_dim(low_a, start, size, 1)
        return lax.dot_general(
            columns, right, (((0,), (0,)), ((), ())), preferred_element_type=full
        )

    sends = []
    for right, place, position in ways:
        top, bottom = far_chunk((position + 2) & 3, low_a, right)
        sends.extend(((top, place(1)), (bottom, place(3))))
    nears = [
        near for right, _, position in ways for near in near_chunks(position, low_a, right)
    ]
    got = together(sends)
    nears = add_halves(nears, got)
    sends = [
        (near, place(step))
        for near, (place, step) in zip(nears, ((at_z, 1), (at_z, 3), (at_y, 1), (at_y, 3)))
    ]
    local = jnp.concatenate(
        (
            jnp.sum(low_a.astype(full), axis=0),
            jnp.sum(low_even.astype(full), axis=0),
            jnp.sum(low_odd.astype(full), axis=0),
        )
    )
    local = share(local.reshape(-1, 128), half_groups)
    owns = [product(right, position * 256, 256) for right, _, position in ways]
    local, owns, got = lax.optimization_barrier((local, owns, tuple(stage(sends))))
    local = jnp.sum(local, axis=0)

    others = ((at_y, yi), (at_z, zi))
    blocks = split_sums(
        jnp.stack((yi, zi)).astype(jnp.int32), (owns[0], *got[:2]), (owns[1], *got[2:])
    )
    got = together(
        [
            (blocks[4 * index + step], place(step))
            for step in (2, 1, 3)
            for index, (place, _) in enumerate(others)
        ]
    )
    totals = jnp.stack(
        [
            sum((other.astype(full) for other in got[index::2]), blocks[4 * index]).astype(low)
            for index in range(2)
        ]
    )
    got, other_local = together([(totals, flip(16)), (local, flip(16))])
    low_means = (local + other_local).reshape(5, width) / pairs
    place = (zi * 256 + yi * 64).astype(jnp.int32).reshape(1)
    both = slope_tiles(place, totals, got, diagonal[None], pairs)
    got = together(
        [(both[index], place(step)) for step in (2, 1, 3) for index, (place, _) in enumerate(others)]
    )
    blocks = [
        assemble(both[index], got[index::2], position) for index, (_, position) in enumerate(others)
    ]

    diagonal_slope = (-2.0 * (1.0 - diagonal)).astype(low).astype(full)
    wide_slope = jnp.broadcast_to(diagonal_slope, (8, width))
    weights, *means = (jnp.broadcast_to(mean, (16, width)).astype(low) for mean in low_means)
    near_even, near_odd = blocks[0][:, width:], blocks[1][:, width:]
    got = together(around(near_even, at_z) + around(near_odd, at_y))
    slope_d = assemble(near_odd, got[3:], yi)
    slope_c = assemble(near_even, got[:3], zi)
    product_d = stage([(times(low_a, slope_d, low), core)])[0]
    across = add(times(low_a, slope_c, full), product_d).astype(low)
    near_even, near_odd = blocks[0][:, :width], blocks[1][:, :width]
    across, near_even, near_odd = lax.optimization_barrier((across, near_even, near_odd))
    across = stage([(across, chip)])[0]
    columns_c, rows_c = slope_terms(slope_c, weights, means[1])
    columns_d, rows_d = slope_terms(slope_d, weights, means[3])
    part_a = up_a_call(1, low_even, low_odd, slope_c, slope_d)
    got = stage(
        [(near_even, at_z(1)), (near_even, at_z(3)), (near_odd, at_y(1)), (near_odd, at_y(3))]
    )
    got, (columns_c, rows_c, columns_d, rows_d) = lax.optimization_barrier(
        (got, (columns_c, rows_c, columns_d, rows_d))
    )
    sends = list(zip(halves(got), (at_z(1), at_z(3), at_y(1), at_y(3))))
    far, part_a = lax.optimization_barrier((tuple(stage(sends)), part_a))
    slope_e = assemble(near_odd, [*far[2:], *got[2:]], yi)
    slope_b = assemble(near_even, [*far[:2], *got[:2]], zi)
    near = times(low_a, slope_e, low)
    columns_b, rows_b, slope_b = slope_terms(slope_b, weights, means[0], wide_slope)
    columns_e, rows_e = slope_terms(slope_e, weights, means[2])
    small = jnp.concatenate((columns_e[:2], columns_d[:2]))
    across, near, small = lax.optimization_barrier((across, near, small))
    diagonal_term = diagonal_slope * diagonal
    near, small = stage([(near, core), (small, core)])
    slots = columns_b[2:3]
    distant = stage([(jnp.concatenate((columns_c[:2] + small[2:4], slots)), chip)])[0]
    rows_a = rows_b[:2] + rows_c[:2] + rows_d[:2] + rows_e[:2]
    rows_a = jnp.concatenate(((rows_a[0] + diagonal_term)[None], rows_a[1:2]))
    stats_a = jnp.concatenate((mean[0:1], inv_a[None], rows_a, jnp.zeros((4, width), full)))
    grad_a = up_a_call(0, low_even, low_odd, slope_b, slope_e, part_a, view_a, stats_a)
    grad_a, distant = lax.optimization_barrier((grad_a, distant))
    slots = slots + distant[2:3]
    loss = jnp.sum(slots + stage([(slots, core)])[0])
    columns = columns_b[:2] + small[0:2] + distant[0:2]
    columns = jnp.concatenate(((columns[0] + diagonal_term)[None], columns[1:2]))
    stats_b = jnp.concatenate((mean[1:2], inv_b[None], columns, jnp.zeros((4, width), full)))
    grad_b = grad_b_call(low_a, slope_b, near, across, view_b, stats_b)
    return (loss, grad_a, grad_b)


def solution(mesh):
    in_specs = (P("dp", "feat"), P("dp", "feat"))
    out_specs = (P(), P("dp", "feat"), P("dp", "feat"))
    return jax.shard_map(
        on_device, mesh=mesh, in_specs=in_specs, out_specs=out_specs, check_vma=False
    )
```

```python
import functools

import jax
import jax.numpy as jnp
from jax import lax
from jax.experimental import pallas as pl
from jax.experimental.pallas import tpu as pltpu
from jax.sharding import PartitionSpec as P

epsilon = 1e-05
off_weight = 0.0051
low = jnp.bfloat16
full = jnp.float32


def at_z(step):
    return "dp", lambda d: d // 4 * 4 + (d + step) % 4


def at_y(step):
    return "dp", lambda d: d // 16 * 16 + (d // 4 + step) % 4 * 4 + d % 4


def flip(bits):
    return "dp", lambda d: d ^ bits


def across_both(member):
    return member ^ (16 * 4 + 2)


core = ("feat", lambda f: f ^ 1)
chip = ("feat", lambda f: f ^ 2)


def stage(sends, after=()):
    held = lax.optimization_barrier(tuple(values for values, _ in sends) + tuple(after))
    received = []
    for values, (_, (axis, place)) in zip(held, sends):
        count = 128 if isinstance(axis, tuple) else lax.axis_size(axis)
        received.append(lax.ppermute(values, axis, [(d, place(d)) for d in range(count)]))
    return received


def together(sends):
    return list(lax.optimization_barrier(tuple(stage(sends))))


def share(values, groups=None):
    count = len(groups[0]) if groups else lax.axis_size("dp")
    pieces = jnp.broadcast_to(values[None], (count,) + values.shape)
    return lax.all_to_all(pieces, "dp", 0, 0, tiled=True, axis_index_groups=groups)


def combine(means, products, rows):
    mean = jnp.mean(means, axis=0)
    shift = means - mean
    shifts = jnp.stack((shift[:, 0] ** 2, shift[:, 1] ** 2, shift[:, 0] * shift[:, 1]), axis=1)
    return mean, jnp.sum(products + rows * shifts, axis=0)


def normalise_kernel(view_b, view_c, stats, out):
    width = view_b.shape[1]
    for index, view in enumerate((view_b, view_c)):
        mean = stats[2 * index : 2 * index + 1, :]
        inverse = stats[2 * index + 1 : 2 * index + 2, :]
        values = (view[...].astype(full) - mean) * inverse
        out[:, index * width : (index + 1) * width] = values.astype(low)


def normalise(view_b, view_c, stats):
    rows, width = view_b.shape
    return pl.pallas_call(
        normalise_kernel,
        grid=(rows // 256,),
        in_specs=[
            pl.BlockSpec((256, width), lambda i: (i, 0)),
            pl.BlockSpec((256, width), lambda i: (i, 0)),
            pl.BlockSpec((8, width), lambda i: (0, 0)),
        ],
        out_specs=pl.BlockSpec((256, 2 * width), lambda i: (i, 0)),
        out_shape=jax.ShapeDtypeStruct((rows, 2 * width), low),
        compiler_params=pltpu.CompilerParams(vmem_limit_bytes=32 * 2**20),
    )(view_b, view_c, stats)


def add_kernel(*refs):
    for index in range(4):
        refs[8 + index][...] = (
            refs[index][...].astype(full) + refs[4 + index][...].astype(full)
        ).astype(low)


def add_halves(blocks, received):
    rows, columns = received[0].shape
    halves = [pl.BlockSpec((rows, 512), lambda i, h=h: (h, i)) for h in (0, 1, 0, 1)]
    return pl.pallas_call(
        add_kernel,
        grid=(columns // 512,),
        in_specs=halves + [pl.BlockSpec((rows, 512), lambda i: (0, i))] * 4,
        out_specs=halves,
        out_shape=[jax.ShapeDtypeStruct(block.shape, low) for block in blocks],
        input_output_aliases={index: index for index in range(4)},
        compiler_params=pltpu.CompilerParams(vmem_limit_bytes=32 * 2**20),
    )(*blocks, *received)


small_cost = pl.CostEstimate(flops=1, bytes_accessed=1, transcendentals=0)
params = pltpu.CompilerParams(vmem_limit_bytes=48 * 2**20)
large = pltpu.CompilerParams(vmem_limit_bytes=56 * 2**20)
over_columns = (((1,), (1,)), ((), ()))


def whole(*shape):
    return pl.BlockSpec(shape, lambda *_: (0,) * len(shape))


def slope_kernel(place, total, received, diagonal, out, *, pairs):
    corr = add(total[...], received[...]) / pairs
    shape = corr.shape
    own = place[0]
    row = lax.broadcasted_iota(jnp.int32, shape, 1)
    on_diagonal = (lax.broadcasted_iota(jnp.int32, shape, 2) == own + row) & (
        lax.broadcasted_iota(jnp.int32, shape, 0) == 0
    )
    lane = lax.broadcasted_iota(jnp.int32, diagonal.shape, 1)
    rest = 1.0 - diagonal[...]
    rest = jnp.where((lane >= own) & (lane < own + shape[1]), rest * rest, 0.0)
    loss = jnp.sum(jnp.where(on_diagonal, 0.0, off_weight * corr * corr)) + jnp.sum(rest)
    loss = jnp.full((1, 1, 128), loss)
    high = loss.astype(low).astype(full)
    middle = (loss - high).astype(low).astype(full)
    slots = jnp.zeros(shape, full)
    for index, part in enumerate((high, middle, loss - high - middle)):
        slots = jnp.where(row == index, jnp.max(part), slots)
    out[...] = jnp.where(on_diagonal, slots, 2.0 * off_weight * corr).astype(low)


def slope_tiles(place, total, received, diagonal, pairs):
    shape = received.shape
    return pl.pallas_call(
        functools.partial(slope_kernel, pairs=pairs),
        grid_spec=pltpu.PrefetchScalarGridSpec(
            num_scalar_prefetch=1,
            grid=(1,),
            in_specs=[whole(*shape), whole(*shape), whole(1, diagonal.shape[1])],
            out_specs=whole(*shape),
        ),
        out_shape=jax.ShapeDtypeStruct(shape, low),
        compiler_params=params,
    )(place, total, received, diagonal)


def far_kernel(position, left, right, top, bottom):
    columns = left[:, pl.ds(pl.multiple_of(position[0] * 256, 256), 256)]
    part = lax.dot_general(
        columns, right[...], (((0,), (0,)), ((), ())), preferred_element_type=full
    ).astype(low)
    top[...] = part[:128]
    bottom[...] = part[128:]


def near_kernel(position, left, right, above, below):
    for step, out in ((1, above), (3, below)):
        start = pl.multiple_of(((position[0] + step) & 3) * 256, 256)
        out[...] = lax.dot_general(
            left[:, pl.ds(start, 256)],
            right[...],
            (((0,), (0,)), ((), ())),
            preferred_element_type=full,
        ).astype(low)


def near_chunks(position, left, right):
    rows, width = left.shape
    columns = right.shape[1]
    return pl.pallas_call(
        near_kernel,
        grid_spec=pltpu.PrefetchScalarGridSpec(
            num_scalar_prefetch=1,
            grid=(columns // 512,),
            in_specs=[whole(rows, width), pl.BlockSpec((rows, 512), lambda i, p: (0, i))],
            out_specs=[pl.BlockSpec((256, 512), lambda i, p: (0, i))] * 2,
        ),
        out_shape=[jax.ShapeDtypeStruct((256, columns), low)] * 2,
        compiler_params=params,
    )(position.astype(jnp.int32).reshape(1), left, right)


def far_chunk(position, left, right):
    rows, width = left.shape
    columns = right.shape[1]
    return pl.pallas_call(
        far_kernel,
        grid_spec=pltpu.PrefetchScalarGridSpec(
            num_scalar_prefetch=1,
            grid=(columns // 512,),
            in_specs=[whole(rows, width), pl.BlockSpec((rows, 512), lambda i, p: (0, i))],
            out_specs=[pl.BlockSpec((128, 512), lambda i, p: (0, i))] * 2,
        ),
        out_shape=[jax.ShapeDtypeStruct((128, columns), low)] * 2,
        compiler_params=params,
    )(position.astype(jnp.int32).reshape(1), left, right)


def product_kernel(left, right, out):
    out[...] = jnp.dot(left[...], right[...], preferred_element_type=full).astype(out.dtype)


def times(left, right, kind):
    rows, depth = left.shape
    columns = right.shape[1]
    return pl.pallas_call(
        product_kernel,
        grid=(rows // 256,),
        in_specs=[pl.BlockSpec((256, depth), lambda i: (i, 0)), whole(depth, columns)],
        out_specs=pl.BlockSpec((256, columns), lambda i: (i, 0)),
        out_shape=jax.ShapeDtypeStruct((rows, columns), kind),
        compiler_params=params,
        cost_estimate=small_cost,
    )(left, right)


def upstream(even, odd, slope_even, slope_odd):
    up = lax.dot_general(even[...], slope_even[...], over_columns, preferred_element_type=full)
    return up + lax.dot_general(odd[...], slope_odd[...], over_columns, preferred_element_type=full)


def part_kernel(even, odd, slope_even, slope_odd, out):
    out[...] = upstream(even, odd, slope_even, slope_odd)


def grad_kernel(even, odd, slope_even, slope_odd, part, view, stats, out):
    up = part[...] + upstream(even, odd, slope_even, slope_odd)
    inverse = stats[1:2]
    norm = (view[...].astype(full) - stats[0:1]) * inverse
    out[...] = (inverse * (up - stats[3:4] - norm * stats[2:3])).astype(low)


def up_a_call(half, low_even, low_odd, slope_even, slope_odd, *more):
    rows = low_even.shape[0]
    width = slope_even.shape[0]
    left = pl.BlockSpec((rows, width), lambda i: (0, half))
    right = pl.BlockSpec((256, width), lambda i: (i, 0))
    tile = pl.BlockSpec((rows, 256), lambda i: (0, i))
    line = pl.BlockSpec((8, 256), lambda i: (0, i))
    return pl.pallas_call(
        grad_kernel if more else part_kernel,
        grid=(width // 256,),
        in_specs=[left, left, right, right] + ([tile, tile, line] if more else []),
        out_specs=tile,
        out_shape=jax.ShapeDtypeStruct((rows, width), low if more else full),
        compiler_params=large if more else params,
        cost_estimate=small_cost,
    )(low_even, low_odd, slope_even, slope_odd, *more)


def halves_kernel(*refs):
    for index in range(4):
        refs[4 + index][...] = refs[index][...]


def halves(blocks):
    rows, columns = blocks[0].shape
    return pl.pallas_call(
        halves_kernel,
        grid=(2,),
        in_specs=[
            pl.BlockSpec((rows // 2, columns // 2), lambda i, h=h: (h, i)) for h in (0, 1, 0, 1)
        ],
        out_specs=[pl.BlockSpec((rows // 2, columns // 2), lambda i: (0, i))] * 4,
        out_shape=[jax.ShapeDtypeStruct((rows // 2, columns), low)] * 4,
        compiler_params=params,
    )(*blocks)


def grad_b_kernel(left, slope, near, across, view, stats, out):
    up = jnp.dot(left[...], slope[...], preferred_element_type=full)
    up = up + near[...].astype(full) + across[...].astype(full)
    inverse = stats[1:2]
    norm = (view[...].astype(full) - stats[0:1]) * inverse
    out[...] = (inverse * (up - stats[3:4] - norm * stats[2:3])).astype(low)


def grad_b_call(left, slope, near, across, view, stats):
    rows, width = view.shape
    tile = pl.BlockSpec((256, width), lambda i: (i, 0))
    return pl.pallas_call(
        grad_b_kernel,
        grid=(rows // 256,),
        in_specs=[tile, whole(*slope.shape)] + [tile] * 3 + [whole(8, width)],
        out_specs=tile,
        out_shape=jax.ShapeDtypeStruct((rows, width), low),
        compiler_params=large,
        cost_estimate=small_cost,
    )(left, slope, near, across, view, stats)


def split_kernel(places, *refs):
    step = pl.program_id(0)
    for index in range(2):
        own, first, second = refs[3 * index : 3 * index + 3]
        total = own[...] + first[...].astype(full) + second[...].astype(full)
        for place in range(4):
            out = refs[6 + 4 * index + place]

            @pl.when(step == place)
            def _(out=out, total=total):
                out[...] = total.astype(out.dtype)


def split_sums(places, even, odd):
    rows, columns = even[0].shape
    size = rows // 4

    def block(index):
        return pl.BlockSpec((size, columns), lambda k, p: ((p[index] + k) & 3, 0))

    kinds = [full, low, low, low] * 2
    return pl.pallas_call(
        split_kernel,
        grid_spec=pltpu.PrefetchScalarGridSpec(
            num_scalar_prefetch=1,
            grid=(4,),
            in_specs=[block(0)] * 3 + [block(1)] * 3,
            out_specs=[whole(size, columns)] * 8,
        ),
        out_shape=[jax.ShapeDtypeStruct((size, columns), kind) for kind in kinds],
        compiler_params=params,
    )(places, *even, *odd)


def terms_kernel(slope, weights, means, diagonal_slope, columns, rows, *fixed):
    step = pl.program_id(0)

    @pl.when(step == 0)
    def _():
        columns[...] = jnp.zeros_like(columns)

    values = slope[...]
    if fixed:
        shape = values.shape
        on_diagonal = lax.broadcasted_iota(
            jnp.int32, shape, 1
        ) == step * 256 + lax.broadcasted_iota(jnp.int32, shape, 0)
        wide = values.astype(full)
        columns[2:3] += jnp.sum(jnp.where(on_diagonal, wide, 0.0), axis=0, keepdims=True)
        off = jnp.where(on_diagonal, 0.0, wide)
        values = jnp.where(on_diagonal, diagonal_slope[0:1], wide).astype(low)
        fixed[0][...] = values
    else:
        off = values.astype(full)
    squares = off * off * (0.5 / off_weight)
    columns[0:1] += jnp.sum(squares, axis=0, keepdims=True)
    columns[1:2] += jnp.dot(weights[...], values, preferred_element_type=full)[0:1]
    high = squares.astype(low)
    rest = (squares - high.astype(full)).astype(low)
    ones = jnp.ones((8, values.shape[1]), low)
    rows[0:1] = (
        lax.dot_general(ones, high, over_columns, preferred_element_type=full)
        + lax.dot_general(ones, rest, over_columns, preferred_element_type=full)
    )[0:1]
    rows[1:2] = lax.dot_general(means[...], values, over_columns, preferred_element_type=full)[0:1]
    rows[2:8] = jnp.zeros((6, 256), full)


def slope_terms(slope, weights, means, diagonal_slope=None):
    width = slope.shape[0]
    fix = diagonal_slope is not None
    tile = pl.BlockSpec((256, width), lambda i: (i, 0))
    outs = [jax.ShapeDtypeStruct((8, width), full)] * 2
    return pl.pallas_call(
        terms_kernel,
        grid=(4,),
        in_specs=[
            tile,
            pl.BlockSpec((16, 256), lambda i: (0, i)),
            whole(16, width),
            whole(8, width),
        ],
        out_specs=[whole(8, width), pl.BlockSpec((8, 256), lambda i: (0, i))] + [tile] * fix,
        out_shape=outs + [jax.ShapeDtypeStruct(slope.shape, low)] * fix,
        input_output_aliases={0: 2} if fix else {},
        compiler_params=params,
        cost_estimate=small_cost,
    )(slope, weights, means, diagonal_slope if fix else jnp.zeros((8, width), full))


def assemble_kernel(position, *refs):
    step = pl.program_id(0)
    out = refs[-1]
    halves = len(refs) == 6
    half = out.shape[0] // 2
    for index in range(4):

        @pl.when(step == index)
        def _(index=index):
            if halves and index == 1:
                out[:half] = refs[1][...]
                out[half:] = refs[2][...]
            else:
                out[...] = refs[index + halves * (index > 1)][...]


def add(one, other):
    return one.astype(full) + other.astype(full)


def pick(stack, index, axis):
    return lax.dynamic_index_in_dim(stack, index, axis, keepdims=False)


def put(stack, part, start):
    return lax.dynamic_update_slice_in_dim(stack, part, start, 0)


def around(block, place):
    return [(block, place(step)) for step in (2, 1, 3)]


def assemble(block, others, position):
    rows, columns = block.shape
    return pl.pallas_call(
        assemble_kernel,
        grid_spec=pltpu.PrefetchScalarGridSpec(
            num_scalar_prefetch=1,
            grid=(4,),
            in_specs=[whole(*part.shape) for part in (block, *others)],
            out_specs=pl.BlockSpec(
                (rows, columns),
                lambda k, p: ((p[0] - (k == 1) * 2 - (k == 2) * 1 - (k == 3) * 3) & 3, 0),
            ),
        ),
        out_shape=jax.ShapeDtypeStruct((4 * rows, columns), block.dtype),
        compiler_params=pltpu.CompilerParams(vmem_limit_bytes=32 * 2**20),
    )(position.astype(jnp.int32).reshape(1), block, *others)


def on_device(view_a, view_b):
    dp_count = lax.axis_size("dp")
    rows, width = view_a.shape
    pairs = rows * dp_count
    dp_index = lax.axis_index("dp")
    xi, yi, zi = dp_index >> 4, (dp_index >> 2) & 3, dp_index & 3
    view_c = stage([(view_b, chip)])[0]
    first = view_a.astype(full)
    second = view_b.astype(full)
    means = jnp.stack((jnp.mean(first, axis=0), jnp.mean(second, axis=0)))
    rest_a, rest_b = first - means[0], second - means[1]
    products = jnp.stack(
        (
            jnp.sum(rest_a * rest_a, axis=0),
            jnp.sum(rest_b * rest_b, axis=0),
            jnp.sum(rest_a * rest_b, axis=0),
        )
    )
    half_groups = [[16 * x + i for i in range(16)] for x in range(2)]
    shared = share(jnp.concatenate((means, products)).reshape(-1, 128), half_groups)
    shared = shared.reshape(16, 5, width)
    mean, products = combine(shared[:, :2], shared[:, 2:], rows)
    parts = jnp.concatenate((mean, products))
    part_b = jnp.stack((mean[1], products[1]))
    view_d = stage([(view_b, core)])[0]
    parts, part_b, view_c, view_d = lax.optimization_barrier((parts, part_b, view_c, view_d))
    other, part_c, part_d, view_e = together(
        [
            (parts, flip(16)),
            (part_b, chip),
            (part_b, (("dp", "feat"), across_both)),
            (view_c, core),
        ]
    )
    both = jnp.stack((parts, other))
    mean, products = combine(both[:, :2], both[:, 2:], pairs // 2)
    inverse = lax.rsqrt(products[:2] / pairs + epsilon)
    inv_a, inv_b = inverse
    diagonal = products[2] / pairs * inv_a * inv_b
    mean_c = 0.5 * (part_c[0] + part_d[0])
    products_c = part_c[1] + part_d[1] + (pairs // 4) * (part_c[0] - part_d[0]) ** 2
    inv_c = lax.rsqrt(products_c / pairs + epsilon)
    stats = jnp.concatenate(
        (jnp.stack((mean[1], inv_b, mean_c, inv_c)), jnp.zeros((4, width), full))
    )
    norm_a = (first - mean[0]) * inv_a
    low_a = norm_a.astype(low)

    low_even = normalise(view_b, view_c, stats)
    low_odd = normalise(view_d, view_e, stage([(stats, core)])[0])
    ways = ((low_even, at_z, zi), (low_odd, at_y, yi))

    def product(right, start, size):
        columns = lax.dynamic_slice_in_dim(low_a, start, size, 1)
        return lax.dot_general(
            columns, right, (((0,), (0,)), ((), ())), preferred_element_type=full
        )

    sends = []
    for right, place, position in ways:
        top, bottom = far_chunk((position + 2) & 3, low_a, right)
        sends.extend(((top, place(1)), (bottom, place(3))))
    nears = [
        near for right, _, position in ways for near in near_chunks(position, low_a, right)
    ]
    got = together(sends)
    nears = add_halves(nears, got)
    sends = [
        (near, place(step))
        for near, (place, step) in zip(nears, ((at_z, 1), (at_z, 3), (at_y, 1), (at_y, 3)))
    ]
    local = jnp.concatenate(
        (
            jnp.sum(low_a.astype(full), axis=0),
            jnp.sum(low_even.astype(full), axis=0),
            jnp.sum(low_odd.astype(full), axis=0),
        )
    )
    local = share(local.reshape(-1, 128), half_groups)
    owns = [product(right, position * 256, 256) for right, _, position in ways]
    local, owns, got = lax.optimization_barrier((local, owns, tuple(stage(sends))))
    local = jnp.sum(local, axis=0)

    others = ((at_y, yi), (at_z, zi))
    blocks = split_sums(
        jnp.stack((yi, zi)).astype(jnp.int32), (owns[0], *got[:2]), (owns[1], *got[2:])
    )
    got = together(
        [
            (blocks[4 * index + step], place(step))
            for step in (2, 1, 3)
            for index, (place, _) in enumerate(others)
        ]
    )
    totals = jnp.stack(
        [
            sum((other.astype(full) for other in got[index::2]), blocks[4 * index]).astype(low)
            for index in range(2)
        ]
    )
    got, other_local = together([(totals, flip(16)), (local, flip(16))])
    low_means = (local + other_local).reshape(5, width) / pairs
    place = (zi * 256 + yi * 64).astype(jnp.int32).reshape(1)
    both = slope_tiles(place, totals, got, diagonal[None], pairs)
    got = together(
        [(both[index], place(step)) for step in (2, 1, 3) for index, (place, _) in enumerate(others)]
    )
    blocks = [
        assemble(both[index], got[index::2], position) for index, (_, position) in enumerate(others)
    ]

    diagonal_slope = (-2.0 * (1.0 - diagonal)).astype(low).astype(full)
    wide_slope = jnp.broadcast_to(diagonal_slope, (8, width))
    weights, *means = (jnp.broadcast_to(mean, (16, width)).astype(low) for mean in low_means)
    near_even, near_odd = blocks[0][:, width:], blocks[1][:, width:]
    got = together(around(near_even, at_z) + around(near_odd, at_y))
    slope_d = assemble(near_odd, got[3:], yi)
    slope_c = assemble(near_even, got[:3], zi)
    product_d = stage([(times(low_a, slope_d, low), core)])[0]
    across = add(times(low_a, slope_c, full), product_d).astype(low)
    near_even, near_odd = blocks[0][:, :width], blocks[1][:, :width]
    across, near_even, near_odd = lax.optimization_barrier((across, near_even, near_odd))
    across = stage([(across, chip)])[0]
    columns_c, rows_c = slope_terms(slope_c, weights, means[1])
    columns_d, rows_d = slope_terms(slope_d, weights, means[3])
    part_a = up_a_call(1, low_even, low_odd, slope_c, slope_d)
    got = stage(
        [(near_even, at_z(1)), (near_even, at_z(3)), (near_odd, at_y(1)), (near_odd, at_y(3))]
    )
    got, (columns_c, rows_c, columns_d, rows_d) = lax.optimization_barrier(
        (got, (columns_c, rows_c, columns_d, rows_d))
    )
    sends = list(zip(halves(got), (at_z(1), at_z(3), at_y(1), at_y(3))))
    far, part_a = lax.optimization_barrier((tuple(stage(sends)), part_a))
    slope_e = assemble(near_odd, [*far[2:], *got[2:]], yi)
    slope_b = assemble(near_even, [*far[:2], *got[:2]], zi)
    near = times(low_a, slope_e, low)
    columns_b, rows_b, slope_b = slope_terms(slope_b, weights, means[0], wide_slope)
    columns_e, rows_e = slope_terms(slope_e, weights, means[2])
    small = jnp.concatenate((columns_e[:2], columns_d[:2]))
    across, near, small = lax.optimization_barrier((across, near, small))
    diagonal_term = diagonal_slope * diagonal
    near, small = stage([(near, core), (small, core)])
    slots = columns_b[2:3]
    distant = stage([(jnp.concatenate((columns_c[:2] + small[2:4], slots)), chip)])[0]
    rows_a = rows_b[:2] + rows_c[:2] + rows_d[:2] + rows_e[:2]
    rows_a = jnp.concatenate(((rows_a[0] + diagonal_term)[None], rows_a[1:2]))
    stats_a = jnp.concatenate((mean[0:1], inv_a[None], rows_a, jnp.zeros((4, width), full)))
    grad_a = up_a_call(0, low_even, low_odd, slope_b, slope_e, part_a, view_a, stats_a)
    grad_a, distant = lax.optimization_barrier((grad_a, distant))
    slots = slots + distant[2:3]
    loss = jnp.sum(slots + stage([(slots, core)])[0])
    columns = columns_b[:2] + small[0:2] + distant[0:2]
    columns = jnp.concatenate(((columns[0] + diagonal_term)[None], columns[1:2]))
    stats_b = jnp.concatenate((mean[1:2], inv_b[None], columns, jnp.zeros((4, width), full)))
    grad_b = grad_b_call(low_a, slope_b, near, across, view_b, stats_b)
    return (loss, grad_a, grad_b)


def solution(mesh):
    in_specs = (P("dp", "feat"), P("dp", "feat"))
    out_specs = (P(), P("dp", "feat"), P("dp", "feat"))
    return jax.shard_map(
        on_device, mesh=mesh, in_specs=in_specs, out_specs=out_specs, check_vma=False
    )
```

```python
import functools

import jax
import jax.numpy as jnp
from jax import lax
from jax.experimental import pallas as pl
from jax.experimental.pallas import tpu as pltpu
from jax.sharding import PartitionSpec as P

epsilon = 1e-05
off_weight = 0.0051
low = jnp.bfloat16
full = jnp.float32


def at_z(step):
    return "dp", lambda d: d // 4 * 4 + (d + step) % 4


def at_y(step):
    return "dp", lambda d: d // 16 * 16 + (d // 4 + step) % 4 * 4 + d % 4


def flip(bits):
    return "dp", lambda d: d ^ bits


def across_both(member):
    return member ^ (16 * 4 + 2)


core = ("feat", lambda f: f ^ 1)
chip = ("feat", lambda f: f ^ 2)


def stage(sends, after=()):
    held = lax.optimization_barrier(tuple(values for values, _ in sends) + tuple(after))
    received = []
    for values, (_, (axis, place)) in zip(held, sends):
        count = 128 if isinstance(axis, tuple) else lax.axis_size(axis)
        received.append(lax.ppermute(values, axis, [(d, place(d)) for d in range(count)]))
    return received


def together(sends):
    return list(lax.optimization_barrier(tuple(stage(sends))))


def share(values, groups=None):
    count = len(groups[0]) if groups else lax.axis_size("dp")
    pieces = jnp.broadcast_to(values[None], (count,) + values.shape)
    return lax.all_to_all(pieces, "dp", 0, 0, tiled=True, axis_index_groups=groups)


def combine(means, products, rows):
    mean = jnp.mean(means, axis=0)
    shift = means - mean
    shifts = jnp.stack((shift[:, 0] ** 2, shift[:, 1] ** 2, shift[:, 0] * shift[:, 1]), axis=1)
    return mean, jnp.sum(products + rows * shifts, axis=0)


def normalise_kernel(view_b, view_c, stats, out):
    width = view_b.shape[1]
    for index, view in enumerate((view_b, view_c)):
        mean = stats[2 * index : 2 * index + 1, :]
        inverse = stats[2 * index + 1 : 2 * index + 2, :]
        values = (view[...].astype(full) - mean) * inverse
        out[:, index * width : (index + 1) * width] = values.astype(low)


def normalise(view_b, view_c, stats):
    rows, width = view_b.shape
    return pl.pallas_call(
        normalise_kernel,
        grid=(rows // 256,),
        in_specs=[
            pl.BlockSpec((256, width), lambda i: (i, 0)),
            pl.BlockSpec((256, width), lambda i: (i, 0)),
            pl.BlockSpec((8, width), lambda i: (0, 0)),
        ],
        out_specs=pl.BlockSpec((256, 2 * width), lambda i: (i, 0)),
        out_shape=jax.ShapeDtypeStruct((rows, 2 * width), low),
        compiler_params=pltpu.CompilerParams(vmem_limit_bytes=32 * 2**20),
    )(view_b, view_c, stats)


def add_kernel(*refs):
    for index in range(4):
        refs[8 + index][...] = (
            refs[index][...].astype(full) + refs[4 + index][...].astype(full)
        ).astype(low)


def add_halves(blocks, received):
    rows, columns = received[0].shape
    halves = [pl.BlockSpec((rows, 1024), lambda i, h=h: (h, i)) for h in (0, 1, 0, 1)]
    return pl.pallas_call(
        add_kernel,
        grid=(columns // 1024,),
        in_specs=halves + [pl.BlockSpec((rows, 1024), lambda i: (0, i))] * 4,
        out_specs=halves,
        out_shape=[jax.ShapeDtypeStruct(block.shape, low) for block in blocks],
        input_output_aliases={index: index for index in range(4)},
        compiler_params=pltpu.CompilerParams(vmem_limit_bytes=32 * 2**20),
    )(*blocks, *received)


small_cost = pl.CostEstimate(flops=1, bytes_accessed=1, transcendentals=0)
params = pltpu.CompilerParams(vmem_limit_bytes=48 * 2**20)
large = pltpu.CompilerParams(vmem_limit_bytes=56 * 2**20)
over_columns = (((1,), (1,)), ((), ()))


def whole(*shape):
    return pl.BlockSpec(shape, lambda *_: (0,) * len(shape))


def slope_kernel(place, total, received, diagonal, out, *, pairs):
    corr = add(total[...], received[...]) / pairs
    shape = corr.shape
    own = place[0]
    row = lax.broadcasted_iota(jnp.int32, shape, 1)
    on_diagonal = (lax.broadcasted_iota(jnp.int32, shape, 2) == own + row) & (
        lax.broadcasted_iota(jnp.int32, shape, 0) == 0
    )
    lane = lax.broadcasted_iota(jnp.int32, diagonal.shape, 1)
    rest = 1.0 - diagonal[...]
    rest = jnp.where((lane >= own) & (lane < own + shape[1]), rest * rest, 0.0)
    loss = jnp.sum(jnp.where(on_diagonal, 0.0, off_weight * corr * corr)) + jnp.sum(rest)
    loss = jnp.full((1, 1, 128), loss)
    high = loss.astype(low).astype(full)
    middle = (loss - high).astype(low).astype(full)
    slots = jnp.zeros(shape, full)
    for index, part in enumerate((high, middle, loss - high - middle)):
        slots = jnp.where(row == index, jnp.max(part), slots)
    out[...] = jnp.where(on_diagonal, slots, 2.0 * off_weight * corr).astype(low)


def slope_tiles(place, total, received, diagonal, pairs):
    shape = received.shape
    return pl.pallas_call(
        functools.partial(slope_kernel, pairs=pairs),
        grid_spec=pltpu.PrefetchScalarGridSpec(
            num_scalar_prefetch=1,
            grid=(1,),
            in_specs=[whole(*shape), whole(*shape), whole(1, diagonal.shape[1])],
            out_specs=whole(*shape),
        ),
        out_shape=jax.ShapeDtypeStruct(shape, low),
        compiler_params=params,
    )(place, total, received, diagonal)


def far_kernel(position, left, right, top, bottom):
    columns = left[:, pl.ds(pl.multiple_of(position[0] * 256, 256), 256)]
    part = lax.dot_general(
        columns, right[...], (((0,), (0,)), ((), ())), preferred_element_type=full
    ).astype(low)
    top[...] = part[:128]
    bottom[...] = part[128:]


def near_kernel(position, left, right, above, below):
    for step, out in ((1, above), (3, below)):
        start = pl.multiple_of(((position[0] + step) & 3) * 256, 256)
        out[...] = lax.dot_general(
            left[:, pl.ds(start, 256)],
            right[...],
            (((0,), (0,)), ((), ())),
            preferred_element_type=full,
        ).astype(low)


def near_chunks(position, left, right):
    rows, width = left.shape
    columns = right.shape[1]
    return pl.pallas_call(
        near_kernel,
        grid_spec=pltpu.PrefetchScalarGridSpec(
            num_scalar_prefetch=1,
            grid=(columns // 512,),
            in_specs=[whole(rows, width), pl.BlockSpec((rows, 512), lambda i, p: (0, i))],
            out_specs=[pl.BlockSpec((256, 512), lambda i, p: (0, i))] * 2,
        ),
        out_shape=[jax.ShapeDtypeStruct((256, columns), low)] * 2,
        compiler_params=params,
    )(position.astype(jnp.int32).reshape(1), left, right)


def far_chunk(position, left, right):
    rows, width = left.shape
    columns = right.shape[1]
    return pl.pallas_call(
        far_kernel,
        grid_spec=pltpu.PrefetchScalarGridSpec(
            num_scalar_prefetch=1,
            grid=(columns // 512,),
            in_specs=[whole(rows, width), pl.BlockSpec((rows, 512), lambda i, p: (0, i))],
            out_specs=[pl.BlockSpec((128, 512), lambda i, p: (0, i))] * 2,
        ),
        out_shape=[jax.ShapeDtypeStruct((128, columns), low)] * 2,
        compiler_params=params,
    )(position.astype(jnp.int32).reshape(1), left, right)


def product_kernel(left, right, out):
    out[...] = jnp.dot(left[...], right[...], preferred_element_type=full).astype(out.dtype)


def times(left, right, kind):
    rows, depth = left.shape
    columns = right.shape[1]
    return pl.pallas_call(
        product_kernel,
        grid=(rows // 256,),
        in_specs=[pl.BlockSpec((256, depth), lambda i: (i, 0)), whole(depth, columns)],
        out_specs=pl.BlockSpec((256, columns), lambda i: (i, 0)),
        out_shape=jax.ShapeDtypeStruct((rows, columns), kind),
        compiler_params=params,
        cost_estimate=small_cost,
    )(left, right)


def upstream(even, odd, slope_even, slope_odd):
    up = lax.dot_general(even[...], slope_even[...], over_columns, preferred_element_type=full)
    return up + lax.dot_general(odd[...], slope_odd[...], over_columns, preferred_element_type=full)


def part_kernel(even, odd, slope_even, slope_odd, out):
    out[...] = upstream(even, odd, slope_even, slope_odd)


def grad_kernel(even, odd, slope_even, slope_odd, part, view, stats, out):
    up = part[...] + upstream(even, odd, slope_even, slope_odd)
    inverse = stats[1:2]
    norm = (view[...].astype(full) - stats[0:1]) * inverse
    out[...] = (inverse * (up - stats[3:4] - norm * stats[2:3])).astype(low)


def up_a_call(half, low_even, low_odd, slope_even, slope_odd, *more):
    rows = low_even.shape[0]
    width = slope_even.shape[0]
    left = pl.BlockSpec((rows, width), lambda i: (0, half))
    right = pl.BlockSpec((256, width), lambda i: (i, 0))
    tile = pl.BlockSpec((rows, 256), lambda i: (0, i))
    line = pl.BlockSpec((8, 256), lambda i: (0, i))
    return pl.pallas_call(
        grad_kernel if more else part_kernel,
        grid=(width // 256,),
        in_specs=[left, left, right, right] + ([tile, tile, line] if more else []),
        out_specs=tile,
        out_shape=jax.ShapeDtypeStruct((rows, width), low if more else full),
        compiler_params=large if more else params,
        cost_estimate=small_cost,
    )(low_even, low_odd, slope_even, slope_odd, *more)


def halves_kernel(*refs):
    for index in range(4):
        refs[4 + index][...] = refs[index][...]


def halves(blocks):
    rows, columns = blocks[0].shape
    return pl.pallas_call(
        halves_kernel,
        grid=(2,),
        in_specs=[
            pl.BlockSpec((rows // 2, columns // 2), lambda i, h=h: (h, i)) for h in (0, 1, 0, 1)
        ],
        out_specs=[pl.BlockSpec((rows // 2, columns // 2), lambda i: (0, i))] * 4,
        out_shape=[jax.ShapeDtypeStruct((rows // 2, columns), low)] * 4,
        compiler_params=params,
    )(*blocks)


def grad_b_kernel(left, slope, near, across, view, stats, out):
    up = jnp.dot(left[...], slope[...], preferred_element_type=full)
    up = up + near[...].astype(full) + across[...].astype(full)
    inverse = stats[1:2]
    norm = (view[...].astype(full) - stats[0:1]) * inverse
    out[...] = (inverse * (up - stats[3:4] - norm * stats[2:3])).astype(low)


def grad_b_call(left, slope, near, across, view, stats):
    rows, width = view.shape
    tile = pl.BlockSpec((256, width), lambda i: (i, 0))
    return pl.pallas_call(
        grad_b_kernel,
        grid=(rows // 256,),
        in_specs=[tile, whole(*slope.shape)] + [tile] * 3 + [whole(8, width)],
        out_specs=tile,
        out_shape=jax.ShapeDtypeStruct((rows, width), low),
        compiler_params=large,
        cost_estimate=small_cost,
    )(left, slope, near, across, view, stats)


def split_kernel(places, *refs):
    step = pl.program_id(0)
    for index in range(2):
        own, first, second = refs[3 * index : 3 * index + 3]
        total = own[...] + first[...].astype(full) + second[...].astype(full)
        for place in range(4):
            out = refs[6 + 4 * index + place]

            @pl.when(step == place)
            def _(out=out, total=total):
                out[...] = total.astype(out.dtype)


def split_sums(places, even, odd):
    rows, columns = even[0].shape
    size = rows // 4

    def block(index):
        return pl.BlockSpec((size, columns), lambda k, p: ((p[index] + k) & 3, 0))

    kinds = [full, low, low, low] * 2
    return pl.pallas_call(
        split_kernel,
        grid_spec=pltpu.PrefetchScalarGridSpec(
            num_scalar_prefetch=1,
            grid=(4,),
            in_specs=[block(0)] * 3 + [block(1)] * 3,
            out_specs=[whole(size, columns)] * 8,
        ),
        out_shape=[jax.ShapeDtypeStruct((size, columns), kind) for kind in kinds],
        compiler_params=params,
    )(places, *even, *odd)


def terms_kernel(slope, weights, means, diagonal_slope, columns, rows, *fixed):
    step = pl.program_id(0)

    @pl.when(step == 0)
    def _():
        columns[...] = jnp.zeros_like(columns)

    values = slope[...]
    if fixed:
        shape = values.shape
        on_diagonal = lax.broadcasted_iota(
            jnp.int32, shape, 1
        ) == step * 256 + lax.broadcasted_iota(jnp.int32, shape, 0)
        wide = values.astype(full)
        columns[2:3] += jnp.sum(jnp.where(on_diagonal, wide, 0.0), axis=0, keepdims=True)
        off = jnp.where(on_diagonal, 0.0, wide)
        values = jnp.where(on_diagonal, diagonal_slope[0:1], wide).astype(low)
        fixed[0][...] = values
    else:
        off = values.astype(full)
    squares = off * off * (0.5 / off_weight)
    columns[0:1] += jnp.sum(squares, axis=0, keepdims=True)
    columns[1:2] += jnp.dot(weights[...], values, preferred_element_type=full)[0:1]
    high = squares.astype(low)
    rest = (squares - high.astype(full)).astype(low)
    ones = jnp.ones((8, values.shape[1]), low)
    rows[0:1] = (
        lax.dot_general(ones, high, over_columns, preferred_element_type=full)
        + lax.dot_general(ones, rest, over_columns, preferred_element_type=full)
    )[0:1]
    rows[1:2] = lax.dot_general(means[...], values, over_columns, preferred_element_type=full)[0:1]
    rows[2:8] = jnp.zeros((6, 256), full)


def slope_terms(slope, weights, means, diagonal_slope=None):
    width = slope.shape[0]
    fix = diagonal_slope is not None
    tile = pl.BlockSpec((256, width), lambda i: (i, 0))
    outs = [jax.ShapeDtypeStruct((8, width), full)] * 2
    return pl.pallas_call(
        terms_kernel,
        grid=(4,),
        in_specs=[
            tile,
            pl.BlockSpec((16, 256), lambda i: (0, i)),
            whole(16, width),
            whole(8, width),
        ],
        out_specs=[whole(8, width), pl.BlockSpec((8, 256), lambda i: (0, i))] + [tile] * fix,
        out_shape=outs + [jax.ShapeDtypeStruct(slope.shape, low)] * fix,
        input_output_aliases={0: 2} if fix else {},
        compiler_params=params,
        cost_estimate=small_cost,
    )(slope, weights, means, diagonal_slope if fix else jnp.zeros((8, width), full))


def assemble_kernel(position, *refs):
    step = pl.program_id(0)
    out = refs[-1]
    halves = len(refs) == 6
    half = out.shape[0] // 2
    for index in range(4):

        @pl.when(step == index)
        def _(index=index):
            if halves and index == 1:
                out[:half] = refs[1][...]
                out[half:] = refs[2][...]
            else:
                out[...] = refs[index + halves * (index > 1)][...]


def add(one, other):
    return one.astype(full) + other.astype(full)


def pick(stack, index, axis):
    return lax.dynamic_index_in_dim(stack, index, axis, keepdims=False)


def put(stack, part, start):
    return lax.dynamic_update_slice_in_dim(stack, part, start, 0)


def around(block, place):
    return [(block, place(step)) for step in (2, 1, 3)]


def assemble(block, others, position):
    rows, columns = block.shape
    return pl.pallas_call(
        assemble_kernel,
        grid_spec=pltpu.PrefetchScalarGridSpec(
            num_scalar_prefetch=1,
            grid=(4,),
            in_specs=[whole(*part.shape) for part in (block, *others)],
            out_specs=pl.BlockSpec(
                (rows, columns),
                lambda k, p: ((p[0] - (k == 1) * 2 - (k == 2) * 1 - (k == 3) * 3) & 3, 0),
            ),
        ),
        out_shape=jax.ShapeDtypeStruct((4 * rows, columns), block.dtype),
        compiler_params=pltpu.CompilerParams(vmem_limit_bytes=32 * 2**20),
    )(position.astype(jnp.int32).reshape(1), block, *others)


def on_device(view_a, view_b):
    dp_count = lax.axis_size("dp")
    rows, width = view_a.shape
    pairs = rows * dp_count
    dp_index = lax.axis_index("dp")
    xi, yi, zi = dp_index >> 4, (dp_index >> 2) & 3, dp_index & 3
    view_c = stage([(view_b, chip)])[0]
    first = view_a.astype(full)
    second = view_b.astype(full)
    means = jnp.stack((jnp.mean(first, axis=0), jnp.mean(second, axis=0)))
    rest_a, rest_b = first - means[0], second - means[1]
    products = jnp.stack(
        (
            jnp.sum(rest_a * rest_a, axis=0),
            jnp.sum(rest_b * rest_b, axis=0),
            jnp.sum(rest_a * rest_b, axis=0),
        )
    )
    half_groups = [[16 * x + i for i in range(16)] for x in range(2)]
    shared = share(jnp.concatenate((means, products)).reshape(-1, 128), half_groups)
    shared = shared.reshape(16, 5, width)
    mean, products = combine(shared[:, :2], shared[:, 2:], rows)
    parts = jnp.concatenate((mean, products))
    part_b = jnp.stack((mean[1], products[1]))
    view_d = stage([(view_b, core)])[0]
    parts, part_b, view_c, view_d = lax.optimization_barrier((parts, part_b, view_c, view_d))
    other, part_c, part_d, view_e = together(
        [
            (parts, flip(16)),
            (part_b, chip),
            (part_b, (("dp", "feat"), across_both)),
            (view_c, core),
        ]
    )
    both = jnp.stack((parts, other))
    mean, products = combine(both[:, :2], both[:, 2:], pairs // 2)
    inverse = lax.rsqrt(products[:2] / pairs + epsilon)
    inv_a, inv_b = inverse
    diagonal = products[2] / pairs * inv_a * inv_b
    mean_c = 0.5 * (part_c[0] + part_d[0])
    products_c = part_c[1] + part_d[1] + (pairs // 4) * (part_c[0] - part_d[0]) ** 2
    inv_c = lax.rsqrt(products_c / pairs + epsilon)
    stats = jnp.concatenate(
        (jnp.stack((mean[1], inv_b, mean_c, inv_c)), jnp.zeros((4, width), full))
    )
    norm_a = (first - mean[0]) * inv_a
    low_a = norm_a.astype(low)

    low_even = normalise(view_b, view_c, stats)
    low_odd = normalise(view_d, view_e, stage([(stats, core)])[0])
    ways = ((low_even, at_z, zi), (low_odd, at_y, yi))

    def product(right, start, size):
        columns = lax.dynamic_slice_in_dim(low_a, start, size, 1)
        return lax.dot_general(
            columns, right, (((0,), (0,)), ((), ())), preferred_element_type=full
        )

    sends = []
    for right, place, position in ways:
        top, bottom = far_chunk((position + 2) & 3, low_a, right)
        sends.extend(((top, place(1)), (bottom, place(3))))
    nears = [
        near for right, _, position in ways for near in near_chunks(position, low_a, right)
    ]
    got = together(sends)
    nears = add_halves(nears, got)
    sends = [
        (near, place(step))
        for near, (place, step) in zip(nears, ((at_z, 1), (at_z, 3), (at_y, 1), (at_y, 3)))
    ]
    local = jnp.concatenate(
        (
            jnp.sum(low_a.astype(full), axis=0),
            jnp.sum(low_even.astype(full), axis=0),
            jnp.sum(low_odd.astype(full), axis=0),
        )
    )
    local = share(local.reshape(-1, 128), half_groups)
    owns = [product(right, position * 256, 256) for right, _, position in ways]
    local, owns, got = lax.optimization_barrier((local, owns, tuple(stage(sends))))
    local = jnp.sum(local, axis=0)

    others = ((at_y, yi), (at_z, zi))
    blocks = split_sums(
        jnp.stack((yi, zi)).astype(jnp.int32), (owns[0], *got[:2]), (owns[1], *got[2:])
    )
    got = together(
        [
            (blocks[4 * index + step], place(step))
            for step in (2, 1, 3)
            for index, (place, _) in enumerate(others)
        ]
    )
    totals = jnp.stack(
        [
            sum((other.astype(full) for other in got[index::2]), blocks[4 * index]).astype(low)
            for index in range(2)
        ]
    )
    got, other_local = together([(totals, flip(16)), (local, flip(16))])
    low_means = (local + other_local).reshape(5, width) / pairs
    place = (zi * 256 + yi * 64).astype(jnp.int32).reshape(1)
    both = slope_tiles(place, totals, got, diagonal[None], pairs)
    got = together(
        [(both[index], place(step)) for step in (2, 1, 3) for index, (place, _) in enumerate(others)]
    )
    blocks = [
        assemble(both[index], got[index::2], position) for index, (_, position) in enumerate(others)
    ]

    diagonal_slope = (-2.0 * (1.0 - diagonal)).astype(low).astype(full)
    wide_slope = jnp.broadcast_to(diagonal_slope, (8, width))
    weights, *means = (jnp.broadcast_to(mean, (16, width)).astype(low) for mean in low_means)
    near_even, near_odd = blocks[0][:, width:], blocks[1][:, width:]
    got = together(around(near_even, at_z) + around(near_odd, at_y))
    slope_d = assemble(near_odd, got[3:], yi)
    slope_c = assemble(near_even, got[:3], zi)
    product_d = stage([(times(low_a, slope_d, low), core)])[0]
    across = add(times(low_a, slope_c, full), product_d).astype(low)
    near_even, near_odd = blocks[0][:, :width], blocks[1][:, :width]
    across, near_even, near_odd = lax.optimization_barrier((across, near_even, near_odd))
    across = stage([(across, chip)])[0]
    columns_c, rows_c = slope_terms(slope_c, weights, means[1])
    columns_d, rows_d = slope_terms(slope_d, weights, means[3])
    part_a = up_a_call(1, low_even, low_odd, slope_c, slope_d)
    got = stage(
        [(near_even, at_z(1)), (near_even, at_z(3)), (near_odd, at_y(1)), (near_odd, at_y(3))]
    )
    got, (columns_c, rows_c, columns_d, rows_d) = lax.optimization_barrier(
        (got, (columns_c, rows_c, columns_d, rows_d))
    )
    sends = list(zip(halves(got), (at_z(1), at_z(3), at_y(1), at_y(3))))
    far, part_a = lax.optimization_barrier((tuple(stage(sends)), part_a))
    slope_e = assemble(near_odd, [*far[2:], *got[2:]], yi)
    slope_b = assemble(near_even, [*far[:2], *got[:2]], zi)
    near = times(low_a, slope_e, low)
    columns_b, rows_b, slope_b = slope_terms(slope_b, weights, means[0], wide_slope)
    columns_e, rows_e = slope_terms(slope_e, weights, means[2])
    small = jnp.concatenate((columns_e[:2], columns_d[:2]))
    across, near, small = lax.optimization_barrier((across, near, small))
    diagonal_term = diagonal_slope * diagonal
    near, small = stage([(near, core), (small, core)])
    slots = columns_b[2:3]
    distant = stage([(jnp.concatenate((columns_c[:2] + small[2:4], slots)), chip)])[0]
    rows_a = rows_b[:2] + rows_c[:2] + rows_d[:2] + rows_e[:2]
    rows_a = jnp.concatenate(((rows_a[0] + diagonal_term)[None], rows_a[1:2]))
    stats_a = jnp.concatenate((mean[0:1], inv_a[None], rows_a, jnp.zeros((4, width), full)))
    grad_a = up_a_call(0, low_even, low_odd, slope_b, slope_e, part_a, view_a, stats_a)
    grad_a, distant = lax.optimization_barrier((grad_a, distant))
    slots = slots + distant[2:3]
    loss = jnp.sum(slots + stage([(slots, core)])[0])
    columns = columns_b[:2] + small[0:2] + distant[0:2]
    columns = jnp.concatenate(((columns[0] + diagonal_term)[None], columns[1:2]))
    stats_b = jnp.concatenate((mean[1:2], inv_b[None], columns, jnp.zeros((4, width), full)))
    grad_b = grad_b_call(low_a, slope_b, near, across, view_b, stats_b)
    return (loss, grad_a, grad_b)


def solution(mesh):
    in_specs = (P("dp", "feat"), P("dp", "feat"))
    out_specs = (P(), P("dp", "feat"), P("dp", "feat"))
    return jax.shard_map(
        on_device, mesh=mesh, in_specs=in_specs, out_specs=out_specs, check_vma=False
    )
```
